32 devices in a mesh: parts: 2 (over y), group: 4 (over z), tensor: 4 (over x, core).
Axes of the slice: x: 2, y: 2, z: 4, core: 2. Of those that a mesh axis runs over, the one named last changes fastest.
Arguments:
- queries: bfloat16 [512, 8192], P(('parts', 'group'), 'tensor'), parts along dimension 0, may hold values from -36 to 36
- keys: bfloat16 [512, 1024], P(('parts', 'group'), 'tensor'), parts along dimension 0, may hold values from -64 to 64
- values: bfloat16 [512, 1024], P(('parts', 'group'), 'tensor'), parts along dimension 0, may hold values from -6 to 6
- prefix_keys: bfloat16 [2048, 1024], P(('parts', 'group'), 'tensor'), parts along dimension 0, may hold values from -6 to 6
- prefix_values: bfloat16 [2048, 1024], P(('parts', 'group'), 'tensor'), parts along dimension 0, may hold values from -6 to 6
- spread: int32 [8], P('parts'), parts along dimension 0, may hold values from 0 to 3, as said below
- turn: int32 [8], P('parts'), parts along dimension 0, may hold values from 0 to 7
- new_blocks: int32 [8, 4], P('parts'), parts along dimension 0, may hold values from 1 to 2, as said below
- prefix_len: int32 [8, 4], P('parts'), parts along dimension 0, may hold values from 1 to 64, as said below
- owner: int32 [8, 4], P('parts'), parts along dimension 0, may hold values from 0 to 3, as said below
- page_start: int32 [8, 4], P('parts'), parts along dimension 0, may hold values from 0 to 6, as said below
Outputs:
- attention: bfloat16 [512, 8192], P(('parts', 'group'), 'tensor'), parts along dimension 0
- cache: bfloat16 [64, 2, 8, 1024], P(('parts', 'group'), None, 'tensor'), parts along dimension 0
The draws below stay inside these ranges and needn't reach their ends.
There are 2 independent parts, one for each index of `parts`. The reference program is written for one: setup_inputs(seed, part) draws one part's arguments, and reference() takes and returns one part's arrays. A program takes and returns all parts, laid end to end along the dimension named above; each array names one. Nothing has to cross between parts.
Inputs may be any that keep to these rules, and one draw needn't show every extreme that they name: `spread`: A permutation of the numbers below 4. `new_blocks`: in every group one prompt has exactly 2 new blocks. `prefix_len`: in every group one prompt has exactly 64 cached tokens. `owner`: the prompts of one prefill group have different owners, and every decode group owns exactly one prompt of each index p. `page_start`: A multiple of 2; the prompts owned by one decode group start at different pages.
All inputs are finite; a program needn't handle non-finite values.
Results may differ from the reference program's by a relative error of at most 0.012.
The reference program's roundings to bfloat16 on the way (of `weights`) count: a program that leaves them out, or rounds other values in their place, can miss the bound.
Values may be sent and summed in bfloat16 or wider, within the bound.
No kernel may reach another device: no remote copies, remote signals or barrier semaphores. Data moves between devices by JAX's collectives and lax.ppermute only.
A program may use at most 64 MiB of HBM per device.

```python
import math
import jax
import jax.numpy as jnp
from jax import lax

HEAD = 128
Q_HEADS = 64
KV_HEADS = 8
BLOCK = 8
MAXP = 2
CTXP = 64
GROUPS = 4
PROMPTS = 4
SLOTS = 8
PAGES = 8
ROWS = 256
PREFIX = 1024


def owner_plan(key):
    plan_key = jax.random.fold_in(key, 77)
    shift_key, order_key = jax.random.split(plan_key)
    shifts = jax.random.permutation(shift_key, GROUPS)[:PROMPTS].astype(jnp.int32)

    def one_order(row_key):
        return jax.random.permutation(row_key, PROMPTS)
    orders = jax.vmap(one_order)(jax.random.split(order_key, GROUPS)).astype(jnp.int32)
    homes = (jnp.arange(GROUPS, dtype=jnp.int32)[:, None] + shifts[None, :]) % GROUPS
    return (homes, orders)


def draw_queries(key, part):
    own_key = jax.random.fold_in(key, 1)
    drawn = jnp.clip(jax.random.normal(own_key, (ROWS, Q_HEADS * HEAD), jnp.float32), -6.0, 6.0)
    return drawn.astype(jnp.bfloat16)


def draw_keys(key, part):
    own_key = jax.random.fold_in(key, 2)
    drawn = jnp.clip(jax.random.normal(own_key, (ROWS, KV_HEADS * HEAD), jnp.float32), -6.0, 6.0)
    return drawn.astype(jnp.bfloat16)


def draw_spread(key, part):
    own_key = jax.random.fold_in(key, 21)
    return jax.random.permutation(own_key, GROUPS).astype(jnp.int32)


def draw_new_blocks(key, part):
    own_key = jax.random.fold_in(key, 11)
    length_key, column_key = jax.random.split(own_key)
    lengths = jax.random.randint(length_key, (GROUPS, PROMPTS), 1, MAXP + 1)
    column = jax.random.randint(column_key, (GROUPS,), 0, PROMPTS)
    full_prompt = jnp.arange(PROMPTS)[None, :] == column[:, None]
    return jnp.where(full_prompt, MAXP, lengths).astype(jnp.int32)


def draw_prefix_len(key, part):
    own_key = jax.random.fold_in(key, 12)
    length_key, column_key = jax.random.split(own_key)
    lengths = jax.random.randint(length_key, (GROUPS, PROMPTS), 1, CTXP + 1)
    column = jax.random.randint(column_key, (GROUPS,), 0, PROMPTS)
    full_prompt = jnp.arange(PROMPTS)[None, :] == column[:, None]
    return jnp.where(full_prompt, CTXP, lengths).astype(jnp.int32)


def draw_owner(key, part):
    homes, orders = owner_plan(key)
    return homes.astype(jnp.int32)


def draw_page_start(key, part):
    homes, orders = owner_plan(key)
    prompt_index = jnp.broadcast_to(jnp.arange(PROMPTS, dtype=jnp.int32)[None, :], (GROUPS, PROMPTS))
    return (orders[homes, prompt_index] * MAXP).astype(jnp.int32)


def set_ends(values, stream_key, smallest, largest):
    index_at = [jax.random.randint(jax.random.fold_in(stream_key, axis), (), 0, length) for axis, length in enumerate(values.shape)]
    widest = values.shape.index(max(values.shape))
    beside = index_at[:widest] + [(index_at[widest] + 1) % values.shape[widest]] + index_at[widest + 1:]
    return values.at[tuple(index_at)].set(smallest).at[tuple(beside)].set(largest)


def shard_levels(stream_key, dims, shards, smallest, high):
    factor_of = 1.0
    for dim, shards_of in shards:
        draws = jax.random.uniform(jax.random.fold_in(jax.random.fold_in(stream_key, 6), dim), (shards_of,), jnp.float32, smallest / len(shards), high / len(shards))
        factor_of = factor_of * jnp.repeat(jnp.exp(draws), dims[dim] // shards_of).reshape((-1,) + (1,) * (len(dims) - 1 - dim))
    return factor_of


def scatter_about(key, dims, scale, bound, pieces=(), kind=jnp.bfloat16):
    entries = jax.random.normal(key, dims, jnp.float32) * scale
    if len(pieces) > 0:
        entries = shard_levels(key, dims, pieces, -0.22, 0.18) * entries
    return jnp.clip(entries, min=-bound, max=bound).astype(kind)


def setup_inputs(seed: int = 0, part: int = 0) -> dict:
    key_list = jax.random.split(jax.random.key(seed), 12)
    part_keys = jax.random.split(jax.random.fold_in(key_list[11], part), 12)
    queries = draw_queries(jax.random.fold_in(jax.random.fold_in(key_list[11], part), 71), part)
    keys = draw_keys(jax.random.fold_in(jax.random.fold_in(key_list[11], part), 71), part)
    values = scatter_about(part_keys[2], (ROWS, KV_HEADS * HEAD), 1.0, 6.0, ((0, 4), (1, 4)))
    prefix_keys = scatter_about(part_keys[3], (PREFIX, KV_HEADS * HEAD), 1.0, 6.0, ((0, 4), (1, 4)))
    prefix_values = scatter_about(part_keys[4], (PREFIX, KV_HEADS * HEAD), 1.0, 6.0, ((0, 4), (1, 4)))
    spread = draw_spread(jax.random.fold_in(jax.random.fold_in(key_list[11], part), 71), part)
    turn = set_ends(jax.random.randint(part_keys[6], (GROUPS,), 0, SLOTS), jax.random.fold_in(part_keys[6], 1), 0, SLOTS - 1).astype(jnp.int32)
    new_blocks = draw_new_blocks(jax.random.fold_in(jax.random.fold_in(key_list[11], part), 71), part)
    prefix_len = draw_prefix_len(jax.random.fold_in(jax.random.fold_in(key_list[11], part), 71), part)
    owner = draw_owner(jax.random.fold_in(jax.random.fold_in(key_list[11], part), 71), part)
    page_start = draw_page_start(jax.random.fold_in(jax.random.fold_in(key_list[11], part), 71), part)
    return {"queries": queries, "keys": keys, "values": values, "prefix_keys": prefix_keys, "prefix_values": prefix_values, "spread": spread, "turn": turn, "new_blocks": new_blocks, "prefix_len": prefix_len, "owner": owner, "page_start": page_start}


def rotate(tensor_in, position):
    half_width = tensor_in.shape[-1] // 2
    ladder = jnp.arange(half_width, dtype=jnp.int32).astype(jnp.float32)
    frequency = jnp.exp(ladder * (-2.0 * math.log(500000.0) / tensor_in.shape[-1]))
    angles = position.astype(jnp.float32)[:, None] * frequency[None, :]
    cosine = jnp.cos(angles)[:, None, :]
    sine_part = jnp.sin(angles)[:, None, :]
    first_half = tensor_in[..., :half_width].astype(jnp.float32)
    second = tensor_in[..., half_width:].astype(jnp.float32)
    joined = jnp.concatenate([first_half * cosine - second * sine_part, second * cosine + first_half * sine_part], axis=-1)
    return joined.astype(jnp.bfloat16)

def layout(lengths, prefix, slot_count, block_rows):
    prompt_ends = jnp.cumsum(lengths).astype(jnp.int32)
    starts = (prompt_ends - lengths).astype(jnp.int32)
    slot_index = jnp.arange(slot_count, dtype=jnp.int32)
    segment = lax.optimization_barrier(jnp.sum((slot_index[:, None] >= prompt_ends[None, :]).astype(jnp.int32), axis=1)).astype(jnp.int32)
    prompt_index = jnp.arange(lengths.shape[0], dtype=jnp.int32)
    member = (segment[:, None] == prompt_index[None, :]).astype(jnp.int32)
    first_slot = lax.optimization_barrier(jnp.sum(member * starts[None, :], axis=1)).astype(jnp.int32)
    offset = lax.optimization_barrier(jnp.sum(member * prefix[None, :], axis=1)).astype(jnp.int32)
    token_index = jnp.arange(block_rows, dtype=jnp.int32)
    position = (offset + (slot_index - first_slot) * block_rows)[:, None] + token_index[None, :]
    return (segment, starts, position.reshape(-1).astype(jnp.int32))

def reference(queries, keys, values, prefix_keys, prefix_values, spread, turn, new_blocks, prefix_len, owner, page_start):
    slot_rows = SLOTS * BLOCK
    window = MAXP * BLOCK
    head_ratio = Q_HEADS // KV_HEADS
    score_scale = 1.0 / math.sqrt(HEAD)
    group_index = jnp.arange(GROUPS, dtype=jnp.int32)
    slot_index = jnp.arange(SLOTS, dtype=jnp.int32)
    source = (group_index[:, None] + spread[slot_index % GROUPS][None, :]) % GROUPS
    source_slot = (slot_index[None, :] + turn[source]) % SLOTS
    block_index = (source * SLOTS + source_slot).reshape(-1).astype(jnp.int32)

    def packed_rows(source_rows):
        blocks = source_rows.reshape(GROUPS * SLOTS, BLOCK, source_rows.shape[1])
        return jnp.take(blocks, block_index, axis=0).reshape(GROUPS, slot_rows, source_rows.shape[1])

    def one_group(operands):
        group_q, group_k, group_v, cached_k, cached_v, lengths, prefix = operands
        segment, starts, position = layout(lengths, prefix, SLOTS, BLOCK)
        rot_q = rotate(group_q.reshape(slot_rows, Q_HEADS, HEAD), position)
        rot_k = rotate(group_k.reshape(slot_rows, KV_HEADS, HEAD), position)
        local_index = jnp.arange(window, dtype=jnp.int32)
        row_pick = jnp.clip(starts[:, None] * BLOCK + local_index[None, :], 0, slot_rows - 1).reshape(-1).astype(jnp.int32)
        query_own = jnp.take(rot_q, row_pick, axis=0).astype(jnp.float32).reshape(PROMPTS, window, KV_HEADS, head_ratio, HEAD)
        key_own = jnp.concatenate([cached_k.reshape(PROMPTS, CTXP, KV_HEADS, HEAD), jnp.take(rot_k, row_pick, axis=0).reshape(PROMPTS, window, KV_HEADS, HEAD)], axis=1).astype(jnp.float32)
        value_own = jnp.concatenate([cached_v.reshape(PROMPTS, CTXP, KV_HEADS, HEAD), jnp.take(group_v.reshape(slot_rows, KV_HEADS, HEAD), row_pick, axis=0).reshape(PROMPTS, window, KV_HEADS, HEAD)], axis=1).astype(jnp.float32)
        context_index = jnp.arange(CTXP, dtype=jnp.int32)
        cached = jnp.broadcast_to((context_index[None, :] < prefix[:, None])[:, None, :], (PROMPTS, window, CTXP))
        fresh_keys = jnp.broadcast_to((local_index[None, :] <= local_index[:, None])[None], (PROMPTS, window, window))
        own_mask = jnp.concatenate([cached, fresh_keys], axis=2)
        scores = jnp.einsum('pqhgd,pkhd->phgqk', query_own, key_own) * score_scale
        scores = jnp.where(own_mask[:, None, None], scores, -1e+30)
        row_top = lax.optimization_barrier(jnp.max(scores, axis=-1, keepdims=True))
        row_exps = jnp.exp(scores - row_top)
        weights = (row_exps / lax.optimization_barrier(jnp.sum(row_exps, axis=-1, keepdims=True))).astype(jnp.bfloat16)
        mixed = jnp.einsum('phgqk,pkhd->pqhgd', weights.astype(jnp.float32), value_own)
        flat_out = mixed.reshape(PROMPTS * window, Q_HEADS * HEAD)
        row_segment = jnp.repeat(segment, BLOCK)
        prompt_index = jnp.arange(PROMPTS, dtype=jnp.int32)
        row_start = lax.optimization_barrier(jnp.sum(jnp.where(row_segment[:, None] == prompt_index[None, :], starts[None, :] * BLOCK, 0), axis=1))
        row_index = jnp.arange(slot_rows, dtype=jnp.int32)
        back_index = jnp.clip(row_segment * window + row_index - row_start, 0, PROMPTS * window - 1).astype(jnp.int32)
        rows_out = jnp.take(flat_out, back_index, axis=0)
        live_rows = (row_segment < PROMPTS)[:, None]
        attended = jnp.where(live_rows, rows_out, 0.0).astype(jnp.bfloat16)
        finished = jnp.stack([rot_k.reshape(SLOTS, BLOCK, KV_HEADS * HEAD), group_v.reshape(SLOTS, BLOCK, KV_HEADS * HEAD)], axis=1)
        return (attended, finished, starts)
    attention, finished, starts = lax.map(one_group, (packed_rows(queries), packed_rows(keys), packed_rows(values), prefix_keys.reshape(GROUPS, PROMPTS * CTXP, KV_HEADS * HEAD), prefix_values.reshape(GROUPS, PROMPTS * CTXP, KV_HEADS * HEAD), new_blocks, prefix_len))
    attention = attention.reshape(GROUPS * slot_rows, Q_HEADS * HEAD)
    step_index = jnp.arange(MAXP, dtype=jnp.int32)
    slot_pick = jnp.clip(starts[:, :, None] + step_index[None, None, :], 0, SLOTS - 1)
    flat_pick = (group_index[:, None, None] * SLOTS + slot_pick).reshape(-1).astype(jnp.int32)
    chosen = jnp.take(finished.reshape(GROUPS * SLOTS, 2, BLOCK, KV_HEADS * HEAD), flat_pick, axis=0)
    keep_slot = (step_index[None, None, :] < new_blocks[:, :, None]).reshape(-1)
    chosen = jnp.where(keep_slot[:, None, None, None], chosen, jnp.zeros_like(chosen))
    target = ((owner * PAGES + page_start)[:, :, None] + step_index[None, None, :]).reshape(-1).astype(jnp.int32)
    cache = jnp.zeros((GROUPS * PAGES, 2, BLOCK, KV_HEADS * HEAD), jnp.bfloat16).at[target].set(chosen)
    return (attention, cache)
```

```python
import functools
import math

import jax
import jax.numpy as jnp
import numpy as np
from jax import lax
from jax.experimental import pallas as pl
from jax.experimental.pallas import tpu as pltpu
from jax.sharding import PartitionSpec as P

HEAD = 128
BLOCK = 8
MAXP = 2
CTXP = 64
VMEM_LIMIT = 48 * 1024 * 1024

SMEM = pl.BlockSpec(memory_space=pltpu.SMEM)
VMEM = pl.BlockSpec(memory_space=pltpu.VMEM)
ANY = pl.BlockSpec(memory_space=pl.ANY)


def rope_table():
    count = CTXP + MAXP * BLOCK
    half = HEAD // 2
    frequency = np.exp(np.arange(half) * (-2.0 * math.log(500000.0) / HEAD))
    angles = np.arange(count)[:, None] * frequency[None, :]
    cosine, sine = np.cos(angles), np.sin(angles)
    return (
        np.concatenate([cosine, cosine], axis=1).astype(np.float32),
        np.concatenate([-sine, sine], axis=1).astype(np.float32),
    )


def loop(count, body, unrolled=16):
    if count <= unrolled:
        for index in range(count):
            body(index)
    else:
        lax.fori_loop(0, count, lambda index, carry: (body(index), carry)[1], 0)


def turned(head_block, cosine, sine):
    return head_block * cosine + pltpu.roll(head_block, HEAD // 2, 1) * sine


def dispatch_kernel(groups, spread, turn, queries, keys, values, out, sem):
    own = lax.axis_index("group")
    slots, _, width_q = queries.shape
    width_k = keys.shape[2]
    capacity = slots // groups

    def column(c):
        target = lax.rem(own - spread[c] + groups, groups)
        for step in range(capacity):
            source = lax.rem(c + groups * step + turn[own], slots)
            at = out.at[target, step]
            for ref, first, width in (
                (queries, 0, width_q),
                (keys, width_q, width_k),
                (values, width_q + width_k, width_k),
            ):
                pltpu.make_async_copy(ref.at[source], at.at[:, pl.ds(first, width)], sem).start()

    loop(groups, column)
    pltpu.make_async_copy(out, out, sem).wait()


def slot_table(own, new_blocks, prefix_len, prompt, offset, live):
    prompts = new_blocks.shape[1]
    slots = live.shape[0]

    def clear(j):
        prompt[j] = 0
        offset[j] = 0
        live[j] = 0

    loop(slots, clear)

    def one(p, start):
        blocks = new_blocks[own, p]
        cached = prefix_len[own, p]
        for step in range(MAXP):
            at = jnp.minimum(start + step, slots - 1)

            @pl.when(step < blocks)
            def _():
                prompt[at] = p
                offset[at] = cached + step * BLOCK
                live[at] = 1 + step

        return start + blocks

    lax.fori_loop(0, prompts, one, 0)


def pages_kernel(
    groups, tensors, spread, turn, new_blocks, prefix_len, owner, keys, values, cosine, sine, out, rows,
    dest_group, dest_owner,
):
    own = lax.axis_index("group")
    slots, _, width_k = keys.shape
    capacity = slots // groups
    prompts = new_blocks.shape[1]
    tokens = BLOCK // tensors

    def column(c):
        target = lax.rem(own - spread[c] + groups, groups)
        for step in range(capacity):
            j = c + groups * step
            source = lax.rem(j + turn[own], slots)

            def find(p, carry):
                start, place, holder = carry
                blocks = new_blocks[target, p]
                inside = (j >= start) & (j < start + blocks)
                place = jnp.where(inside, prefix_len[target, p] + (j - start) * BLOCK, place)
                holder = jnp.where(inside, owner[target, p], holder)
                return start + blocks, place, holder

            carry = (jnp.int32(0), jnp.int32(0), jnp.int32(-1))
            if prompts <= 8:
                for p in range(prompts):
                    carry = find(p, carry)
            else:
                carry = lax.fori_loop(0, prompts, find, carry)
            _, place, holder = carry
            dest_group[source] = target
            dest_owner[source] = holder
            cos = cosine[pl.ds(place, BLOCK), :]
            sin = sine[pl.ds(place, BLOCK), :]
            block = keys[source].astype(jnp.float32)
            at = pl.multiple_of(source * BLOCK, BLOCK)
            rows[pl.ds(at, BLOCK), :] = jnp.concatenate(
                [
                    turned(block[:, h * HEAD : (h + 1) * HEAD], cos, sin)
                    for h in range(width_k // HEAD)
                ],
                axis=1,
            )
            at = pl.multiple_of((slots + source) * BLOCK, BLOCK)
            rows[pl.ds(at, BLOCK), :] = values[source].astype(jnp.float32)

    loop(groups, column)
    body = rows[...].astype(jnp.bfloat16)
    part = 2 * tokens
    shape = (tensors * groups * part, 2 * slots * BLOCK)
    row = lax.broadcasted_iota(jnp.int32, shape, 0)
    col = lax.broadcasted_iota(jnp.int32, shape, 1)
    row_tensor = row // (groups * part)
    row_group = (row // part) % groups
    same = ((row // tokens) % 2 == col // (slots * BLOCK)) & (
        row_tensor * tokens + row % tokens == col % BLOCK
    )
    code = jnp.where(same, row_group * slots + (col // BLOCK) % slots, -1)

    def send(d):
        def mark(b, total):
            wanted = jnp.where(dest_owner[b] == d, dest_group[b] * slots + b, -2)
            return total | (code == wanted)

        if slots <= 8:
            total = code == -2
            for b in range(slots):
                total = mark(b, total)
            pick = total.astype(jnp.float32)
        else:
            pick = lax.fori_loop(
                0,
                slots,
                lambda b, total: jnp.where(
                    code == jnp.where(dest_owner[b] == d, dest_group[b] * slots + b, -2), 1.0, total
                ),
                jnp.zeros(shape, jnp.float32),
            )
        moved = jnp.dot(pick.astype(jnp.bfloat16), body, preferred_element_type=jnp.float32)
        out[pl.ds(d * tensors, tensors)] = moved.astype(jnp.bfloat16).reshape(
            tensors, groups * part, width_k
        )

    loop(groups, send)


def attention_kernel(
    groups, heads_q, heads_k, spread, new_blocks, prefix_len, arrived, prefix_keys, prefix_values, cosine, sine,
    out, prompt, offset, live,
):
    own = lax.axis_index("group")
    slots = out.shape[0]
    ratio = heads_q // heads_k
    width_q = heads_q * HEAD
    width_k = heads_k * HEAD
    slot_table(own, new_blocks, prefix_len, prompt, offset, live)
    scale = math.log2(math.e) / math.sqrt(HEAD)
    span = CTXP + 2 * BLOCK
    rows = ratio * BLOCK
    lane = lax.broadcasted_iota(jnp.int32, (rows, span), 1)
    token = lax.broadcasted_iota(jnp.int32, (rows, span), 0) % BLOCK
    fresh = (lane >= CTXP + BLOCK) & (lane - (CTXP + BLOCK) <= token)
    before = (lane >= CTXP) & (lane < CTXP + BLOCK)

    def slot(j):
        p, place, state = prompt[j], offset[j], live[j]
        root = lax.rem(own + spread[lax.rem(j, groups)], groups)
        jj = jnp.maximum(j - 1, 0)
        back = lax.rem(own + spread[lax.rem(jj, groups)], groups)
        here = arrived.at[root, j // groups]
        prev = arrived.at[back, jj // groups]
        cos = cosine[pl.ds(place, BLOCK), :]
        sin = sine[pl.ds(place, BLOCK), :]
        early = jnp.maximum(place - BLOCK, 0)
        cos_prev = cosine[pl.ds(early, BLOCK), :]
        sin_prev = sine[pl.ds(early, BLOCK), :]
        region = pl.ds(pl.multiple_of(p * CTXP, CTXP), CTXP)
        cached = prefix_len[own, p]
        mask = fresh | (lane < jnp.minimum(cached, CTXP)) | (before & (state == 2))
        for h in range(heads_k):
            at = slice(width_q + h * HEAD, width_q + (h + 1) * HEAD)
            new_key = jnp.concatenate(
                [
                    turned(prev[:, at].astype(jnp.float32), cos_prev, sin_prev),
                    turned(here[:, at].astype(jnp.float32), cos, sin),
                ],
                axis=0,
            ).astype(jnp.bfloat16)
            at = slice(width_q + width_k + h * HEAD, width_q + width_k + (h + 1) * HEAD)
            new_value = jnp.concatenate(
                [prev[:, at].astype(jnp.float32), here[:, at].astype(jnp.float32)], axis=0
            ).astype(jnp.bfloat16)
            at = slice(h * HEAD, (h + 1) * HEAD)
            key = jnp.concatenate([prefix_keys[region, at], new_key], axis=0)
            value = jnp.concatenate([prefix_values[region, at], new_value], axis=0)
            query = jnp.concatenate(
                [
                    turned(here[:, n * HEAD : (n + 1) * HEAD].astype(jnp.float32), cos, sin)
                    for n in range(h * ratio, (h + 1) * ratio)
                ],
                axis=0,
            ).astype(jnp.bfloat16)
            scores = lax.dot_general(
                query, key, (((1,), (1,)), ((), ())), preferred_element_type=jnp.float32
            )
            scores = jnp.where(mask, scores, -1e30)
            top = jnp.max(scores, axis=1, keepdims=True)
            powers = jnp.exp2((scores - top) * scale)
            weights = powers / jnp.sum(powers, axis=1, keepdims=True)
            mixed = jnp.dot(weights.astype(jnp.bfloat16), value, preferred_element_type=jnp.float32)
            mixed = jnp.where(state > 0, mixed, 0.0)
            for n in range(ratio):
                first = (h * ratio + n) * HEAD
                out[j, :, first : first + HEAD] = mixed[n * BLOCK : (n + 1) * BLOCK].astype(
                    jnp.bfloat16
                )

    loop(slots, slot)


def cache_kernel(groups, tensors, spread, new_blocks, owner, page_start, arrived, out, source):
    own = lax.axis_index("group")
    prompts = new_blocks.shape[1]
    tokens = BLOCK // tensors
    part = 2 * tokens
    pages = prompts * MAXP

    def of_group(g):
        def one(p, start):
            blocks = new_blocks[g, p]
            mine = owner[g, p] == own
            for step in range(MAXP):
                j = start + step
                root = lax.rem(g + spread[lax.rem(j, groups)], groups)
                at = jnp.where(mine, page_start[g, p] + step, pages)
                source[at] = jnp.where(step < blocks, root * groups + g, -1)
            return start + blocks

        start = jnp.int32(0)
        if prompts <= 8:
            for p in range(prompts):
                start = one(p, start)
        else:
            lax.fori_loop(0, prompts, one, start)

    loop(groups, of_group)
    shape = (pages * part, groups * groups * part)
    row = lax.broadcasted_iota(jnp.int32, shape, 0)
    col = lax.broadcasted_iota(jnp.int32, shape, 1)
    limit = groups * groups
    code = jnp.where(row % part == col % part, (row // part) * limit + col // part, -1)

    def mark(page, total):
        wanted = jnp.where(source[page] >= 0, page * limit + source[page], -2)
        return jnp.where(code == wanted, 1.0, total)

    pick = jnp.zeros(shape, jnp.float32)
    if pages <= 8:
        for page in range(pages):
            pick = mark(page, pick)
    else:
        pick = lax.fori_loop(0, pages, mark, pick)
    pick = pick.astype(jnp.bfloat16)
    width_k = arrived.shape[3]
    for t in range(tensors):
        body = arrived[:, t].reshape(groups * groups * part, width_k)
        moved = jnp.dot(pick, body, preferred_element_type=jnp.float32).astype(jnp.bfloat16)
        out[:, t * width_k : (t + 1) * width_k] = moved


def per_device(
    queries,
    keys,
    values,
    prefix_keys,
    prefix_values,
    spread,
    turn,
    new_blocks,
    prefix_len,
    owner,
    page_start,
):
    groups = lax.axis_size("group")
    tensors = lax.axis_size("tensor")
    width_q = queries.shape[1]
    width_k = keys.shape[1]
    heads_q = width_q // HEAD
    heads_k = width_k // HEAD
    slots = queries.shape[0] // BLOCK
    capacity = slots // groups
    prompts = new_blocks.shape[1]
    tokens = BLOCK // tensors
    pages = prompts * MAXP
    cosine, sine = (jnp.asarray(table) for table in rope_table())
    params = pltpu.CompilerParams(vmem_limit_bytes=VMEM_LIMIT)
    blocks_q = queries.reshape(slots, BLOCK, width_q)
    blocks_k = keys.reshape(slots, BLOCK, width_k)
    blocks_v = values.reshape(slots, BLOCK, width_k)

    sent = pl.pallas_call(
        functools.partial(dispatch_kernel, groups),
        out_shape=jax.ShapeDtypeStruct((groups, capacity, BLOCK, width_q + 2 * width_k), jnp.bfloat16),
        in_specs=[SMEM] * 2 + [ANY] * 3,
        out_specs=ANY,
        scratch_shapes=[pltpu.SemaphoreType.DMA],
        compiler_params=params,
        name="dispatch",
    )(spread, turn, blocks_q, blocks_k, blocks_v)
    arrived = lax.all_to_all(sent, "group", split_axis=0, concat_axis=0, tiled=True)

    finished = pl.pallas_call(
        functools.partial(pages_kernel, groups, tensors),
        out_shape=jax.ShapeDtypeStruct((groups * tensors, groups * 2 * tokens, width_k), jnp.bfloat16),
        in_specs=[SMEM] * 5 + [VMEM] * 4,
        out_specs=VMEM,
        scratch_shapes=[
            pltpu.VMEM((2 * slots * BLOCK, width_k), jnp.float32),
            pltpu.SMEM((slots,), jnp.int32),
            pltpu.SMEM((slots,), jnp.int32),
        ],
        compiler_params=params,
        name="finish_pages",
    )(spread, turn, new_blocks, prefix_len, owner, blocks_k, blocks_v, cosine, sine)
    handed = lax.all_to_all(finished, ("group", "tensor"), split_axis=0, concat_axis=0, tiled=True)

    attention = pl.pallas_call(
        functools.partial(attention_kernel, groups, heads_q, heads_k),
        out_shape=jax.ShapeDtypeStruct((slots, BLOCK, width_q), jnp.bfloat16),
        in_specs=[SMEM] * 3 + [VMEM] * 5,
        out_specs=VMEM,
        scratch_shapes=[pltpu.SMEM((slots,), jnp.int32)] * 3,
        compiler_params=params,
        name="attention",
    )(spread, new_blocks, prefix_len, arrived, prefix_keys, prefix_values, cosine, sine)

    cache = pl.pallas_call(
        functools.partial(cache_kernel, groups, tensors),
        out_shape=jax.ShapeDtypeStruct((pages * 2 * tokens, tensors * width_k), jnp.bfloat16),
        in_specs=[SMEM] * 4 + [VMEM],
        out_specs=VMEM,
        scratch_shapes=[pltpu.SMEM((pages + 1,), jnp.int32)],
        compiler_params=params,
        name="place_pages",
    )(
        spread,
        new_blocks,
        owner,
        page_start,
        handed.reshape(groups, tensors, groups * 2 * tokens, width_k),
    )
    return (
        attention.reshape(slots * BLOCK, width_q),
        cache.reshape(pages, 2, tokens, tensors * width_k),
    )


def solution(mesh):
    return jax.shard_map(
        per_device,
        mesh=mesh,
        in_specs=(
            P(("parts", "group"), "tensor"),
            P(("parts", "group"), "tensor"),
            P(("parts", "group"), "tensor"),
            P(("parts", "group"), "tensor"),
            P(("parts", "group"), "tensor"),
            P("parts"),
            P("parts"),
            P("parts", None),
            P("parts", None),
            P("parts", None),
            P("parts", None),
        ),
        out_specs=(P(("parts", "group"), "tensor"), P(("parts", "group"), None, "tensor", None)),
        check_vma=False,
    )
```

```python
import functools
import math

import jax
import jax.numpy as jnp
import numpy as np
from jax import lax
from jax.experimental import pallas as pl
from jax.experimental.pallas import tpu as pltpu
from jax.sharding import PartitionSpec as P

HEAD = 128
BLOCK = 8
MAXP = 2
CTXP = 64

SMEM = pl.BlockSpec(memory_space=pltpu.SMEM)
VMEM = pl.BlockSpec(memory_space=pltpu.VMEM)
ANY = pl.BlockSpec(memory_space=pl.ANY)


def rope_table():
    count = CTXP + MAXP * BLOCK
    half = HEAD // 2
    frequency = np.exp(np.arange(half) * (-2.0 * math.log(500000.0) / HEAD))
    angles = np.arange(count)[:, None] * frequency[None, :]
    cosine, sine = np.cos(angles), np.sin(angles)
    return (
        np.concatenate([cosine, cosine], axis=1).astype(np.float32),
        np.concatenate([-sine, sine], axis=1).astype(np.float32),
    )


def loop(count, body, unrolled=16):
    if count <= unrolled:
        for index in range(count):
            body(index)
    else:
        lax.fori_loop(0, count, lambda index, carry: (body(index), carry)[1], 0)


def turned(head_block, cosine, sine):
    return head_block * cosine + pltpu.roll(head_block, HEAD // 2, 1) * sine


def dispatch_kernel(groups, spread, turn, queries, keys, values, *rest):
    outs, sem = rest[:groups], rest[groups]
    own = lax.axis_index("group")
    slots, _, width_q = queries.shape
    width_k = keys.shape[2]
    capacity = slots // groups
    for distance in range(groups):
        first_slot = column_of(spread, groups, distance) + turn[own]
        for step in range(capacity):
            source = lax.rem(first_slot + groups * step, slots)
            at = outs[distance].at[step]
            for ref, first, width in (
                (queries, 0, width_q),
                (keys, width_q, width_k),
                (values, width_q + width_k, width_k),
            ):
                pltpu.make_async_copy(
                    ref.at[source], at.at[:, pl.ds(first, width)], sem.at[distance]
                ).start()
    for distance in range(groups):
        pltpu.make_async_copy(outs[distance], outs[distance], sem.at[distance]).wait()


def column_of(spread, groups, distance):
    wanted = (groups - distance) % groups
    if groups <= 8:
        return sum(jnp.where(spread[c] == wanted, c, 0) for c in range(groups))
    return lax.fori_loop(
        0, groups, lambda c, found: jnp.where(spread[c] == wanted, c, found), jnp.int32(0)
    )


def slot_table(own, new_blocks, prefix_len, prompt, offset, live):
    prompts = new_blocks.shape[1]
    slots = live.shape[0] - 1

    def clear(j):
        prompt[j] = 0
        offset[j] = 0
        live[j] = 0

    loop(slots, clear)

    def one(p, start):
        blocks = new_blocks[own, p]
        cached = prefix_len[own, p]
        for step in range(MAXP):
            at = jnp.where(step < blocks, start + step, slots)
            prompt[at] = p
            offset[at] = cached + step * BLOCK
            live[at] = 1 + step
        return start + blocks

    start = jnp.int32(0)
    if prompts <= 8:
        for p in range(prompts):
            start = one(p, start)
    else:
        lax.fori_loop(0, prompts, one, start)


def pages_kernel(
    groups, tensors, spread, turn, new_blocks, prefix_len, owner, keys, values, cosine, sine, out, rows,
    dest_group, dest_owner,
):
    own = lax.axis_index("group")
    slots, _, width_k = keys.shape
    capacity = slots // groups
    prompts = new_blocks.shape[1]
    tokens = BLOCK // tensors

    def column(c):
        target = lax.rem(own - spread[c] + groups, groups)
        for step in range(capacity):
            j = c + groups * step
            source = lax.rem(j + turn[own], slots)

            def find(p, carry):
                start, place, holder = carry
                blocks = new_blocks[target, p]
                inside = (j >= start) & (j < start + blocks)
                place = jnp.where(inside, prefix_len[target, p] + (j - start) * BLOCK, place)
                holder = jnp.where(inside, owner[target, p], holder)
                return start + blocks, place, holder

            carry = (jnp.int32(0), jnp.int32(0), jnp.int32(-1))
            if prompts <= 8:
                for p in range(prompts):
                    carry = find(p, carry)
            else:
                carry = lax.fori_loop(0, prompts, find, carry)
            _, place, holder = carry
            dest_group[source] = target
            dest_owner[source] = holder
            cos = cosine[pl.ds(place, BLOCK), :]
            sin = sine[pl.ds(place, BLOCK), :]
            block = keys[source].astype(jnp.float32)
            at = pl.multiple_of(source * BLOCK, BLOCK)
            rows[pl.ds(at, BLOCK), :] = jnp.concatenate(
                [
                    turned(block[:, h * HEAD : (h + 1) * HEAD], cos, sin)
                    for h in range(width_k // HEAD)
                ],
                axis=1,
            )
            at = pl.multiple_of((slots + source) * BLOCK, BLOCK)
            rows[pl.ds(at, BLOCK), :] = values[source].astype(jnp.float32)

    loop(groups, column)
    body = rows[...].astype(jnp.bfloat16)
    part = 2 * tokens
    shape = (tensors * groups * part, 2 * slots * BLOCK)
    row = lax.broadcasted_iota(jnp.int32, shape, 0)
    col = lax.broadcasted_iota(jnp.int32, shape, 1)
    row_tensor = row // (groups * part)
    row_group = (row // part) % groups
    same = ((row // tokens) % 2 == col // (slots * BLOCK)) & (
        row_tensor * tokens + row % tokens == col % BLOCK
    )
    code = jnp.where(same, row_group * slots + (col // BLOCK) % slots, -1)

    def send(d):
        def mark(b, total):
            wanted = jnp.where(dest_owner[b] == d, dest_group[b] * slots + b, -2)
            return total | (code == wanted)

        if slots <= 8:
            total = code == -2
            for b in range(slots):
                total = mark(b, total)
            pick = total.astype(jnp.float32)
        else:
            pick = lax.fori_loop(
                0,
                slots,
                lambda b, total: jnp.where(
                    code == jnp.where(dest_owner[b] == d, dest_group[b] * slots + b, -2), 1.0, total
                ),
                jnp.zeros(shape, jnp.float32),
            )
        moved = jnp.dot(pick.astype(jnp.bfloat16), body, preferred_element_type=jnp.float32)
        out[pl.ds(d * tensors, tensors)] = moved.astype(jnp.bfloat16).reshape(
            tensors, groups * part, width_k
        )

    loop(groups, send)


def attention_kernel(groups, heads_q, heads_k, spread, new_blocks, prefix_len, prefix_keys, prefix_values, cosine, sine, *rest):
    arrived, (out, prompt, offset, live, new_keys, new_values) = rest[:groups], rest[groups:]
    own = lax.axis_index("group")
    slots = out.shape[0]
    capacity = slots // groups
    ratio = heads_q // heads_k
    width_q = heads_q * HEAD
    width_k = heads_k * HEAD
    slot_table(own, new_blocks, prefix_len, prompt, offset, live)
    scale = math.log2(math.e) / math.sqrt(HEAD)
    span = CTXP + 2 * BLOCK
    lane = lax.broadcasted_iota(jnp.int32, (BLOCK, span), 1)
    token = lax.broadcasted_iota(jnp.int32, (BLOCK, span), 0)
    fresh = (lane >= CTXP + BLOCK) & (lane - (CTXP + BLOCK) <= token)
    before = (lane >= CTXP) & (lane < CTXP + BLOCK)

    blocks = []
    for distance in range(groups):
        first_slot = column_of(spread, groups, distance)
        for step in range(capacity):
            j = first_slot + groups * step
            here = arrived[distance].at[step]
            cos = cosine[pl.ds(offset[j], BLOCK), :]
            sin = sine[pl.ds(offset[j], BLOCK), :]
            new_keys[j] = jnp.concatenate(
                [
                    turned(here[:, first : first + HEAD].astype(jnp.float32), cos, sin)
                    for first in range(width_q, width_q + width_k, HEAD)
                ],
                axis=1,
            )
            new_values[j] = here[:, width_q + width_k :].astype(jnp.float32)
            blocks.append((j, here, cos, sin))

    for at in range(0, len(blocks), 8):
        some = blocks[at : at + 8]
        for h in range(heads_k):
            part = slice(h * HEAD, (h + 1) * HEAD)
            scores = []
            for j, here, cos, sin in some:
                prev = jnp.maximum(j - 1, 0)
                region = pl.ds(pl.multiple_of(prompt[j] * CTXP, CTXP), CTXP)
                mask = fresh | (lane < prefix_len[own, prompt[j]]) & (lane < CTXP) | before & (live[j] == 2)
                new_key = jnp.concatenate([new_keys[prev, :, part], new_keys[j, :, part]], axis=0)
                key = jnp.concatenate([prefix_keys[region, part], new_key.astype(jnp.bfloat16)], axis=0)
                query = jnp.concatenate(
                    [
                        turned(here[:, n * HEAD : (n + 1) * HEAD].astype(jnp.float32), cos, sin)
                        for n in range(h * ratio, (h + 1) * ratio)
                    ],
                    axis=0,
                ).astype(jnp.bfloat16)
                score = lax.dot_general(
                    query, key, (((1,), (1,)), ((), ())), preferred_element_type=jnp.float32
                )
                scores.append(jnp.where(mask[None], score.reshape(ratio, BLOCK, span), -1e30))
            score = jnp.concatenate(scores, axis=0)
            top = jnp.max(score, axis=2, keepdims=True)
            powers = jnp.exp2((score - top) * scale)
            weights = powers * (1.0 / jnp.sum(powers, axis=2, keepdims=True))
            weights = weights.reshape(len(some), ratio * BLOCK, span).astype(jnp.bfloat16)
            for place, (j, here, cos, sin) in enumerate(some):
                prev = jnp.maximum(j - 1, 0)
                region = pl.ds(pl.multiple_of(prompt[j] * CTXP, CTXP), CTXP)
                new_value = jnp.concatenate([new_values[prev, :, part], new_values[j, :, part]], axis=0)
                value = jnp.concatenate([prefix_values[region, part], new_value.astype(jnp.bfloat16)], axis=0)
                mixed = jnp.dot(weights[place], value, preferred_element_type=jnp.float32)
                mixed = jnp.where(live[j] > 0, mixed, 0.0)
                for n in range(ratio):
                    first = (h * ratio + n) * HEAD
                    out[j, :, first : first + HEAD] = mixed[n * BLOCK : (n + 1) * BLOCK].astype(
                        jnp.bfloat16
                    )


def cache_kernel(groups, tensors, spread, new_blocks, owner, page_start, arrived, out, source):
    own = lax.axis_index("group")
    prompts = new_blocks.shape[1]
    tokens = BLOCK // tensors
    part = 2 * tokens
    pages = prompts * MAXP

    def of_group(g):
        def one(p, start):
            blocks = new_blocks[g, p]
            mine = owner[g, p] == own
            for step in range(MAXP):
                j = start + step
                root = lax.rem(g + spread[lax.rem(j, groups)], groups)
                at = jnp.where(mine, page_start[g, p] + step, pages)
                source[at] = jnp.where(step < blocks, root * groups + g, -1)
            return start + blocks

        start = jnp.int32(0)
        if prompts <= 8:
            for p in range(prompts):
                start = one(p, start)
        else:
            lax.fori_loop(0, prompts, one, start)

    loop(groups, of_group)
    shape = (pages * part, groups * groups * part)
    row = lax.broadcasted_iota(jnp.int32, shape, 0)
    col = lax.broadcasted_iota(jnp.int32, shape, 1)
    limit = groups * groups
    code = jnp.where(row % part == col % part, (row // part) * limit + col // part, -1)

    def mark(page, total):
        wanted = jnp.where(source[page] >= 0, page * limit + source[page], -2)
        return jnp.where(code == wanted, 1.0, total)

    pick = jnp.zeros(shape, jnp.float32)
    if pages <= 8:
        for page in range(pages):
            pick = mark(page, pick)
    else:
        pick = lax.fori_loop(0, pages, mark, pick)
    pick = pick.astype(jnp.bfloat16)
    width_k = arrived.shape[3]
    for t in range(tensors):
        body = arrived[:, t].reshape(groups * groups * part, width_k)
        moved = jnp.dot(pick, body, preferred_element_type=jnp.float32)
        out[:, :, t * width_k : (t + 1) * width_k] = moved.reshape(
            pages * 2, tokens, width_k
        ).astype(jnp.bfloat16)


def per_device(
    queries,
    keys,
    values,
    prefix_keys,
    prefix_values,
    spread,
    turn,
    new_blocks,
    prefix_len,
    owner,
    page_start,
):
    groups = lax.axis_size("group")
    tensors = lax.axis_size("tensor")
    width_q = queries.shape[1]
    width_k = keys.shape[1]
    heads_q = width_q // HEAD
    heads_k = width_k // HEAD
    slots = queries.shape[0] // BLOCK
    capacity = slots // groups
    prompts = new_blocks.shape[1]
    tokens = BLOCK // tensors
    pages = prompts * MAXP
    cosine, sine = (jnp.asarray(table) for table in rope_table())
    blocks_q = queries.reshape(slots, BLOCK, width_q)
    blocks_k = keys.reshape(slots, BLOCK, width_k)
    blocks_v = values.reshape(slots, BLOCK, width_k)

    chunk = jax.ShapeDtypeStruct((capacity, BLOCK, width_q + 2 * width_k), jnp.bfloat16)
    sent = pl.pallas_call(
        functools.partial(dispatch_kernel, groups),
        out_shape=[chunk] * groups,
        in_specs=[SMEM] * 2 + [ANY] * 3,
        out_specs=[ANY] * groups,
        scratch_shapes=[pltpu.SemaphoreType.DMA((groups,))],
        name="dispatch",
    )(spread, turn, blocks_q, blocks_k, blocks_v)
    arrived = [sent[0]] + [
        lax.ppermute(sent[d], "group", [(g, (g + d) % groups) for g in range(groups)])
        for d in range(1, groups)
    ]

    finished = pl.pallas_call(
        functools.partial(pages_kernel, groups, tensors),
        out_shape=jax.ShapeDtypeStruct((groups * tensors, groups * 2 * tokens, width_k), jnp.bfloat16),
        in_specs=[SMEM] * 5 + [VMEM] * 4,
        out_specs=VMEM,
        scratch_shapes=[
            pltpu.VMEM((2 * slots * BLOCK, width_k), jnp.float32),
            pltpu.SMEM((slots,), jnp.int32),
            pltpu.SMEM((slots,), jnp.int32),
        ],
        cost_estimate=pl.CostEstimate(flops=10**7, bytes_accessed=6 * 10**6, transcendentals=0),
        name="finish_pages",
    )(spread, turn, new_blocks, prefix_len, owner, blocks_k, blocks_v, cosine, sine)
    handed = lax.all_to_all(finished, ("group", "tensor"), split_axis=0, concat_axis=0, tiled=True)

    attention = pl.pallas_call(
        functools.partial(attention_kernel, groups, heads_q, heads_k),
        out_shape=jax.ShapeDtypeStruct((slots, BLOCK, width_q), jnp.bfloat16),
        in_specs=[SMEM] * 3 + [VMEM] * (4 + groups),
        out_specs=VMEM,
        scratch_shapes=[pltpu.SMEM((slots + 1,), jnp.int32)] * 3
        + [pltpu.VMEM((slots, BLOCK, width_k), jnp.float32)] * 2,
        cost_estimate=pl.CostEstimate(flops=10**8, bytes_accessed=15 * 10**6, transcendentals=0),
        name="attention",
    )(spread, new_blocks, prefix_len, prefix_keys, prefix_values, cosine, sine, *arrived)

    cache = pl.pallas_call(
        functools.partial(cache_kernel, groups, tensors),
        out_shape=jax.ShapeDtypeStruct((pages * 2, tokens, tensors * width_k), jnp.bfloat16),
        in_specs=[SMEM] * 4 + [VMEM],
        out_specs=VMEM,
        scratch_shapes=[pltpu.SMEM((pages + 1,), jnp.int32)],
        name="place_pages",
    )(
        spread,
        new_blocks,
        owner,
        page_start,
        handed.reshape(groups, tensors, groups * 2 * tokens, width_k),
    )
    return (
        attention.reshape(slots * BLOCK, width_q),
        cache.reshape(pages, 2, tokens, tensors * width_k),
    )


def solution(mesh):
    return jax.shard_map(
        per_device,
        mesh=mesh,
        in_specs=(
            P(("parts", "group"), "tensor"),
            P(("parts", "group"), "tensor"),
            P(("parts", "group"), "tensor"),
            P(("parts", "group"), "tensor"),
            P(("parts", "group"), "tensor"),
            P("parts"),
            P("parts"),
            P("parts", None),
            P("parts", None),
            P("parts", None),
            P("parts", None),
        ),
        out_specs=(P(("parts", "group"), "tensor"), P(("parts", "group"), None, "tensor", None)),
        check_vma=False,
    )
```

```python
import functools
import math

import jax
import jax.numpy as jnp
import numpy as np
from jax import lax
from jax.experimental import pallas as pl
from jax.experimental.pallas import tpu as pltpu
from jax.sharding import PartitionSpec as P

HEAD = 128
BLOCK = 8
MAXP = 2
CTXP = 64

VMEM_LIMIT = 24 * 1024 * 1024

SMEM = pl.BlockSpec(memory_space=pltpu.SMEM)
VMEM = pl.BlockSpec(memory_space=pltpu.VMEM)
PROMPT, OFFSET, LIVE, CACHED, SOURCE, COLUMN = range(6)
ANY = pl.BlockSpec(memory_space=pl.ANY)
HBM = pl.BlockSpec(memory_space=pltpu.HBM)


def rope_table():
    count = CTXP + MAXP * BLOCK
    half = HEAD // 2
    frequency = np.exp(np.arange(half) * (-2.0 * math.log(500000.0) / HEAD))
    angles = np.arange(count)[:, None] * frequency[None, :]
    cosine, sine = np.cos(angles), np.sin(angles)
    return (
        np.concatenate([cosine, cosine], axis=1).astype(np.float32),
        np.concatenate([-sine, sine], axis=1).astype(np.float32),
    )


def loop(count, body, unrolled=16):
    if count <= unrolled:
        for index in range(count):
            body(index)
    else:
        lax.fori_loop(0, count, lambda index, carry: (body(index), carry)[1], 0)


def turned(head_block, cosine, sine):
    return head_block * cosine + pltpu.roll(head_block, HEAD // 2, 1) * sine


def dispatch_kernel(groups, spread_in, turn_in, queries_in, keys_in, values_in, *rest):
    outs, (spread, turn, queries, keys, values, sem) = rest[:groups], rest[groups:]
    own = lax.axis_index("group")
    slots, _, width_q = queries.shape
    width_k = keys.shape[2]
    capacity = slots // groups
    copies = [
        pltpu.make_async_copy(source, target, sem.at[n])
        for n, (source, target) in enumerate(
            (
                (spread_in, spread),
                (turn_in, turn),
                (queries_in, queries),
                (keys_in, keys),
                (values_in, values),
            )
        )
    ]
    for copy in copies:
        copy.start()
    for copy in copies[:2]:
        copy.wait()
    sources = []
    for distance in range(groups):
        first_slot = column_of(spread, groups, distance) + turn[own]
        sources.append([lax.rem(first_slot + groups * step, slots) for step in range(capacity)])
    for copy in copies[2:]:
        copy.wait()
    for distance in range(groups):
        for step in range(capacity):
            source = sources[distance][step]
            out = outs[distance]
            out[step, :, :width_q] = queries[source]
            out[step, :, width_q : width_q + width_k] = keys[source]
            out[step, :, width_q + width_k :] = values[source]


def column_of(spread, groups, distance):
    wanted = (groups - distance) % groups
    if groups <= 8:
        return sum(jnp.where(spread[c] == wanted, c, 0) for c in range(groups))
    return lax.fori_loop(
        0, groups, lambda c, found: jnp.where(spread[c] == wanted, c, found), jnp.int32(0)
    )


def make_plan(groups, own, spread, new_blocks, prefix_len, owner, page_start, plan):
    prompts = new_blocks.shape[1]
    slots = prompts * MAXP

    def clear(j):
        plan[PROMPT, j] = 0
        plan[OFFSET, j] = 0
        plan[LIVE, j] = 0
        plan[CACHED, j] = 0

    loop(slots, clear)

    def one(p, start):
        blocks = new_blocks[own, p]
        cached = prefix_len[own, p]
        for step in range(MAXP):
            at = jnp.where(step < blocks, start + step, slots)
            plan[PROMPT, at] = p
            plan[OFFSET, at] = cached + step * BLOCK
            plan[LIVE, at] = 1 + step
            plan[CACHED, at] = cached
        return start + blocks

    start = jnp.int32(0)
    if prompts <= 8:
        for p in range(prompts):
            start = one(p, start)
    else:
        lax.fori_loop(0, prompts, one, start)

    def of_group(g):
        def one(p, start):
            blocks = new_blocks[g, p]
            mine = owner[g, p] == own
            for step in range(MAXP):
                root = lax.rem(g + spread[lax.rem(start + step, groups)], groups)
                at = jnp.where(mine, page_start[g, p] + step, slots)
                plan[SOURCE, at] = jnp.where(step < blocks, root * groups + g, -1)
            return start + blocks

        start = jnp.int32(0)
        if prompts <= 8:
            for p in range(prompts):
                start = one(p, start)
        else:
            lax.fori_loop(0, prompts, one, start)

    loop(groups, of_group)
    for distance in range(groups):
        plan[COLUMN, distance] = column_of(spread, groups, distance)


def pages_kernel(
    groups, tensors, spread, turn, new_blocks, prefix_len, owner, page_start, keys, values, cosine, sine,
    _, out, plan, rows, dest_group, dest_owner,
):
    own = lax.axis_index("group")
    slots, _, width_k = keys.shape
    capacity = slots // groups
    prompts = new_blocks.shape[1]
    tokens = BLOCK // tensors

    def column(c):
        target = lax.rem(own - spread[c] + groups, groups)
        for step in range(capacity):
            j = c + groups * step
            source = lax.rem(j + turn[own], slots)

            def find(p, carry):
                start, place, holder = carry
                blocks = new_blocks[target, p]
                inside = (j >= start) & (j < start + blocks)
                place = jnp.where(inside, prefix_len[target, p] + (j - start) * BLOCK, place)
                holder = jnp.where(inside, owner[target, p], holder)
                return start + blocks, place, holder

            carry = (jnp.int32(0), jnp.int32(0), jnp.int32(-1))
            if prompts <= 8:
                for p in range(prompts):
                    carry = find(p, carry)
            else:
                carry = lax.fori_loop(0, prompts, find, carry)
            _, place, holder = carry
            dest_group[source] = target
            dest_owner[source] = holder
            cos = cosine[pl.ds(place, BLOCK), :]
            sin = sine[pl.ds(place, BLOCK), :]
            block = keys[source].astype(jnp.float32)
            at = pl.multiple_of(source * BLOCK, BLOCK)
            rows[pl.ds(at, BLOCK), :] = jnp.concatenate(
                [
                    turned(block[:, h * HEAD : (h + 1) * HEAD], cos, sin)
                    for h in range(width_k // HEAD)
                ],
                axis=1,
            )
            at = pl.multiple_of((slots + source) * BLOCK, BLOCK)
            rows[pl.ds(at, BLOCK), :] = values[source].astype(jnp.float32)

    loop(groups, column)
    body = rows[...].astype(jnp.bfloat16)
    part = 2 * tokens
    shape = (tensors * groups * part, 2 * slots * BLOCK)
    row = lax.broadcasted_iota(jnp.int32, shape, 0)
    col = lax.broadcasted_iota(jnp.int32, shape, 1)
    row_tensor = row // (groups * part)
    row_group = (row // part) % groups
    same = ((row // tokens) % 2 == col // (slots * BLOCK)) & (
        row_tensor * tokens + row % tokens == col % BLOCK
    )
    code = jnp.where(same, row_group * slots + (col // BLOCK) % slots, -1)

    def send(d):
        def mark(b, total):
            wanted = jnp.where(dest_owner[b] == d, dest_group[b] * slots + b, -2)
            return total | (code == wanted)

        if slots <= 8:
            total = code == -2
            for b in range(slots):
                total = mark(b, total)
            pick = total.astype(jnp.float32)
        else:
            pick = lax.fori_loop(
                0,
                slots,
                lambda b, total: jnp.where(
                    code == jnp.where(dest_owner[b] == d, dest_group[b] * slots + b, -2), 1.0, total
                ),
                jnp.zeros(shape, jnp.float32),
            )
        moved = jnp.dot(pick.astype(jnp.bfloat16), body, preferred_element_type=jnp.float32)
        out[pl.ds(d * tensors, tensors)] = moved.astype(jnp.bfloat16).reshape(
            tensors, groups * part, width_k
        )

    loop(groups, send)
    make_plan(groups, own, spread, new_blocks, prefix_len, owner, page_start, plan)


def attention_kernel(groups, heads_q, heads_k, plan, prefix_keys, prefix_values, cosine, sine, *rest):
    arrived, (out, new_keys, new_values) = rest[:groups], rest[groups:]
    slots = out.shape[0]
    capacity = slots // groups
    ratio = heads_q // heads_k
    width_q = heads_q * HEAD
    width_k = heads_k * HEAD
    scale = math.log2(math.e) / math.sqrt(HEAD)
    span = CTXP + 2 * BLOCK
    lane = lax.broadcasted_iota(jnp.int32, (BLOCK, span), 1)
    token = lax.broadcasted_iota(jnp.int32, (BLOCK, span), 0)
    fresh = (lane >= CTXP + BLOCK) & (lane - (CTXP + BLOCK) <= token)
    before = (lane >= CTXP) & (lane < CTXP + BLOCK)

    blocks = []
    for distance in range(groups):
        first_slot = plan[COLUMN, distance]
        for step in range(capacity):
            j = first_slot + groups * step
            here = arrived[distance].at[step]
            cos = cosine[pl.ds(plan[OFFSET, j], BLOCK), :]
            sin = sine[pl.ds(plan[OFFSET, j], BLOCK), :]
            new_keys[j] = jnp.concatenate(
                [
                    turned(here[:, first : first + HEAD].astype(jnp.float32), cos, sin)
                    for first in range(width_q, width_q + width_k, HEAD)
                ],
                axis=1,
            )
            new_values[j] = here[:, width_q + width_k :].astype(jnp.float32)
            blocks.append((j, here, cos, sin))

    for at in range(0, len(blocks), 8):
        some = blocks[at : at + 8]
        for h in range(heads_k):
            part = slice(h * HEAD, (h + 1) * HEAD)
            scores = []
            for j, here, cos, sin in some:
                prev = jnp.maximum(j - 1, 0)
                region = pl.ds(pl.multiple_of(plan[PROMPT, j] * CTXP, CTXP), CTXP)
                mask = fresh | (lane < plan[CACHED, j]) & (lane < CTXP) | before & (plan[LIVE, j] == 2)
                new_key = jnp.concatenate([new_keys[prev, :, part], new_keys[j, :, part]], axis=0)
                key = jnp.concatenate([prefix_keys[region, part], new_key.astype(jnp.bfloat16)], axis=0)
                query = jnp.concatenate(
                    [
                        turned(here[:, n * HEAD : (n + 1) * HEAD].astype(jnp.float32), cos, sin)
                        for n in range(h * ratio, (h + 1) * ratio)
                    ],
                    axis=0,
                ).astype(jnp.bfloat16)
                score = lax.dot_general(
                    query, key, (((1,), (1,)), ((), ())), preferred_element_type=jnp.float32
                )
                scores.append(jnp.where(mask[None], score.reshape(ratio, BLOCK, span), -1e30))
            score = jnp.concatenate(scores, axis=0)
            top = jnp.max(score, axis=2, keepdims=True)
            powers = jnp.exp2((score - top) * scale)
            weights = powers * (1.0 / jnp.sum(powers, axis=2, keepdims=True))
            weights = weights.reshape(len(some), ratio * BLOCK, span).astype(jnp.bfloat16)
            for place, (j, here, cos, sin) in enumerate(some):
                prev = jnp.maximum(j - 1, 0)
                region = pl.ds(pl.multiple_of(plan[PROMPT, j] * CTXP, CTXP), CTXP)
                new_value = jnp.concatenate([new_values[prev, :, part], new_values[j, :, part]], axis=0)
                value = jnp.concatenate([prefix_values[region, part], new_value.astype(jnp.bfloat16)], axis=0)
                mixed = jnp.dot(weights[place], value, preferred_element_type=jnp.float32)
                mixed = jnp.where(plan[LIVE, j] > 0, mixed, 0.0)
                for n in range(ratio):
                    first = (h * ratio + n) * HEAD
                    out[j, :, first : first + HEAD] = mixed[n * BLOCK : (n + 1) * BLOCK].astype(
                        jnp.bfloat16
                    )


def cache_kernel(groups, tensors, plan, arrived, out):
    tokens = BLOCK // tensors
    part = 2 * tokens
    pages = out.shape[0] // 2
    shape = (pages * part, groups * groups * part)
    row = lax.broadcasted_iota(jnp.int32, shape, 0)
    col = lax.broadcasted_iota(jnp.int32, shape, 1)
    limit = groups * groups
    code = jnp.where(row % part == col % part, (row // part) * limit + col // part, -1)

    def mark(page, total):
        wanted = jnp.where(plan[SOURCE, page] >= 0, page * limit + plan[SOURCE, page], -2)
        return jnp.where(code == wanted, 1.0, total)

    pick = jnp.zeros(shape, jnp.float32)
    if pages <= 8:
        for page in range(pages):
            pick = mark(page, pick)
    else:
        pick = lax.fori_loop(0, pages, mark, pick)
    pick = pick.astype(jnp.bfloat16)
    width_k = arrived.shape[3]
    for t in range(tensors):
        body = arrived[:, t].reshape(groups * groups * part, width_k)
        moved = jnp.dot(pick, body, preferred_element_type=jnp.float32)
        out[:, :, t * width_k : (t + 1) * width_k] = moved.reshape(
            pages * 2, tokens, width_k
        ).astype(jnp.bfloat16)


def per_device(
    queries,
    keys,
    values,
    prefix_keys,
    prefix_values,
    spread,
    turn,
    new_blocks,
    prefix_len,
    owner,
    page_start,
):
    groups = lax.axis_size("group")
    tensors = lax.axis_size("tensor")
    width_q = queries.shape[1]
    width_k = keys.shape[1]
    heads_q = width_q // HEAD
    heads_k = width_k // HEAD
    slots = queries.shape[0] // BLOCK
    capacity = slots // groups
    prompts = new_blocks.shape[1]
    tokens = BLOCK // tensors
    pages = prompts * MAXP
    cosine, sine = (jnp.asarray(table) for table in rope_table())
    params = pltpu.CompilerParams(vmem_limit_bytes=VMEM_LIMIT)
    blocks_q = queries.reshape(slots, BLOCK, width_q)
    blocks_k = keys.reshape(slots, BLOCK, width_k)
    blocks_v = values.reshape(slots, BLOCK, width_k)

    chunk = jax.ShapeDtypeStruct((capacity, BLOCK, width_q + 2 * width_k), jnp.bfloat16)
    sent = pl.pallas_call(
        functools.partial(dispatch_kernel, groups),
        out_shape=[chunk] * groups,
        in_specs=[HBM] * 5,
        out_specs=[VMEM] * groups,
        scratch_shapes=[pltpu.SMEM((groups,), jnp.int32)] * 2
        + [pltpu.VMEM(blocks.shape, jnp.bfloat16) for blocks in (blocks_q, blocks_k, blocks_v)]
        + [pltpu.SemaphoreType.DMA((5,))],
        compiler_params=params,
        cost_estimate=pl.CostEstimate(flops=10**6, bytes_accessed=5 * 10**6, transcendentals=0),
        name="dispatch",
    )(
        *(
            pltpu.with_memory_space_constraint(operand, pltpu.HBM)
            for operand in (spread, turn, blocks_q, blocks_k, blocks_v)
        )
    )
    arrived = [sent[0]] + [
        lax.ppermute(sent[d], "group", [(g, (g + d) % groups) for g in range(groups)])
        for d in range(1, groups)
    ]

    finished, plan = pl.pallas_call(
        functools.partial(pages_kernel, groups, tensors),
        out_shape=[
            jax.ShapeDtypeStruct((groups * tensors, groups * 2 * tokens, width_k), jnp.bfloat16),
            jax.ShapeDtypeStruct((6, max(slots, groups) + 1), jnp.int32),
        ],
        in_specs=[SMEM] * 6 + [VMEM] * 4 + [ANY],
        out_specs=[VMEM, SMEM],
        compiler_params=params,
        scratch_shapes=[
            pltpu.VMEM((2 * slots * BLOCK, width_k), jnp.float32),
            pltpu.SMEM((slots,), jnp.int32),
            pltpu.SMEM((slots,), jnp.int32),
        ],
        cost_estimate=pl.CostEstimate(flops=10**7, bytes_accessed=6 * 10**6, transcendentals=0),
        name="finish_pages",
    )(
        spread, turn, new_blocks, prefix_len, owner, page_start, blocks_k, blocks_v, cosine, sine, sent[0]
    )
    handed = lax.all_to_all(finished, ("group", "tensor"), split_axis=0, concat_axis=0, tiled=True)

    attention = pl.pallas_call(
        functools.partial(attention_kernel, groups, heads_q, heads_k),
        out_shape=jax.ShapeDtypeStruct((slots, BLOCK, width_q), jnp.bfloat16),
        in_specs=[SMEM] + [VMEM] * (4 + groups),
        out_specs=VMEM,
        scratch_shapes=[pltpu.VMEM((slots, BLOCK, width_k), jnp.float32)] * 2,
        compiler_params=params,
        cost_estimate=pl.CostEstimate(flops=10**8, bytes_accessed=15 * 10**6, transcendentals=0),
        name="attention",
    )(plan, prefix_keys, prefix_values, cosine, sine, *arrived)

    cache = pl.pallas_call(
        functools.partial(cache_kernel, groups, tensors),
        out_shape=jax.ShapeDtypeStruct((pages * 2, tokens, tensors * width_k), jnp.bfloat16),
        in_specs=[SMEM, VMEM],
        out_specs=VMEM,
        compiler_params=params,
        cost_estimate=pl.CostEstimate(flops=10**6, bytes_accessed=5 * 10**6, transcendentals=0),
        name="place_pages",
    )(plan, handed.reshape(groups, tensors, groups * 2 * tokens, width_k))
    return (
        attention.reshape(slots * BLOCK, width_q),
        cache.reshape(pages, 2, tokens, tensors * width_k),
    )


def solution(mesh):
    return jax.shard_map(
        per_device,
        mesh=mesh,
        in_specs=(
            P(("parts", "group"), "tensor"),
            P(("parts", "group"), "tensor"),
            P(("parts", "group"), "tensor"),
            P(("parts", "group"), "tensor"),
            P(("parts", "group"), "tensor"),
            P("parts"),
            P("parts"),
            P("parts", None),
            P("parts", None),
            P("parts", None),
            P("parts", None),
        ),
        out_specs=(P(("parts", "group"), "tensor"), P(("parts", "group"), None, "tensor", None)),
        check_vma=False,
    )
```

```python
import functools
import math

import jax
import jax.numpy as jnp
import numpy as np
from jax import lax
from jax.experimental import pallas as pl
from jax.experimental.pallas import tpu as pltpu
from jax.sharding import PartitionSpec as P

HEAD = 128
BLOCK = 8
MAXP = 2
CTXP = 64

VMEM_LIMIT = 24 * 1024 * 1024

SMEM = pl.BlockSpec(memory_space=pltpu.SMEM)
VMEM = pl.BlockSpec(memory_space=pltpu.VMEM)
PROMPT, OFFSET, LIVE, CACHED, SOURCE, COLUMN = range(6)
ANY = pl.BlockSpec(memory_space=pl.ANY)
HBM = pl.BlockSpec(memory_space=pltpu.HBM)


def rope_table():
    count = CTXP + MAXP * BLOCK
    half = HEAD // 2
    frequency = np.exp(np.arange(half) * (-2.0 * math.log(500000.0) / HEAD))
    angles = np.arange(count)[:, None] * frequency[None, :]
    cosine, sine = np.cos(angles), np.sin(angles)
    return (
        np.concatenate([cosine, cosine], axis=1).astype(np.float32),
        np.concatenate([-sine, sine], axis=1).astype(np.float32),
    )


def loop(count, body, unrolled=16):
    if count <= unrolled:
        for index in range(count):
            body(index)
    else:
        lax.fori_loop(0, count, lambda index, carry: (body(index), carry)[1], 0)


def turned(head_block, cosine, sine):
    return head_block * cosine + pltpu.roll(head_block, HEAD // 2, 1) * sine


def dispatch_kernel(groups, spread_in, turn_in, queries_in, keys_in, values_in, *rest):
    outs, (spread, turn, queries, keys, values, sem) = rest[:groups], rest[groups:]
    own = lax.axis_index("group")
    slots, _, width_q = queries.shape
    width_k = keys.shape[2]
    capacity = slots // groups
    copies = [
        pltpu.make_async_copy(source, target, sem.at[n])
        for n, (source, target) in enumerate(
            (
                (spread_in, spread),
                (turn_in, turn),
                (queries_in, queries),
                (keys_in, keys),
                (values_in, values),
            )
        )
    ]
    for copy in copies:
        copy.start()
    for copy in copies[:2]:
        copy.wait()
    sources = []
    for distance in range(groups):
        first_slot = column_of(spread, groups, distance) + turn[own]
        sources.append([lax.rem(first_slot + groups * step, slots) for step in range(capacity)])
    for copy in copies[2:]:
        copy.wait()
    for distance in range(groups):
        for step in range(capacity):
            source = sources[distance][step]
            out = outs[distance]
            out[step, :, :width_q] = queries[source]
            out[step, :, width_q : width_q + width_k] = keys[source]
            out[step, :, width_q + width_k :] = values[source]


def column_of(spread, groups, distance):
    wanted = (groups - distance) % groups
    if groups <= 8:
        return sum(jnp.where(spread[c] == wanted, c, 0) for c in range(groups))
    return lax.fori_loop(
        0, groups, lambda c, found: jnp.where(spread[c] == wanted, c, found), jnp.int32(0)
    )


def make_plan(groups, own, spread, new_blocks, prefix_len, owner, page_start, plan):
    prompts = new_blocks.shape[1]
    slots = prompts * MAXP

    def clear(j):
        plan[PROMPT, j] = 0
        plan[OFFSET, j] = 0
        plan[LIVE, j] = 0
        plan[CACHED, j] = 0

    loop(slots, clear)

    def one(p, start):
        blocks = new_blocks[own, p]
        cached = prefix_len[own, p]
        for step in range(MAXP):
            at = jnp.where(step < blocks, start + step, slots)
            plan[PROMPT, at] = p
            plan[OFFSET, at] = cached + step * BLOCK
            plan[LIVE, at] = 1 + step
            plan[CACHED, at] = cached
        return start + blocks

    start = jnp.int32(0)
    if prompts <= 8:
        for p in range(prompts):
            start = one(p, start)
    else:
        lax.fori_loop(0, prompts, one, start)

    def of_group(g):
        def one(p, start):
            blocks = new_blocks[g, p]
            mine = owner[g, p] == own
            for step in range(MAXP):
                root = lax.rem(g + spread[lax.rem(start + step, groups)], groups)
                at = jnp.where(mine, page_start[g, p] + step, slots)
                plan[SOURCE, at] = jnp.where(step < blocks, root * groups + g, -1)
            return start + blocks

        start = jnp.int32(0)
        if prompts <= 8:
            for p in range(prompts):
                start = one(p, start)
        else:
            lax.fori_loop(0, prompts, one, start)

    loop(groups, of_group)
    for distance in range(groups):
        plan[COLUMN, distance] = column_of(spread, groups, distance)


def pages_kernel(
    groups, tensors, spread, turn, new_blocks, prefix_len, owner, page_start, keys, values, cosine, sine,
    _, out, plan, rows, dest_group, dest_owner,
):
    own = lax.axis_index("group")
    slots, _, width_k = keys.shape
    capacity = slots // groups
    prompts = new_blocks.shape[1]
    tokens = BLOCK // tensors

    def column(c):
        target = lax.rem(own - spread[c] + groups, groups)
        for step in range(capacity):
            j = c + groups * step
            source = lax.rem(j + turn[own], slots)

            def find(p, carry):
                start, place, holder = carry
                blocks = new_blocks[target, p]
                inside = (j >= start) & (j < start + blocks)
                place = jnp.where(inside, prefix_len[target, p] + (j - start) * BLOCK, place)
                holder = jnp.where(inside, owner[target, p], holder)
                return start + blocks, place, holder

            carry = (jnp.int32(0), jnp.int32(0), jnp.int32(-1))
            if prompts <= 8:
                for p in range(prompts):
                    carry = find(p, carry)
            else:
                carry = lax.fori_loop(0, prompts, find, carry)
            _, place, holder = carry
            dest_group[source] = target
            dest_owner[source] = holder
            cos = cosine[pl.ds(place, BLOCK), :]
            sin = sine[pl.ds(place, BLOCK), :]
            block = keys[source].astype(jnp.float32)
            at = pl.multiple_of(source * BLOCK, BLOCK)
            rows[pl.ds(at, BLOCK), :] = jnp.concatenate(
                [
                    turned(block[:, h * HEAD : (h + 1) * HEAD], cos, sin)
                    for h in range(width_k // HEAD)
                ],
                axis=1,
            )
            at = pl.multiple_of((slots + source) * BLOCK, BLOCK)
            rows[pl.ds(at, BLOCK), :] = values[source].astype(jnp.float32)

    loop(groups, column)
    body = rows[...].astype(jnp.bfloat16)
    part = 2 * tokens
    shape = (tensors * groups * part, 2 * slots * BLOCK)
    row = lax.broadcasted_iota(jnp.int32, shape, 0)
    col = lax.broadcasted_iota(jnp.int32, shape, 1)
    row_tensor = row // (groups * part)
    row_group = (row // part) % groups
    same = ((row // tokens) % 2 == col // (slots * BLOCK)) & (
        row_tensor * tokens + row % tokens == col % BLOCK
    )
    code = jnp.where(same, row_group * slots + (col // BLOCK) % slots, -1)

    def send(d):
        def mark(b, total):
            wanted = jnp.where(dest_owner[b] == d, dest_group[b] * slots + b, -2)
            return total | (code == wanted)

        if slots <= 8:
            total = code == -2
            for b in range(slots):
                total = mark(b, total)
            pick = total.astype(jnp.float32)
        else:
            pick = lax.fori_loop(
                0,
                slots,
                lambda b, total: jnp.where(
                    code == jnp.where(dest_owner[b] == d, dest_group[b] * slots + b, -2), 1.0, total
                ),
                jnp.zeros(shape, jnp.float32),
            )
        moved = jnp.dot(pick.astype(jnp.bfloat16), body, preferred_element_type=jnp.float32)
        out[pl.ds(d * tensors, tensors)] = moved.astype(jnp.bfloat16).reshape(
            tensors, groups * part, width_k
        )

    loop(groups, send)
    make_plan(groups, own, spread, new_blocks, prefix_len, owner, page_start, plan)


def attention_kernel(groups, heads_q, heads_k, plan, prefix_keys, prefix_values, cosine, sine, *rest):
    arrived, (out, new_keys, new_values) = rest[:groups], rest[groups:]
    slots = out.shape[0]
    capacity = slots // groups
    ratio = heads_q // heads_k
    width_q = heads_q * HEAD
    width_k = heads_k * HEAD
    scale = math.log2(math.e) / math.sqrt(HEAD)
    span = CTXP + 2 * BLOCK
    lane = lax.broadcasted_iota(jnp.int32, (BLOCK, span), 1)
    token = lax.broadcasted_iota(jnp.int32, (BLOCK, span), 0)
    fresh = (lane >= CTXP + BLOCK) & (lane - (CTXP + BLOCK) <= token)
    before = (lane >= CTXP) & (lane < CTXP + BLOCK)

    blocks = []
    for distance in range(groups):
        first_slot = plan[COLUMN, distance]
        for step in range(capacity):
            j = first_slot + groups * step
            here = arrived[distance].at[step]
            cos = cosine[pl.ds(plan[OFFSET, j], BLOCK), :]
            sin = sine[pl.ds(plan[OFFSET, j], BLOCK), :]
            new_keys[j] = jnp.concatenate(
                [
                    turned(here[:, first : first + HEAD].astype(jnp.float32), cos, sin)
                    for first in range(width_q, width_q + width_k, HEAD)
                ],
                axis=1,
            )
            new_values[j] = here[:, width_q + width_k :].astype(jnp.float32)
            blocks.append((j, here, cos, sin))

    for at in range(0, len(blocks), 8):
        some = blocks[at : at + 8]
        for h in range(heads_k):
            part = slice(h * HEAD, (h + 1) * HEAD)
            scores = []
            for j, here, cos, sin in some:
                prev = jnp.maximum(j - 1, 0)
                region = pl.ds(pl.multiple_of(plan[PROMPT, j] * CTXP, CTXP), CTXP)
                mask = fresh | (lane < plan[CACHED, j]) & (lane < CTXP) | before & (plan[LIVE, j] == 2)
                new_key = jnp.concatenate([new_keys[prev, :, part], new_keys[j, :, part]], axis=0)
                key = jnp.concatenate([prefix_keys[region, part], new_key.astype(jnp.bfloat16)], axis=0)
                query = jnp.concatenate(
                    [
                        turned(here[:, n * HEAD : (n + 1) * HEAD].astype(jnp.float32), cos, sin)
                        for n in range(h * ratio, (h + 1) * ratio)
                    ],
                    axis=0,
                ).astype(jnp.bfloat16)
                score = lax.dot_general(
                    query, key, (((1,), (1,)), ((), ())), preferred_element_type=jnp.float32
                )
                scores.append(jnp.where(mask[None], score.reshape(ratio, BLOCK, span), -1e30))
            score = jnp.concatenate(scores, axis=0)
            top = jnp.max(score, axis=2, keepdims=True)
            powers = jnp.exp2((score - top) * scale)
            weights = powers * (1.0 / jnp.sum(powers, axis=2, keepdims=True))
            weights = weights.reshape(len(some), ratio * BLOCK, span).astype(jnp.bfloat16)
            for place, (j, here, cos, sin) in enumerate(some):
                prev = jnp.maximum(j - 1, 0)
                region = pl.ds(pl.multiple_of(plan[PROMPT, j] * CTXP, CTXP), CTXP)
                new_value = jnp.concatenate([new_values[prev, :, part], new_values[j, :, part]], axis=0)
                value = jnp.concatenate([prefix_values[region, part], new_value.astype(jnp.bfloat16)], axis=0)
                mixed = jnp.dot(weights[place], value, preferred_element_type=jnp.float32)
                mixed = jnp.where(plan[LIVE, j] > 0, mixed, 0.0)
                for n in range(ratio):
                    first = (h * ratio + n) * HEAD
                    out[j, :, first : first + HEAD] = mixed[n * BLOCK : (n + 1) * BLOCK].astype(
                        jnp.bfloat16
                    )


def cache_kernel(groups, tensors, plan, arrived, out):
    tokens = BLOCK // tensors
    part = 2 * tokens
    pages = out.shape[0] // 2
    shape = (pages * part, groups * groups * part)
    row = lax.broadcasted_iota(jnp.int32, shape, 0)
    col = lax.broadcasted_iota(jnp.int32, shape, 1)
    limit = groups * groups
    code = jnp.where(row % part == col % part, (row // part) * limit + col // part, -1)

    def mark(page, total):
        wanted = jnp.where(plan[SOURCE, page] >= 0, page * limit + plan[SOURCE, page], -2)
        return jnp.where(code == wanted, 1.0, total)

    pick = jnp.zeros(shape, jnp.float32)
    if pages <= 8:
        for page in range(pages):
            pick = mark(page, pick)
    else:
        pick = lax.fori_loop(0, pages, mark, pick)
    pick = pick.astype(jnp.bfloat16)
    width_k = arrived.shape[3]
    for t in range(tensors):
        body = arrived[:, t].reshape(groups * groups * part, width_k)
        moved = jnp.dot(pick, body, preferred_element_type=jnp.float32)
        out[:, :, t * width_k : (t + 1) * width_k] = moved.reshape(
            pages * 2, tokens, width_k
        ).astype(jnp.bfloat16)


def per_device(
    queries,
    keys,
    values,
    prefix_keys,
    prefix_values,
    spread,
    turn,
    new_blocks,
    prefix_len,
    owner,
    page_start,
):
    groups = lax.axis_size("group")
    tensors = lax.axis_size("tensor")
    width_q = queries.shape[1]
    width_k = keys.shape[1]
    heads_q = width_q // HEAD
    heads_k = width_k // HEAD
    slots = queries.shape[0] // BLOCK
    capacity = slots // groups
    prompts = new_blocks.shape[1]
    tokens = BLOCK // tensors
    pages = prompts * MAXP
    cosine, sine = (jnp.asarray(table) for table in rope_table())
    params = pltpu.CompilerParams(vmem_limit_bytes=VMEM_LIMIT)
    blocks_q = queries.reshape(slots, BLOCK, width_q)
    blocks_k = keys.reshape(slots, BLOCK, width_k)
    blocks_v = values.reshape(slots, BLOCK, width_k)

    chunk = jax.ShapeDtypeStruct((capacity, BLOCK, width_q + 2 * width_k), jnp.bfloat16)
    sent = pl.pallas_call(
        functools.partial(dispatch_kernel, groups),
        out_shape=[chunk] * groups,
        in_specs=[HBM] * 5,
        out_specs=[VMEM] * groups,
        scratch_shapes=[pltpu.SMEM((groups,), jnp.int32)] * 2
        + [pltpu.VMEM(blocks.shape, jnp.bfloat16) for blocks in (blocks_q, blocks_k, blocks_v)]
        + [pltpu.SemaphoreType.DMA((5,))],
        compiler_params=params,
        cost_estimate=pl.CostEstimate(flops=10**6, bytes_accessed=5 * 10**6, transcendentals=0),
        name="dispatch",
    )(
        *(
            pltpu.with_memory_space_constraint(operand, pltpu.HBM)
            for operand in (spread, turn, blocks_q, blocks_k, blocks_v)
        )
    )
    arrived = [sent[0]] + [
        lax.ppermute(sent[d], "group", [(g, (g + d) % groups) for g in range(groups)])
        for d in range(1, groups)
    ]

    finished, plan = pl.pallas_call(
        functools.partial(pages_kernel, groups, tensors),
        out_shape=[
            jax.ShapeDtypeStruct((groups * tensors, groups * 2 * tokens, width_k), jnp.bfloat16),
            jax.ShapeDtypeStruct((6, max(slots, groups) + 1), jnp.int32),
        ],
        in_specs=[SMEM] * 6 + [VMEM] * 4 + [ANY],
        out_specs=[VMEM, SMEM],
        compiler_params=params,
        scratch_shapes=[
            pltpu.VMEM((2 * slots * BLOCK, width_k), jnp.float32),
            pltpu.SMEM((slots,), jnp.int32),
            pltpu.SMEM((slots,), jnp.int32),
        ],
        cost_estimate=pl.CostEstimate(flops=10**7, bytes_accessed=60 * 10**6, transcendentals=0),
        name="finish_pages",
    )(
        spread, turn, new_blocks, prefix_len, owner, page_start, blocks_k, blocks_v, cosine, sine, sent[0]
    )
    handed = lax.all_to_all(finished, ("group", "tensor"), split_axis=0, concat_axis=0, tiled=True)

    attention = pl.pallas_call(
        functools.partial(attention_kernel, groups, heads_q, heads_k),
        out_shape=jax.ShapeDtypeStruct((slots, BLOCK, width_q), jnp.bfloat16),
        in_specs=[SMEM] + [VMEM] * (4 + groups),
        out_specs=VMEM,
        scratch_shapes=[pltpu.VMEM((slots, BLOCK, width_k), jnp.float32)] * 2,
        compiler_params=params,
        cost_estimate=pl.CostEstimate(flops=10**8, bytes_accessed=200 * 10**6, transcendentals=0),
        name="attention",
    )(plan, prefix_keys, prefix_values, cosine, sine, *arrived)

    cache = pl.pallas_call(
        functools.partial(cache_kernel, groups, tensors),
        out_shape=jax.ShapeDtypeStruct((pages * 2, tokens, tensors * width_k), jnp.bfloat16),
        in_specs=[SMEM, VMEM],
        out_specs=VMEM,
        compiler_params=params,
        cost_estimate=pl.CostEstimate(flops=10**6, bytes_accessed=5 * 10**6, transcendentals=0),
        name="place_pages",
    )(plan, handed.reshape(groups, tensors, groups * 2 * tokens, width_k))
    return (
        attention.reshape(slots * BLOCK, width_q),
        cache.reshape(pages, 2, tokens, tensors * width_k),
    )


def solution(mesh):
    return jax.shard_map(
        per_device,
        mesh=mesh,
        in_specs=(
            P(("parts", "group"), "tensor"),
            P(("parts", "group"), "tensor"),
            P(("parts", "group"), "tensor"),
            P(("parts", "group"), "tensor"),
            P(("parts", "group"), "tensor"),
            P("parts"),
            P("parts"),
            P("parts", None),
            P("parts", None),
            P("parts", None),
            P("parts", None),
        ),
        out_specs=(P(("parts", "group"), "tensor"), P(("parts", "group"), None, "tensor", None)),
        check_vma=False,
    )
```

```python
import functools
import math

import jax
import jax.numpy as jnp
import numpy as np
from jax import lax
from jax.experimental import pallas as pl
from jax.experimental.pallas import tpu as pltpu
from jax.sharding import PartitionSpec as P

HEAD = 128
BLOCK = 8
MAXP = 2
CTXP = 64

VMEM_LIMIT = 24 * 1024 * 1024

SMEM = pl.BlockSpec(memory_space=pltpu.SMEM)
VMEM = pl.BlockSpec(memory_space=pltpu.VMEM)
PROMPT, OFFSET, LIVE, CACHED, SOURCE, COLUMN = range(6)
ANY = pl.BlockSpec(memory_space=pl.ANY)
HBM = pl.BlockSpec(memory_space=pltpu.HBM)


def rope_table():
    count = CTXP + MAXP * BLOCK
    half = HEAD // 2
    frequency = np.exp(np.arange(half) * (-2.0 * math.log(500000.0) / HEAD))
    angles = np.arange(count)[:, None] * frequency[None, :]
    cosine, sine = np.cos(angles), np.sin(angles)
    return (
        np.concatenate([cosine, cosine], axis=1).astype(np.float32),
        np.concatenate([-sine, sine], axis=1).astype(np.float32),
    )


def loop(count, body, unrolled=16):
    if count <= unrolled:
        for index in range(count):
            body(index)
    else:
        lax.fori_loop(0, count, lambda index, carry: (body(index), carry)[1], 0)


def turned(head_block, cosine, sine):
    return head_block * cosine + pltpu.roll(head_block, HEAD // 2, 1) * sine


def dispatch_kernel(groups, tensors, spread_in, turn_in, queries_in, keys_in, values_in, *rest):
    outs, splits, rest = rest[:groups], rest[groups : groups + tensors], rest[groups + tensors :]
    spread, turn, queries, keys, values, sem = rest
    own = lax.axis_index("group")
    own_tensor = lax.axis_index("tensor")
    slots, _, width_q = queries.shape
    width_k = keys.shape[2]
    capacity = slots // groups
    copies = [
        pltpu.make_async_copy(source, target, sem.at[n])
        for n, (source, target) in enumerate(
            (
                (spread_in, spread),
                (turn_in, turn),
                (queries_in, queries),
                (keys_in, keys),
                (values_in, values),
            )
        )
    ]
    for copy in copies:
        copy.start()
    for copy in copies[:2]:
        copy.wait()
    sources = []
    for distance in range(groups):
        first_slot = column_of(spread, groups, distance) + turn[own]
        sources.append([lax.rem(first_slot + groups * step, slots) for step in range(capacity)])
    tokens = BLOCK // tensors
    rows = 2 * slots * BLOCK
    row = lax.broadcasted_iota(jnp.int32, (rows, rows), 0)
    col = lax.broadcasted_iota(jnp.int32, (rows, rows), 1)
    share = lax.rem(row // (2 * slots * tokens) + own_tensor, tensors)
    wanted = (row // tokens) % (2 * slots) * BLOCK + share * tokens + row % tokens
    pick = (col == wanted).astype(jnp.float32).astype(jnp.bfloat16)
    for copy in copies[3:]:
        copy.wait()
    body = jnp.concatenate(
        [
            ref[...].astype(jnp.float32).reshape(slots * BLOCK, width_k)
            for ref in (keys, values)
        ],
        axis=0,
    ).astype(jnp.bfloat16)
    moved = jnp.dot(pick, body, preferred_element_type=jnp.float32).astype(jnp.bfloat16)
    for distance in range(tensors):
        size = 2 * slots * tokens
        splits[distance][...] = moved[distance * size : (distance + 1) * size]
    copies[2].wait()
    for distance in range(groups):
        for step in range(capacity):
            source = sources[distance][step]
            out = outs[distance]
            out[step, :, :width_q] = queries[source]
            out[step, :, width_q : width_q + width_k] = keys[source]
            out[step, :, width_q + width_k :] = values[source]


def column_of(spread, groups, distance):
    wanted = (groups - distance) % groups
    if groups <= 8:
        return sum(jnp.where(spread[c] == wanted, c, 0) for c in range(groups))
    return lax.fori_loop(
        0, groups, lambda c, found: jnp.where(spread[c] == wanted, c, found), jnp.int32(0)
    )


def make_plan(groups, own, spread, new_blocks, prefix_len, owner, page_start, plan):
    prompts = new_blocks.shape[1]
    slots = prompts * MAXP

    def clear(j):
        plan[PROMPT, j] = 0
        plan[OFFSET, j] = 0
        plan[LIVE, j] = 0
        plan[CACHED, j] = 0

    loop(slots, clear)

    def one(p, start):
        blocks = new_blocks[own, p]
        cached = prefix_len[own, p]
        for step in range(MAXP):
            at = jnp.where(step < blocks, start + step, slots)
            plan[PROMPT, at] = p
            plan[OFFSET, at] = cached + step * BLOCK
            plan[LIVE, at] = 1 + step
            plan[CACHED, at] = cached
        return start + blocks

    start = jnp.int32(0)
    if prompts <= 8:
        for p in range(prompts):
            start = one(p, start)
    else:
        lax.fori_loop(0, prompts, one, start)

    def of_group(g):
        def one(p, start):
            blocks = new_blocks[g, p]
            mine = owner[g, p] == own
            for step in range(MAXP):
                root = lax.rem(g + spread[lax.rem(start + step, groups)], groups)
                at = jnp.where(mine, page_start[g, p] + step, slots)
                away = lax.rem(own - root + groups, groups)
                plan[SOURCE, at] = jnp.where(step < blocks, away * groups + g, -1)
            return start + blocks

        start = jnp.int32(0)
        if prompts <= 8:
            for p in range(prompts):
                start = one(p, start)
        else:
            lax.fori_loop(0, prompts, one, start)

    loop(groups, of_group)
    for distance in range(groups):
        plan[COLUMN, distance] = column_of(spread, groups, distance)


def pages_kernel(
    groups, tensors, spread, turn, new_blocks, prefix_len, owner, page_start, cosine, sine, *rest
):
    halves, rest = rest[:tensors], rest[tensors:]
    outs, (plan, cos, sin, dest_code) = rest[:groups], rest[groups:]
    own = lax.axis_index("group")
    own_tensor = lax.axis_index("tensor")
    slots = dest_code.shape[0]
    width_k = halves[0].shape[1]
    capacity = slots // groups
    prompts = new_blocks.shape[1]
    tokens = BLOCK // tensors

    def column(c):
        target = lax.rem(own - spread[c] + groups, groups)
        for step in range(capacity):
            j = c + groups * step
            source = lax.rem(j + turn[own], slots)

            def find(p, carry):
                start, place, holder = carry
                blocks = new_blocks[target, p]
                inside = (j >= start) & (j < start + blocks)
                place = jnp.where(inside, prefix_len[target, p] + (j - start) * BLOCK, place)
                holder = jnp.where(inside, owner[target, p], holder)
                return start + blocks, place, holder

            carry = (jnp.int32(0), jnp.int32(0), jnp.int32(-1))
            if prompts <= 8:
                for p in range(prompts):
                    carry = find(p, carry)
            else:
                carry = lax.fori_loop(0, prompts, find, carry)
            _, place, holder = carry
            away = lax.rem(holder - own + groups, groups)
            code = (away * groups + target) * slots + source
            dest_code[source] = jnp.where(holder >= 0, code, -2)
            first = place + own_tensor * tokens
            cos[pl.ds(source * tokens, tokens), :] = cosine[pl.ds(first, tokens), :]
            sin[pl.ds(source * tokens, tokens), :] = sine[pl.ds(first, tokens), :]

    loop(groups, column)
    part = 2 * tokens
    shape = (groups * groups * part, 2 * slots * tokens)
    row = lax.broadcasted_iota(jnp.int32, shape, 0)
    col = lax.broadcasted_iota(jnp.int32, shape, 1)
    same = ((row // tokens) % 2 == col // (slots * tokens)) & (row % tokens == col % tokens)
    code = jnp.where(same, (row // part) * slots + (col // tokens) % slots, -1)

    def mark(b, total):
        return jnp.where(code == dest_code[b], 1.0, total)

    pick = jnp.zeros(shape, jnp.float32)
    if slots <= 8:
        for b in range(slots):
            pick = mark(b, pick)
    else:
        pick = lax.fori_loop(0, slots, mark, pick)
    pick = pick.astype(jnp.bfloat16)
    half = slots * tokens
    for distance in range(tensors):
        ref = halves[distance]
        block = ref[:half].astype(jnp.float32)
        block = jnp.concatenate(
            [
                turned(block[:, first : first + HEAD], cos[...], sin[...])
                for first in range(0, width_k, HEAD)
            ],
            axis=1,
        )
        block = jnp.concatenate([block.astype(jnp.bfloat16), ref[half:]], axis=0)
        moved = jnp.dot(pick, block, preferred_element_type=jnp.float32).astype(jnp.bfloat16)
        sender = lax.rem(own_tensor - distance + tensors, tensors)
        at = pl.ds(pl.multiple_of(sender * width_k, HEAD), width_k)
        for d in range(groups):
            size = groups * part
            outs[d][:, at] = moved[d * size : (d + 1) * size]
    make_plan(groups, own, spread, new_blocks, prefix_len, owner, page_start, plan)


def attention_kernel(groups, heads_q, heads_k, plan, prefix_keys, prefix_values, cosine, sine, *rest):
    arrived, (out, new_keys, new_values) = rest[:groups], rest[groups:]
    slots = out.shape[0]
    capacity = slots // groups
    ratio = heads_q // heads_k
    width_q = heads_q * HEAD
    width_k = heads_k * HEAD
    scale = math.log2(math.e) / math.sqrt(HEAD)
    span = CTXP + 2 * BLOCK
    lane = lax.broadcasted_iota(jnp.int32, (BLOCK, span), 1)
    token = lax.broadcasted_iota(jnp.int32, (BLOCK, span), 0)
    fresh = (lane >= CTXP + BLOCK) & (lane - (CTXP + BLOCK) <= token)
    before = (lane >= CTXP) & (lane < CTXP + BLOCK)

    blocks = []
    for distance in range(groups):
        first_slot = plan[COLUMN, distance]
        for step in range(capacity):
            j = first_slot + groups * step
            here = arrived[distance].at[step]
            cos = cosine[pl.ds(plan[OFFSET, j], BLOCK), :]
            sin = sine[pl.ds(plan[OFFSET, j], BLOCK), :]
            new_keys[j] = jnp.concatenate(
                [
                    turned(here[:, first : first + HEAD].astype(jnp.float32), cos, sin)
                    for first in range(width_q, width_q + width_k, HEAD)
                ],
                axis=1,
            )
            new_values[j] = here[:, width_q + width_k :].astype(jnp.float32)
            blocks.append((j, here, cos, sin))

    for at in range(0, len(blocks), 8):
        some = blocks[at : at + 8]
        for h in range(heads_k):
            part = slice(h * HEAD, (h + 1) * HEAD)
            scores = []
            for j, here, cos, sin in some:
                prev = jnp.maximum(j - 1, 0)
                region = pl.ds(pl.multiple_of(plan[PROMPT, j] * CTXP, CTXP), CTXP)
                mask = fresh | (lane < plan[CACHED, j]) & (lane < CTXP) | before & (plan[LIVE, j] == 2)
                new_key = jnp.concatenate([new_keys[prev, :, part], new_keys[j, :, part]], axis=0)
                key = jnp.concatenate([prefix_keys[region, part], new_key.astype(jnp.bfloat16)], axis=0)
                query = jnp.concatenate(
                    [
                        turned(here[:, n * HEAD : (n + 1) * HEAD].astype(jnp.float32), cos, sin)
                        for n in range(h * ratio, (h + 1) * ratio)
                    ],
                    axis=0,
                ).astype(jnp.bfloat16)
                score = lax.dot_general(
                    query, key, (((1,), (1,)), ((), ())), preferred_element_type=jnp.float32
                )
                scores.append(jnp.where(mask[None], score.reshape(ratio, BLOCK, span), -1e30))
            score = jnp.concatenate(scores, axis=0)
            top = jnp.max(score, axis=2, keepdims=True)
            powers = jnp.exp2((score - top) * scale)
            weights = powers * (1.0 / jnp.sum(powers, axis=2, keepdims=True))
            weights = weights.reshape(len(some), ratio * BLOCK, span).astype(jnp.bfloat16)
            for place, (j, here, cos, sin) in enumerate(some):
                prev = jnp.maximum(j - 1, 0)
                region = pl.ds(pl.multiple_of(plan[PROMPT, j] * CTXP, CTXP), CTXP)
                new_value = jnp.concatenate([new_values[prev, :, part], new_values[j, :, part]], axis=0)
                value = jnp.concatenate([prefix_values[region, part], new_value.astype(jnp.bfloat16)], axis=0)
                mixed = jnp.dot(weights[place], value, preferred_element_type=jnp.float32)
                mixed = jnp.where(plan[LIVE, j] > 0, mixed, 0.0)
                for n in range(ratio):
                    first = (h * ratio + n) * HEAD
                    out[j, :, first : first + HEAD] = mixed[n * BLOCK : (n + 1) * BLOCK].astype(
                        jnp.bfloat16
                    )


def cache_kernel(groups, tensors, plan, *rest):
    arrived, out = rest[:groups], rest[groups]
    tokens = BLOCK // tensors
    part = 2 * tokens
    pages = out.shape[0] // 2
    shape = (pages * part, groups * groups * part)
    row = lax.broadcasted_iota(jnp.int32, shape, 0)
    col = lax.broadcasted_iota(jnp.int32, shape, 1)
    limit = groups * groups
    code = jnp.where(row % part == col % part, (row // part) * limit + col // part, -1)

    def mark(page, total):
        wanted = jnp.where(plan[SOURCE, page] >= 0, page * limit + plan[SOURCE, page], -2)
        return jnp.where(code == wanted, 1.0, total)

    pick = jnp.zeros(shape, jnp.float32)
    if pages <= 8:
        for page in range(pages):
            pick = mark(page, pick)
    else:
        pick = lax.fori_loop(0, pages, mark, pick)
    pick = pick.astype(jnp.bfloat16)
    body = jnp.concatenate([ref[...] for ref in arrived], axis=0)
    moved = jnp.dot(pick, body, preferred_element_type=jnp.float32)
    out[...] = moved.reshape(pages * 2, tokens, out.shape[2]).astype(jnp.bfloat16)


def shifted(chunks, axis):
    size = lax.axis_size(axis)
    return [chunks[0]] + [
        lax.ppermute(chunks[d], axis, [(i, (i + d) % size) for i in range(size)])
        for d in range(1, size)
    ]


def per_device(
    queries,
    keys,
    values,
    prefix_keys,
    prefix_values,
    spread,
    turn,
    new_blocks,
    prefix_len,
    owner,
    page_start,
):
    groups = lax.axis_size("group")
    tensors = lax.axis_size("tensor")
    width_q = queries.shape[1]
    width_k = keys.shape[1]
    heads_q = width_q // HEAD
    heads_k = width_k // HEAD
    slots = queries.shape[0] // BLOCK
    capacity = slots // groups
    prompts = new_blocks.shape[1]
    tokens = BLOCK // tensors
    pages = prompts * MAXP
    cosine, sine = (jnp.asarray(table) for table in rope_table())
    params = pltpu.CompilerParams(vmem_limit_bytes=VMEM_LIMIT)
    blocks_q = queries.reshape(slots, BLOCK, width_q)
    blocks_k = keys.reshape(slots, BLOCK, width_k)
    blocks_v = values.reshape(slots, BLOCK, width_k)

    chunk = jax.ShapeDtypeStruct((capacity, BLOCK, width_q + 2 * width_k), jnp.bfloat16)
    split = jax.ShapeDtypeStruct((2 * slots * tokens, width_k), jnp.bfloat16)
    sent = pl.pallas_call(
        functools.partial(dispatch_kernel, groups, tensors),
        out_shape=[chunk] * groups + [split] * tensors,
        in_specs=[HBM] * 5,
        out_specs=[VMEM] * (groups + tensors),
        scratch_shapes=[pltpu.SMEM((groups,), jnp.int32)] * 2
        + [pltpu.VMEM(blocks.shape, jnp.bfloat16) for blocks in (blocks_q, blocks_k, blocks_v)]
        + [pltpu.SemaphoreType.DMA((5,))],
        compiler_params=params,
        name="dispatch",
    )(
        *(
            pltpu.with_memory_space_constraint(operand, pltpu.HBM)
            for operand in (spread, turn, blocks_q, blocks_k, blocks_v)
        )
    )
    arrived = shifted(sent[:groups], "group")
    halves = shifted(sent[groups:], "tensor")

    pages_out = jax.ShapeDtypeStruct((groups * 2 * tokens, tensors * width_k), jnp.bfloat16)
    *finished, plan = pl.pallas_call(
        functools.partial(pages_kernel, groups, tensors),
        out_shape=[pages_out] * groups
        + [jax.ShapeDtypeStruct((6, max(slots, groups) + 1), jnp.int32)],
        in_specs=[SMEM] * 6 + [VMEM] * (2 + tensors),
        out_specs=[VMEM] * groups + [SMEM],
        compiler_params=params,
        scratch_shapes=[pltpu.VMEM((slots * tokens, HEAD), jnp.float32)] * 2
        + [pltpu.SMEM((slots,), jnp.int32)],
        name="finish_pages",
    )(spread, turn, new_blocks, prefix_len, owner, page_start, cosine, sine, *halves)
    handed = shifted(finished, "group")

    attention = pl.pallas_call(
        functools.partial(attention_kernel, groups, heads_q, heads_k),
        out_shape=jax.ShapeDtypeStruct((slots, BLOCK, width_q), jnp.bfloat16),
        in_specs=[SMEM] + [VMEM] * (4 + groups),
        out_specs=VMEM,
        scratch_shapes=[pltpu.VMEM((slots, BLOCK, width_k), jnp.float32)] * 2,
        compiler_params=params,
        name="attention",
    )(plan, prefix_keys, prefix_values, cosine, sine, *arrived)

    cache = pl.pallas_call(
        functools.partial(cache_kernel, groups, tensors),
        out_shape=jax.ShapeDtypeStruct((pages * 2, tokens, tensors * width_k), jnp.bfloat16),
        in_specs=[SMEM] + [VMEM] * groups,
        out_specs=VMEM,
        compiler_params=params,
        name="place_pages",
    )(plan, *handed)
    return (
        attention.reshape(slots * BLOCK, width_q),
        cache.reshape(pages, 2, tokens, tensors * width_k),
    )


def solution(mesh):
    return jax.shard_map(
        per_device,
        mesh=mesh,
        in_specs=(
            P(("parts", "group"), "tensor"),
            P(("parts", "group"), "tensor"),
            P(("parts", "group"), "tensor"),
            P(("parts", "group"), "tensor"),
            P(("parts", "group"), "tensor"),
            P("parts"),
            P("parts"),
            P("parts", None),
            P("parts", None),
            P("parts", None),
            P("parts", None),
        ),
        out_specs=(P(("parts", "group"), "tensor"), P(("parts", "group"), None, "tensor", None)),
        check_vma=False,
    )
```

```python
import functools
import math

import jax
import jax.numpy as jnp
import numpy as np
from jax import lax
from jax.experimental import pallas as pl
from jax.experimental.pallas import tpu as pltpu
from jax.sharding import PartitionSpec as P

HEAD = 128
BLOCK = 8
MAXP = 2
CTXP = 64

VMEM_LIMIT = 24 * 1024 * 1024

SMEM = pl.BlockSpec(memory_space=pltpu.SMEM)
VMEM = pl.BlockSpec(memory_space=pltpu.VMEM)
PROMPT, OFFSET, LIVE, CACHED, SOURCE, COLUMN, TAKEN, PLACE = range(8)
GATHER_BYTES = 8 * 1024 * 1024
ANY = pl.BlockSpec(memory_space=pl.ANY)
HBM = pl.BlockSpec(memory_space=pltpu.HBM)


def rope_table():
    count = CTXP + MAXP * BLOCK
    half = HEAD // 2
    frequency = np.exp(np.arange(half) * (-2.0 * math.log(500000.0) / HEAD))
    angles = np.arange(count)[:, None] * frequency[None, :]
    cosine, sine = np.cos(angles), np.sin(angles)
    return (
        np.concatenate([cosine, cosine], axis=1).astype(np.float32),
        np.concatenate([-sine, sine], axis=1).astype(np.float32),
    )


def loop(count, body, unrolled=16):
    if count <= unrolled:
        for index in range(count):
            body(index)
    else:
        lax.fori_loop(0, count, lambda index, carry: (body(index), carry)[1], 0)


def turned(head_block, cosine, sine):
    return head_block * cosine + pltpu.roll(head_block, HEAD // 2, 1) * sine


def plan_kernel(groups, spread, turn, new_blocks, prefix_len, owner, page_start, _, plan):
    own = lax.axis_index("group")
    make_plan(groups, own, spread, turn, new_blocks, prefix_len, owner, page_start, plan)


def dispatch_kernel(groups, tensors, spread_in, turn_in, queries_in, keys_in, values_in, *rest):
    outs, splits, rest = rest[:groups], rest[groups : groups + tensors], rest[groups + tensors :]
    spread, turn, queries, keys, values, sem = rest
    own = lax.axis_index("group")
    slots, _, width_q = queries.shape
    width_k = keys.shape[2]
    capacity = slots // groups
    copies = [
        pltpu.make_async_copy(source, target, sem.at[n])
        for n, (source, target) in enumerate(
            (
                (spread_in, spread),
                (turn_in, turn),
                (queries_in, queries),
                (keys_in, keys),
                (values_in, values),
            )
        )
    ]
    for copy in copies:
        copy.start()
    for copy in copies[:2]:
        copy.wait()
    sources = []
    for distance in range(groups):
        first_slot = column_of(spread, groups, distance) + turn[own]
        sources.append([lax.rem(first_slot + groups * step, slots) for step in range(capacity)])
    if tensors:
        tokens = BLOCK // tensors
        rows = 2 * slots * BLOCK
        row = lax.broadcasted_iota(jnp.int32, (rows, rows), 0)
        col = lax.broadcasted_iota(jnp.int32, (rows, rows), 1)
        share = lax.rem(row // (2 * slots * tokens) + lax.axis_index("tensor"), tensors)
        wanted = (row // tokens) % (2 * slots) * BLOCK + share * tokens + row % tokens
        pick = (col == wanted).astype(jnp.float32).astype(jnp.bfloat16)
        for copy in copies[3:]:
            copy.wait()
        body = jnp.concatenate(
            [
                ref[...].astype(jnp.float32).reshape(slots * BLOCK, width_k)
                for ref in (keys, values)
            ],
            axis=0,
        ).astype(jnp.bfloat16)
        moved = jnp.dot(pick, body, preferred_element_type=jnp.float32).astype(jnp.bfloat16)
        for distance in range(tensors):
            size = 2 * slots * tokens
            splits[distance][...] = moved[distance * size : (distance + 1) * size]
    else:
        for copy in copies[3:]:
            copy.wait()
    copies[2].wait()
    for distance in range(groups):
        for step in range(capacity):
            source = sources[distance][step]
            out = outs[distance]
            out[step, :, :width_q] = queries[source]
            out[step, :, width_q : width_q + width_k] = keys[source]
            out[step, :, width_q + width_k :] = values[source]


def column_of(spread, groups, distance):
    wanted = (groups - distance) % groups
    if groups <= 8:
        return sum(jnp.where(spread[c] == wanted, c, 0) for c in range(groups))
    return lax.fori_loop(
        0, groups, lambda c, found: jnp.where(spread[c] == wanted, c, found), jnp.int32(0)
    )


def make_plan(groups, own, spread, turn, new_blocks, prefix_len, owner, page_start, plan):
    prompts = new_blocks.shape[1]
    slots = prompts * MAXP

    def clear(j):
        plan[PROMPT, j] = 0
        plan[OFFSET, j] = 0
        plan[LIVE, j] = 0
        plan[CACHED, j] = 0

    loop(slots, clear)

    def one(p, start):
        blocks = new_blocks[own, p]
        cached = prefix_len[own, p]
        for step in range(MAXP):
            at = jnp.where(step < blocks, start + step, slots)
            plan[PROMPT, at] = p
            plan[OFFSET, at] = cached + step * BLOCK
            plan[LIVE, at] = 1 + step
            plan[CACHED, at] = cached
        return start + blocks

    start = jnp.int32(0)
    if prompts <= 8:
        for p in range(prompts):
            start = one(p, start)
    else:
        lax.fori_loop(0, prompts, one, start)

    def of_group(g):
        def one(p, start):
            blocks = new_blocks[g, p]
            mine = owner[g, p] == own
            for step in range(MAXP):
                root = lax.rem(g + spread[lax.rem(start + step, groups)], groups)
                at = jnp.where(mine, page_start[g, p] + step, slots)
                away = lax.rem(own - root + groups, groups)
                plan[SOURCE, at] = jnp.where(step < blocks, away * groups + g, -1)
                plan[TAKEN, at] = root * slots + lax.rem(start + step + turn[root], slots)
                plan[PLACE, at] = prefix_len[g, p] + step * BLOCK
            return start + blocks

        start = jnp.int32(0)
        if prompts <= 8:
            for p in range(prompts):
                start = one(p, start)
        else:
            lax.fori_loop(0, prompts, one, start)

    loop(groups, of_group)
    for distance in range(groups):
        plan[COLUMN, distance] = column_of(spread, groups, distance)


def pages_kernel(
    groups, tensors, spread, turn, new_blocks, prefix_len, owner, page_start, cosine, sine, *rest
):
    halves, rest = rest[:tensors], rest[tensors:]
    outs, (plan, cos, sin, dest_code) = rest[:groups], rest[groups:]
    own = lax.axis_index("group")
    own_tensor = lax.axis_index("tensor")
    slots = dest_code.shape[0]
    width_k = halves[0].shape[1]
    capacity = slots // groups
    prompts = new_blocks.shape[1]
    tokens = BLOCK // tensors

    def column(c):
        target = lax.rem(own - spread[c] + groups, groups)
        for step in range(capacity):
            j = c + groups * step
            source = lax.rem(j + turn[own], slots)

            def find(p, carry):
                start, place, holder = carry
                blocks = new_blocks[target, p]
                inside = (j >= start) & (j < start + blocks)
                place = jnp.where(inside, prefix_len[target, p] + (j - start) * BLOCK, place)
                holder = jnp.where(inside, owner[target, p], holder)
                return start + blocks, place, holder

            carry = (jnp.int32(0), jnp.int32(0), jnp.int32(-1))
            if prompts <= 8:
                for p in range(prompts):
                    carry = find(p, carry)
            else:
                carry = lax.fori_loop(0, prompts, find, carry)
            _, place, holder = carry
            away = lax.rem(holder - own + groups, groups)
            code = (away * groups + target) * slots + source
            dest_code[source] = jnp.where(holder >= 0, code, -2)
            first = place + own_tensor * tokens
            cos[pl.ds(source * tokens, tokens), :] = cosine[pl.ds(first, tokens), :]
            sin[pl.ds(source * tokens, tokens), :] = sine[pl.ds(first, tokens), :]

    loop(groups, column)
    part = 2 * tokens
    shape = (groups * groups * part, 2 * slots * tokens)
    row = lax.broadcasted_iota(jnp.int32, shape, 0)
    col = lax.broadcasted_iota(jnp.int32, shape, 1)
    same = ((row // tokens) % 2 == col // (slots * tokens)) & (row % tokens == col % tokens)
    code = jnp.where(same, (row // part) * slots + (col // tokens) % slots, -1)

    def mark(b, total):
        return jnp.where(code == dest_code[b], 1.0, total)

    pick = jnp.zeros(shape, jnp.float32)
    if slots <= 8:
        for b in range(slots):
            pick = mark(b, pick)
    else:
        pick = lax.fori_loop(0, slots, mark, pick)
    pick = pick.astype(jnp.bfloat16)
    half = slots * tokens
    for distance in range(tensors):
        ref = halves[distance]
        block = ref[:half].astype(jnp.float32)
        block = jnp.concatenate(
            [
                turned(block[:, first : first + HEAD], cos[...], sin[...])
                for first in range(0, width_k, HEAD)
            ],
            axis=1,
        )
        block = jnp.concatenate([block.astype(jnp.bfloat16), ref[half:]], axis=0)
        moved = jnp.dot(pick, block, preferred_element_type=jnp.float32).astype(jnp.bfloat16)
        sender = lax.rem(own_tensor - distance + tensors, tensors)
        at = pl.ds(pl.multiple_of(sender * width_k, HEAD), width_k)
        for d in range(groups):
            size = groups * part
            outs[d][:, at] = moved[d * size : (d + 1) * size]
    make_plan(groups, own, spread, turn, new_blocks, prefix_len, owner, page_start, plan)


def attention_kernel(groups, heads_q, heads_k, plan, prefix_keys, prefix_values, cosine, sine, *rest):
    arrived, (out, new_keys, new_values) = rest[:groups], rest[groups:]
    slots = out.shape[0]
    capacity = slots // groups
    ratio = heads_q // heads_k
    width_q = heads_q * HEAD
    width_k = heads_k * HEAD
    scale = math.log2(math.e) / math.sqrt(HEAD)
    span = CTXP + 2 * BLOCK
    lane = lax.broadcasted_iota(jnp.int32, (BLOCK, span), 1)
    token = lax.broadcasted_iota(jnp.int32, (BLOCK, span), 0)
    fresh = (lane >= CTXP + BLOCK) & (lane - (CTXP + BLOCK) <= token)
    before = (lane >= CTXP) & (lane < CTXP + BLOCK)

    blocks = []
    for distance in range(groups):
        first_slot = plan[COLUMN, distance]
        for step in range(capacity):
            j = first_slot + groups * step
            here = arrived[distance].at[step]
            cos = cosine[pl.ds(plan[OFFSET, j], BLOCK), :]
            sin = sine[pl.ds(plan[OFFSET, j], BLOCK), :]
            new_keys[j] = jnp.concatenate(
                [
                    turned(here[:, first : first + HEAD].astype(jnp.float32), cos, sin)
                    for first in range(width_q, width_q + width_k, HEAD)
                ],
                axis=1,
            )
            new_values[j] = here[:, width_q + width_k :].astype(jnp.float32)
            blocks.append((j, here, cos, sin))

    for at in range(0, len(blocks), 8):
        some = blocks[at : at + 8]
        for h in range(heads_k):
            part = slice(h * HEAD, (h + 1) * HEAD)
            scores = []
            for j, here, cos, sin in some:
                prev = jnp.maximum(j - 1, 0)
                region = pl.ds(pl.multiple_of(plan[PROMPT, j] * CTXP, CTXP), CTXP)
                mask = fresh | (lane < plan[CACHED, j]) & (lane < CTXP) | before & (plan[LIVE, j] == 2)
                new_key = jnp.concatenate([new_keys[prev, :, part], new_keys[j, :, part]], axis=0)
                key = jnp.concatenate([prefix_keys[region, part], new_key.astype(jnp.bfloat16)], axis=0)
                query = jnp.concatenate(
                    [
                        turned(here[:, n * HEAD : (n + 1) * HEAD].astype(jnp.float32), cos, sin)
                        for n in range(h * ratio, (h + 1) * ratio)
                    ],
                    axis=0,
                ).astype(jnp.bfloat16)
                score = lax.dot_general(
                    query, key, (((1,), (1,)), ((), ())), preferred_element_type=jnp.float32
                )
                scores.append(jnp.where(mask[None], score.reshape(ratio, BLOCK, span), -1e30))
            score = jnp.concatenate(scores, axis=0)
            top = jnp.max(score, axis=2, keepdims=True)
            powers = jnp.exp2((score - top) * scale)
            weights = powers * (1.0 / jnp.sum(powers, axis=2, keepdims=True))
            weights = weights.reshape(len(some), ratio * BLOCK, span).astype(jnp.bfloat16)
            for place, (j, here, cos, sin) in enumerate(some):
                prev = jnp.maximum(j - 1, 0)
                region = pl.ds(pl.multiple_of(plan[PROMPT, j] * CTXP, CTXP), CTXP)
                new_value = jnp.concatenate([new_values[prev, :, part], new_values[j, :, part]], axis=0)
                value = jnp.concatenate([prefix_values[region, part], new_value.astype(jnp.bfloat16)], axis=0)
                mixed = jnp.dot(weights[place], value, preferred_element_type=jnp.float32)
                mixed = jnp.where(plan[LIVE, j] > 0, mixed, 0.0)
                for n in range(ratio):
                    first = (h * ratio + n) * HEAD
                    out[j, :, first : first + HEAD] = mixed[n * BLOCK : (n + 1) * BLOCK].astype(
                        jnp.bfloat16
                    )


def cache_kernel(groups, tensors, plan, *rest):
    arrived, out = rest[:groups], rest[groups]
    tokens = BLOCK // tensors
    part = 2 * tokens
    pages = out.shape[0] // 2
    shape = (pages * part, groups * groups * part)
    row = lax.broadcasted_iota(jnp.int32, shape, 0)
    col = lax.broadcasted_iota(jnp.int32, shape, 1)
    limit = groups * groups
    code = jnp.where(row % part == col % part, (row // part) * limit + col // part, -1)

    def mark(page, total):
        wanted = jnp.where(plan[SOURCE, page] >= 0, page * limit + plan[SOURCE, page], -2)
        return jnp.where(code == wanted, 1.0, total)

    pick = jnp.zeros(shape, jnp.float32)
    if pages <= 8:
        for page in range(pages):
            pick = mark(page, pick)
    else:
        pick = lax.fori_loop(0, pages, mark, pick)
    pick = pick.astype(jnp.bfloat16)
    body = jnp.concatenate([ref[...] for ref in arrived], axis=0)
    moved = jnp.dot(pick, body, preferred_element_type=jnp.float32)
    out[...] = moved.reshape(pages * 2, tokens, out.shape[2]).astype(jnp.bfloat16)


def gathered_cache_kernel(groups, tensors, plan, keys, values, cosine, sine, _, out):
    own_tensor = lax.axis_index("tensor")
    pages = out.shape[0] // 2
    tokens = BLOCK // tensors
    slots = keys.shape[0] // (groups * tensors)
    width_k = keys.shape[2]
    rows = [[], []]
    for page in range(pages):
        taken = plan[TAKEN, page]
        source = (taken // slots) * (tensors * slots) + lax.rem(taken, slots)
        live = plan[SOURCE, page] >= 0
        cos = cosine[pl.ds(plan[PLACE, page], BLOCK), :]
        sin = sine[pl.ds(plan[PLACE, page], BLOCK), :]
        parts = [[], []]
        for t in range(tensors):
            key = keys[source + t * slots].astype(jnp.float32)
            for first in range(0, width_k, HEAD):
                parts[0].append(turned(key[:, first : first + HEAD], cos, sin))
            parts[1].append(values[source + t * slots].astype(jnp.float32))
        for kind in range(2):
            rows[kind].append(jnp.where(live, jnp.concatenate(parts[kind], axis=1), 0.0))
    body = jnp.concatenate(rows[0] + rows[1], axis=0).astype(jnp.bfloat16)
    shape = (pages * 2 * tokens, 2 * pages * BLOCK)
    row = lax.broadcasted_iota(jnp.int32, shape, 0)
    col = lax.broadcasted_iota(jnp.int32, shape, 1)
    kind = (row // tokens) % 2
    wanted = (kind * pages + row // (2 * tokens)) * BLOCK + own_tensor * tokens + row % tokens
    pick = (col == wanted).astype(jnp.float32).astype(jnp.bfloat16)
    moved = jnp.dot(pick, body, preferred_element_type=jnp.float32)
    out[...] = moved.reshape(pages * 2, tokens, tensors * width_k).astype(jnp.bfloat16)


def in_hbm(operand):
    return pltpu.with_memory_space_constraint(operand, pltpu.HBM)


def shifted(chunks, axis):
    size = lax.axis_size(axis)
    return [chunks[0]] + [
        lax.ppermute(chunks[d], axis, [(i, (i + d) % size) for i in range(size)])
        for d in range(1, size)
    ]


def per_device(
    queries,
    keys,
    values,
    prefix_keys,
    prefix_values,
    spread,
    turn,
    new_blocks,
    prefix_len,
    owner,
    page_start,
):
    groups = lax.axis_size("group")
    tensors = lax.axis_size("tensor")
    width_q = queries.shape[1]
    width_k = keys.shape[1]
    heads_q = width_q // HEAD
    heads_k = width_k // HEAD
    slots = queries.shape[0] // BLOCK
    capacity = slots // groups
    prompts = new_blocks.shape[1]
    tokens = BLOCK // tensors
    pages = prompts * MAXP
    cosine, sine = (jnp.asarray(table) for table in rope_table())
    params = pltpu.CompilerParams(vmem_limit_bytes=VMEM_LIMIT)
    blocks_q = queries.reshape(slots, BLOCK, width_q)
    blocks_k = keys.reshape(slots, BLOCK, width_k)
    blocks_v = values.reshape(slots, BLOCK, width_k)

    chunk = jax.ShapeDtypeStruct((capacity, BLOCK, width_q + 2 * width_k), jnp.bfloat16)
    gather = 4 * groups * tensors * keys.size <= GATHER_BYTES
    splits = 0 if gather else tensors
    split = jax.ShapeDtypeStruct((2 * slots * tokens, width_k), jnp.bfloat16)
    sent = pl.pallas_call(
        functools.partial(dispatch_kernel, groups, splits),
        out_shape=[chunk] * groups + [split] * splits,
        in_specs=[HBM] * 5,
        out_specs=[VMEM] * (groups + splits),
        scratch_shapes=[pltpu.SMEM((groups,), jnp.int32)] * 2
        + [pltpu.VMEM(blocks.shape, jnp.bfloat16) for blocks in (blocks_q, blocks_k, blocks_v)]
        + [pltpu.SemaphoreType.DMA((5,))],
        compiler_params=params,
        name="dispatch",
    )(
        *(in_hbm(operand) for operand in (spread, turn, blocks_q, blocks_k, blocks_v))
    )
    arrived = shifted(sent[:groups], "group")
    plan_shape = jax.ShapeDtypeStruct((8, max(slots, groups) + 1), jnp.int32)
    integers = (spread, turn, new_blocks, prefix_len, owner, page_start)
    if gather:
        every_k, every_v = (
            lax.all_gather(rows, ("group", "tensor"), axis=0, tiled=True).reshape(-1, BLOCK, width_k)
            for rows in (keys, values)
        )
        plan = pl.pallas_call(
            functools.partial(plan_kernel, groups),
            out_shape=plan_shape,
            in_specs=[SMEM] * 6 + [ANY],
            out_specs=SMEM,
            compiler_params=params,
            name="plan",
        )(*integers, sent[0])
    else:
        halves = shifted(sent[groups:], "tensor")

        pages_out = jax.ShapeDtypeStruct((groups * 2 * tokens, tensors * width_k), jnp.bfloat16)
        *finished, plan = pl.pallas_call(
            functools.partial(pages_kernel, groups, tensors),
            out_shape=[pages_out] * groups
            + [plan_shape],
            in_specs=[SMEM] * 6 + [VMEM] * (2 + tensors),
            out_specs=[VMEM] * groups + [SMEM],
            compiler_params=params,
            scratch_shapes=[pltpu.VMEM((slots * tokens, HEAD), jnp.float32)] * 2
            + [pltpu.SMEM((slots,), jnp.int32)],
            name="finish_pages",
        )(*integers, cosine, sine, *halves)
        handed = shifted(finished, "group")

    attention = pl.pallas_call(
        functools.partial(attention_kernel, groups, heads_q, heads_k),
        out_shape=jax.ShapeDtypeStruct((slots, BLOCK, width_q), jnp.bfloat16),
        in_specs=[SMEM] + [VMEM] * (4 + groups),
        out_specs=VMEM,
        scratch_shapes=[pltpu.VMEM((slots, BLOCK, width_k), jnp.float32)] * 2,
        compiler_params=params,
        name="attention",
    )(plan, prefix_keys, prefix_values, cosine, sine, *arrived)

    cache_shape = jax.ShapeDtypeStruct((pages * 2, tokens, tensors * width_k), jnp.bfloat16)
    if gather:
        cache = pl.pallas_call(
            functools.partial(gathered_cache_kernel, groups, tensors),
            out_shape=cache_shape,
            in_specs=[SMEM] + [VMEM] * 4 + [ANY],
            out_specs=VMEM,
            compiler_params=params,
            name="place_pages",
        )(plan, in_hbm(every_k), in_hbm(every_v), cosine, sine, in_hbm(attention))
    else:
        cache = pl.pallas_call(
            functools.partial(cache_kernel, groups, tensors),
            out_shape=cache_shape,
            in_specs=[SMEM] + [VMEM] * groups,
            out_specs=VMEM,
            compiler_params=params,
            name="place_pages",
        )(plan, *handed)
    return (
        attention.reshape(slots * BLOCK, width_q),
        cache.reshape(pages, 2, tokens, tensors * width_k),
    )


def solution(mesh):
    return jax.shard_map(
        per_device,
        mesh=mesh,
        in_specs=(
            P(("parts", "group"), "tensor"),
            P(("parts", "group"), "tensor"),
            P(("parts", "group"), "tensor"),
            P(("parts", "group"), "tensor"),
            P(("parts", "group"), "tensor"),
            P("parts"),
            P("parts"),
            P("parts", None),
            P("parts", None),
            P("parts", None),
            P("parts", None),
        ),
        out_specs=(P(("parts", "group"), "tensor"), P(("parts", "group"), None, "tensor", None)),
        check_vma=False,
    )
```

```python
import functools
import math

import jax
import jax.numpy as jnp
import numpy as np
from jax import lax
from jax.experimental import pallas as pl
from jax.experimental.pallas import tpu as pltpu
from jax.sharding import PartitionSpec as P

HEAD = 128
BLOCK = 8
MAXP = 2
CTXP = 64

VMEM_LIMIT = 24 * 1024 * 1024

SMEM = pl.BlockSpec(memory_space=pltpu.SMEM)
VMEM = pl.BlockSpec(memory_space=pltpu.VMEM)
PROMPT, OFFSET, LIVE, CACHED, SOURCE, COLUMN = range(6)
ANY = pl.BlockSpec(memory_space=pl.ANY)
HBM = pl.BlockSpec(memory_space=pltpu.HBM)


def rope_table():
    count = CTXP + MAXP * BLOCK
    half = HEAD // 2
    frequency = np.exp(np.arange(half) * (-2.0 * math.log(500000.0) / HEAD))
    angles = np.arange(count)[:, None] * frequency[None, :]
    cosine, sine = np.cos(angles), np.sin(angles)
    return (
        np.concatenate([cosine, cosine], axis=1).astype(np.float32),
        np.concatenate([-sine, sine], axis=1).astype(np.float32),
    )


def loop(count, body, unrolled=16):
    if count <= unrolled:
        for index in range(count):
            body(index)
    else:
        lax.fori_loop(0, count, lambda index, carry: (body(index), carry)[1], 0)


def turned(head_block, cosine, sine):
    return head_block * cosine + pltpu.roll(head_block, HEAD // 2, 1) * sine


def dispatch_kernel(groups, spread_in, turn_in, queries_in, keys_in, values_in, *rest):
    outs, (spread, turn, queries, keys, values, sem) = rest[:groups], rest[groups:]
    own = lax.axis_index("group")
    slots, _, width_q = queries.shape
    width_k = keys.shape[2]
    capacity = slots // groups
    copies = [
        pltpu.make_async_copy(source, target, sem.at[n])
        for n, (source, target) in enumerate(
            (
                (spread_in, spread),
                (turn_in, turn),
                (queries_in, queries),
                (keys_in, keys),
                (values_in, values),
            )
        )
    ]
    for copy in copies:
        copy.start()
    for copy in copies[:2]:
        copy.wait()
    sources = []
    for distance in range(groups):
        first_slot = column_of(spread, groups, distance) + turn[own]
        sources.append([lax.rem(first_slot + groups * step, slots) for step in range(capacity)])
    for copy in copies[2:]:
        copy.wait()
    for distance in range(groups):
        for step in range(capacity):
            source = sources[distance][step]
            out = outs[distance]
            out[step, :, :width_q] = queries[source]
            out[step, :, width_q : width_q + width_k] = keys[source]
            out[step, :, width_q + width_k :] = values[source]


def column_of(spread, groups, distance):
    wanted = (groups - distance) % groups
    if groups <= 8:
        return sum(jnp.where(spread[c] == wanted, c, 0) for c in range(groups))
    return lax.fori_loop(
        0, groups, lambda c, found: jnp.where(spread[c] == wanted, c, found), jnp.int32(0)
    )


def make_plan(groups, own, spread, new_blocks, prefix_len, owner, page_start, plan):
    prompts = new_blocks.shape[1]
    slots = prompts * MAXP

    def clear(j):
        plan[PROMPT, j] = 0
        plan[OFFSET, j] = 0
        plan[LIVE, j] = 0
        plan[CACHED, j] = 0

    loop(slots, clear)

    def one(p, start):
        blocks = new_blocks[own, p]
        cached = prefix_len[own, p]
        for step in range(MAXP):
            at = jnp.where(step < blocks, start + step, slots)
            plan[PROMPT, at] = p
            plan[OFFSET, at] = cached + step * BLOCK
            plan[LIVE, at] = 1 + step
            plan[CACHED, at] = cached
        return start + blocks

    start = jnp.int32(0)
    if prompts <= 8:
        for p in range(prompts):
            start = one(p, start)
    else:
        lax.fori_loop(0, prompts, one, start)

    def of_group(g):
        def one(p, start):
            blocks = new_blocks[g, p]
            mine = owner[g, p] == own
            for step in range(MAXP):
                root = lax.rem(g + spread[lax.rem(start + step, groups)], groups)
                at = jnp.where(mine, page_start[g, p] + step, slots)
                plan[SOURCE, at] = jnp.where(step < blocks, root * groups + g, -1)
            return start + blocks

        start = jnp.int32(0)
        if prompts <= 8:
            for p in range(prompts):
                start = one(p, start)
        else:
            lax.fori_loop(0, prompts, one, start)

    loop(groups, of_group)
    for distance in range(groups):
        plan[COLUMN, distance] = column_of(spread, groups, distance)


def pages_kernel(
    groups, tensors, spread, turn, new_blocks, prefix_len, owner, page_start, keys, values, cosine, sine,
    _, out, plan, rows, dest_group, dest_owner,
):
    own = lax.axis_index("group")
    slots, _, width_k = keys.shape
    capacity = slots // groups
    prompts = new_blocks.shape[1]
    tokens = BLOCK // tensors

    def column(c):
        target = lax.rem(own - spread[c] + groups, groups)
        for step in range(capacity):
            j = c + groups * step
            source = lax.rem(j + turn[own], slots)

            def find(p, carry):
                start, place, holder = carry
                blocks = new_blocks[target, p]
                inside = (j >= start) & (j < start + blocks)
                place = jnp.where(inside, prefix_len[target, p] + (j - start) * BLOCK, place)
                holder = jnp.where(inside, owner[target, p], holder)
                return start + blocks, place, holder

            carry = (jnp.int32(0), jnp.int32(0), jnp.int32(-1))
            if prompts <= 8:
                for p in range(prompts):
                    carry = find(p, carry)
            else:
                carry = lax.fori_loop(0, prompts, find, carry)
            _, place, holder = carry
            dest_group[source] = target
            dest_owner[source] = holder
            cos = cosine[pl.ds(place, BLOCK), :]
            sin = sine[pl.ds(place, BLOCK), :]
            block = keys[source].astype(jnp.float32)
            at = pl.multiple_of(source * BLOCK, BLOCK)
            rows[pl.ds(at, BLOCK), :] = jnp.concatenate(
                [
                    turned(block[:, h * HEAD : (h + 1) * HEAD], cos, sin)
                    for h in range(width_k // HEAD)
                ],
                axis=1,
            )
            at = pl.multiple_of((slots + source) * BLOCK, BLOCK)
            rows[pl.ds(at, BLOCK), :] = values[source].astype(jnp.float32)

    loop(groups, column)
    body = rows[...].astype(jnp.bfloat16)
    part = 2 * tokens
    shape = (tensors * groups * part, 2 * slots * BLOCK)
    row = lax.broadcasted_iota(jnp.int32, shape, 0)
    col = lax.broadcasted_iota(jnp.int32, shape, 1)
    row_tensor = row // (groups * part)
    row_group = (row // part) % groups
    same = ((row // tokens) % 2 == col // (slots * BLOCK)) & (
        row_tensor * tokens + row % tokens == col % BLOCK
    )
    code = jnp.where(same, row_group * slots + (col // BLOCK) % slots, -1)

    def send(d):
        def mark(b, total):
            wanted = jnp.where(dest_owner[b] == d, dest_group[b] * slots + b, -2)
            return total | (code == wanted)

        if slots <= 8:
            total = code == -2
            for b in range(slots):
                total = mark(b, total)
            pick = total.astype(jnp.float32)
        else:
            pick = lax.fori_loop(
                0,
                slots,
                lambda b, total: jnp.where(
                    code == jnp.where(dest_owner[b] == d, dest_group[b] * slots + b, -2), 1.0, total
                ),
                jnp.zeros(shape, jnp.float32),
            )
        moved = jnp.dot(pick.astype(jnp.bfloat16), body, preferred_element_type=jnp.float32)
        out[pl.ds(d * tensors, tensors)] = moved.astype(jnp.bfloat16).reshape(
            tensors, groups * part, width_k
        )

    loop(groups, send)
    make_plan(groups, own, spread, new_blocks, prefix_len, owner, page_start, plan)


def attention_kernel(groups, heads_q, heads_k, plan, prefix_keys, prefix_values, cosine, sine, *rest):
    arrived, (out, new_keys, new_values) = rest[:groups], rest[groups:]
    slots = out.shape[0]
    capacity = slots // groups
    ratio = heads_q // heads_k
    width_q = heads_q * HEAD
    width_k = heads_k * HEAD
    scale = math.log2(math.e) / math.sqrt(HEAD)
    span = CTXP + 2 * BLOCK
    lane = lax.broadcasted_iota(jnp.int32, (BLOCK, span), 1)
    token = lax.broadcasted_iota(jnp.int32, (BLOCK, span), 0)
    fresh = (lane >= CTXP + BLOCK) & (lane - (CTXP + BLOCK) <= token)
    before = (lane >= CTXP) & (lane < CTXP + BLOCK)

    blocks = []
    for distance in range(groups):
        first_slot = plan[COLUMN, distance]
        for step in range(capacity):
            j = first_slot + groups * step
            here = arrived[distance].at[step]
            cos = cosine[pl.ds(plan[OFFSET, j], BLOCK), :]
            sin = sine[pl.ds(plan[OFFSET, j], BLOCK), :]
            new_keys[j] = jnp.concatenate(
                [
                    turned(here[:, first : first + HEAD].astype(jnp.float32), cos, sin)
                    for first in range(width_q, width_q + width_k, HEAD)
                ],
                axis=1,
            )
            new_values[j] = here[:, width_q + width_k :].astype(jnp.float32)
            blocks.append((j, here, cos, sin))

    for at in range(0, len(blocks), 8):
        some = blocks[at : at + 8]
        for h in range(heads_k):
            part = slice(h * HEAD, (h + 1) * HEAD)
            scores = []
            for j, here, cos, sin in some:
                prev = jnp.maximum(j - 1, 0)
                region = pl.ds(pl.multiple_of(plan[PROMPT, j] * CTXP, CTXP), CTXP)
                mask = fresh | (lane < plan[CACHED, j]) & (lane < CTXP) | before & (plan[LIVE, j] == 2)
                new_key = jnp.concatenate([new_keys[prev, :, part], new_keys[j, :, part]], axis=0)
                key = jnp.concatenate([prefix_keys[region, part], new_key.astype(jnp.bfloat16)], axis=0)
                query = jnp.concatenate(
                    [
                        turned(here[:, n * HEAD : (n + 1) * HEAD].astype(jnp.float32), cos, sin)
                        for n in range(h * ratio, (h + 1) * ratio)
                    ],
                    axis=0,
                ).astype(jnp.bfloat16)
                score = lax.dot_general(
                    query, key, (((1,), (1,)), ((), ())), preferred_element_type=jnp.float32
                )
                scores.append(jnp.where(mask[None], score.reshape(ratio, BLOCK, span), -1e30))
            score = jnp.concatenate(scores, axis=0)
            top = jnp.max(score, axis=2, keepdims=True)
            powers = jnp.exp2((score - top) * scale)
            weights = powers * (1.0 / jnp.sum(powers, axis=2, keepdims=True))
            weights = weights.reshape(len(some), ratio * BLOCK, span).astype(jnp.bfloat16)
            for place, (j, here, cos, sin) in enumerate(some):
                prev = jnp.maximum(j - 1, 0)
                region = pl.ds(pl.multiple_of(plan[PROMPT, j] * CTXP, CTXP), CTXP)
                new_value = jnp.concatenate([new_values[prev, :, part], new_values[j, :, part]], axis=0)
                value = jnp.concatenate([prefix_values[region, part], new_value.astype(jnp.bfloat16)], axis=0)
                mixed = jnp.dot(weights[place], value, preferred_element_type=jnp.float32)
                mixed = jnp.where(plan[LIVE, j] > 0, mixed, 0.0)
                for n in range(ratio):
                    first = (h * ratio + n) * HEAD
                    out[j, :, first : first + HEAD] = mixed[n * BLOCK : (n + 1) * BLOCK].astype(
                        jnp.bfloat16
                    )


def cache_kernel(groups, tensors, plan, arrived, _, out):
    tokens = BLOCK // tensors
    part = 2 * tokens
    pages = out.shape[0] // 2
    shape = (pages * part, groups * groups * part)
    row = lax.broadcasted_iota(jnp.int32, shape, 0)
    col = lax.broadcasted_iota(jnp.int32, shape, 1)
    limit = groups * groups
    code = jnp.where(row % part == col % part, (row // part) * limit + col // part, -1)

    def mark(page, total):
        wanted = jnp.where(plan[SOURCE, page] >= 0, page * limit + plan[SOURCE, page], -2)
        return jnp.where(code == wanted, 1.0, total)

    pick = jnp.zeros(shape, jnp.float32)
    if pages <= 8:
        for page in range(pages):
            pick = mark(page, pick)
    else:
        pick = lax.fori_loop(0, pages, mark, pick)
    pick = pick.astype(jnp.bfloat16)
    width_k = arrived.shape[3]
    for t in range(tensors):
        body = arrived[:, t].reshape(groups * groups * part, width_k)
        moved = jnp.dot(pick, body, preferred_element_type=jnp.float32)
        out[:, :, t * width_k : (t + 1) * width_k] = moved.reshape(
            pages * 2, tokens, width_k
        ).astype(jnp.bfloat16)


def in_hbm(operand):
    return pltpu.with_memory_space_constraint(operand, pltpu.HBM)


def per_device(
    queries,
    keys,
    values,
    prefix_keys,
    prefix_values,
    spread,
    turn,
    new_blocks,
    prefix_len,
    owner,
    page_start,
):
    groups = lax.axis_size("group")
    tensors = lax.axis_size("tensor")
    width_q = queries.shape[1]
    width_k = keys.shape[1]
    heads_q = width_q // HEAD
    heads_k = width_k // HEAD
    slots = queries.shape[0] // BLOCK
    capacity = slots // groups
    prompts = new_blocks.shape[1]
    tokens = BLOCK // tensors
    pages = prompts * MAXP
    cosine, sine = (jnp.asarray(table) for table in rope_table())
    params = pltpu.CompilerParams(vmem_limit_bytes=VMEM_LIMIT)
    blocks_q = queries.reshape(slots, BLOCK, width_q)
    blocks_k = keys.reshape(slots, BLOCK, width_k)
    blocks_v = values.reshape(slots, BLOCK, width_k)

    chunk = jax.ShapeDtypeStruct((capacity, BLOCK, width_q + 2 * width_k), jnp.bfloat16)
    sent = pl.pallas_call(
        functools.partial(dispatch_kernel, groups),
        out_shape=[chunk] * groups,
        in_specs=[HBM] * 5,
        out_specs=[VMEM] * groups,
        scratch_shapes=[pltpu.SMEM((groups,), jnp.int32)] * 2
        + [pltpu.VMEM(blocks.shape, jnp.bfloat16) for blocks in (blocks_q, blocks_k, blocks_v)]
        + [pltpu.SemaphoreType.DMA((5,))],
        compiler_params=params,
        name="dispatch",
    )(
        *(in_hbm(operand) for operand in (spread, turn, blocks_q, blocks_k, blocks_v))
    )
    arrived = [sent[0]] + [
        lax.ppermute(sent[d], "group", [(g, (g + d) % groups) for g in range(groups)])
        for d in range(1, groups)
    ]

    finished, plan = pl.pallas_call(
        functools.partial(pages_kernel, groups, tensors),
        out_shape=[
            jax.ShapeDtypeStruct((groups * tensors, groups * 2 * tokens, width_k), jnp.bfloat16),
            jax.ShapeDtypeStruct((6, max(slots, groups) + 1), jnp.int32),
        ],
        in_specs=[SMEM] * 6 + [VMEM] * 4 + [ANY],
        out_specs=[VMEM, SMEM],
        compiler_params=params,
        scratch_shapes=[
            pltpu.VMEM((2 * slots * BLOCK, width_k), jnp.float32),
            pltpu.SMEM((slots,), jnp.int32),
            pltpu.SMEM((slots,), jnp.int32),
        ],
        name="finish_pages",
    )(
        spread, turn, new_blocks, prefix_len, owner, page_start, blocks_k, blocks_v, cosine, sine, sent[0]
    )
    handed = lax.fori_loop(
        0,
        lax.optimization_barrier(jnp.int32(1)),
        lambda _, rows: lax.all_to_all(rows, ("group", "tensor"), split_axis=0, concat_axis=0, tiled=True),
        finished,
    )

    attention = pl.pallas_call(
        functools.partial(attention_kernel, groups, heads_q, heads_k),
        out_shape=jax.ShapeDtypeStruct((slots, BLOCK, width_q), jnp.bfloat16),
        in_specs=[SMEM] + [VMEM] * (4 + groups),
        out_specs=VMEM,
        scratch_shapes=[pltpu.VMEM((slots, BLOCK, width_k), jnp.float32)] * 2,
        compiler_params=params,
        name="attention",
    )(plan, prefix_keys, prefix_values, cosine, sine, *arrived)

    cache = pl.pallas_call(
        functools.partial(cache_kernel, groups, tensors),
        out_shape=jax.ShapeDtypeStruct((pages * 2, tokens, tensors * width_k), jnp.bfloat16),
        in_specs=[SMEM, VMEM, ANY],
        out_specs=VMEM,
        compiler_params=params,
        name="place_pages",
    )(plan, handed.reshape(groups, tensors, groups * 2 * tokens, width_k), in_hbm(attention))
    return (
        attention.reshape(slots * BLOCK, width_q),
        cache.reshape(pages, 2, tokens, tensors * width_k),
    )


def solution(mesh):
    return jax.shard_map(
        per_device,
        mesh=mesh,
        in_specs=(
            P(("parts", "group"), "tensor"),
            P(("parts", "group"), "tensor"),
            P(("parts", "group"), "tensor"),
            P(("parts", "group"), "tensor"),
            P(("parts", "group"), "tensor"),
            P("parts"),
            P("parts"),
            P("parts", None),
            P("parts", None),
            P("parts", None),
            P("parts", None),
        ),
        out_specs=(P(("parts", "group"), "tensor"), P(("parts", "group"), None, "tensor", None)),
        check_vma=False,
    )
```

```python
import functools
import math

import jax
import jax.numpy as jnp
import numpy as np
from jax import lax
from jax.experimental import pallas as pl
from jax.experimental.pallas import tpu as pltpu
from jax.sharding import PartitionSpec as P

HEAD = 128
BLOCK = 8
MAXP = 2
CTXP = 64

VMEM_LIMIT = 24 * 1024 * 1024

SMEM = pl.BlockSpec(memory_space=pltpu.SMEM)
VMEM = pl.BlockSpec(memory_space=pltpu.VMEM)
PROMPT, OFFSET, LIVE, CACHED, SOURCE, COLUMN, PLACE = range(7)
ANY = pl.BlockSpec(memory_space=pl.ANY)
HBM = pl.BlockSpec(memory_space=pltpu.HBM)


def rope_table():
    count = CTXP + MAXP * BLOCK
    half = HEAD // 2
    frequency = np.exp(np.arange(half) * (-2.0 * math.log(500000.0) / HEAD))
    angles = np.arange(count)[:, None] * frequency[None, :]
    cosine, sine = np.cos(angles), np.sin(angles)
    return (
        np.concatenate([cosine, cosine], axis=1).astype(np.float32),
        np.concatenate([-sine, sine], axis=1).astype(np.float32),
    )


def loop(count, body, unrolled=16):
    if count <= unrolled:
        for index in range(count):
            body(index)
    else:
        lax.fori_loop(0, count, lambda index, carry: (body(index), carry)[1], 0)


def turned(head_block, cosine, sine):
    return head_block * cosine + pltpu.roll(head_block, HEAD // 2, 1) * sine


def dispatch_kernel(
    groups, spread_in, turn_in, new_blocks_in, owner_in, queries_in, keys_in, values_in, *rest
):
    outs, handed, rest = rest[:groups], rest[groups : 2 * groups], rest[2 * groups :]
    spread, turn, new_blocks, owner, queries, keys, values, table, sem = rest
    own = lax.axis_index("group")
    slots, _, width_q = queries.shape
    width_k = keys.shape[2]
    capacity = slots // groups
    prompts = new_blocks.shape[1]
    copies = [
        pltpu.make_async_copy(source, target, sem.at[n])
        for n, (source, target) in enumerate(
            (
                (spread_in, spread),
                (turn_in, turn),
                (new_blocks_in, new_blocks),
                (owner_in, owner),
                (keys_in, keys),
                (values_in, values),
                (queries_in, queries),
            )
        )
    ]
    for copy in copies:
        copy.start()
    for copy in copies[:4]:
        copy.wait()

    def clear(n):
        table[n] = 0

    loop(groups * groups, clear)

    def column(c):
        target = lax.rem(own - spread[c] + groups, groups)

        def find(p, carry):
            start, holders = carry
            blocks = new_blocks[target, p]
            holders = [
                jnp.where((c + groups * n >= start) & (c + groups * n < start + blocks), owner[target, p], holder)
                for n, holder in enumerate(holders)
            ]
            return start + blocks, holders

        carry = (jnp.int32(0), [jnp.int32(-1)] * capacity)
        if prompts <= 8:
            for p in range(prompts):
                carry = find(p, carry)
        else:
            carry = lax.fori_loop(0, prompts, find, carry)
        for n, holder in enumerate(carry[1]):
            at = lax.rem(holder - own + groups, groups) * groups + target
            table[jnp.where(holder >= 0, at, groups * groups)] = lax.rem(c + groups * n + turn[own], slots)

    loop(groups, column)
    for copy in copies[4:]:
        copy.wait()
    for distance in range(groups):
        first_slot = column_of(spread, groups, distance) + turn[own]
        out = outs[distance]
        for step in range(capacity):
            source = lax.rem(first_slot + groups * step, slots)
            out[step, :, :width_q] = queries[source]
            out[step, :, width_q : width_q + width_k] = keys[source]
            out[step, :, width_q + width_k :] = values[source]

        def page(g):
            source = table[distance * groups + g]
            handed[distance][g, :, :width_k] = keys[source]
            handed[distance][g, :, width_k:] = values[source]

        loop(groups, page)


def column_of(spread, groups, distance):
    wanted = (groups - distance) % groups
    if groups <= 8:
        return sum(jnp.where(spread[c] == wanted, c, 0) for c in range(groups))
    return lax.fori_loop(
        0, groups, lambda c, found: jnp.where(spread[c] == wanted, c, found), jnp.int32(0)
    )


def make_plan(groups, own, spread, new_blocks, prefix_len, owner, page_start, plan):
    prompts = new_blocks.shape[1]
    slots = prompts * MAXP

    def clear(j):
        plan[PROMPT, j] = 0
        plan[OFFSET, j] = 0
        plan[LIVE, j] = 0
        plan[CACHED, j] = 0

    loop(slots, clear)

    def one(p, start):
        blocks = new_blocks[own, p]
        cached = prefix_len[own, p]
        for step in range(MAXP):
            at = jnp.where(step < blocks, start + step, slots)
            plan[PROMPT, at] = p
            plan[OFFSET, at] = cached + step * BLOCK
            plan[LIVE, at] = 1 + step
            plan[CACHED, at] = cached
        return start + blocks

    start = jnp.int32(0)
    if prompts <= 8:
        for p in range(prompts):
            start = one(p, start)
    else:
        lax.fori_loop(0, prompts, one, start)

    def of_group(g):
        def one(p, start):
            blocks = new_blocks[g, p]
            mine = owner[g, p] == own
            for step in range(MAXP):
                root = lax.rem(g + spread[lax.rem(start + step, groups)], groups)
                at = jnp.where(mine, page_start[g, p] + step, slots)
                away = lax.rem(own - root + groups, groups)
                plan[SOURCE, at] = jnp.where(step < blocks, away * groups + g, -1)
                plan[PLACE, at] = prefix_len[g, p] + step * BLOCK
            return start + blocks

        start = jnp.int32(0)
        if prompts <= 8:
            for p in range(prompts):
                start = one(p, start)
        else:
            lax.fori_loop(0, prompts, one, start)

    loop(groups, of_group)
    for distance in range(groups):
        plan[COLUMN, distance] = column_of(spread, groups, distance)


def pages_kernel(
    groups, tensors, spread, new_blocks, prefix_len, owner, page_start, cosine, sine, *rest
):
    chunks, rest = rest[:groups], rest[groups:]
    outs, (plan, blocks, rows) = rest[:tensors], rest[tensors:]
    own = lax.axis_index("group")
    own_tensor = lax.axis_index("tensor")
    pages = new_blocks.shape[1] * MAXP
    width_k = rows.shape[1]
    tokens = BLOCK // tensors
    for distance in range(groups):
        blocks[distance * groups : (distance + 1) * groups] = chunks[distance][...]
    make_plan(groups, own, spread, new_blocks, prefix_len, owner, page_start, plan)

    def assemble(page):
        source = plan[SOURCE, page]
        place = plan[PLACE, page]
        block = blocks[jnp.maximum(source, 0)].astype(jnp.float32)
        block = jnp.where(source >= 0, block, 0.0)
        cos = cosine[pl.ds(place, BLOCK), :]
        sin = sine[pl.ds(place, BLOCK), :]
        for first in range(0, width_k, HEAD):
            part = slice(first, first + HEAD)
            rows[pl.ds(pl.multiple_of(page * BLOCK, BLOCK), BLOCK), part] = turned(
                block[:, part], cos, sin
            )
        rows[pl.ds(pl.multiple_of((pages + page) * BLOCK, BLOCK), BLOCK), :] = block[:, width_k:]

    loop(pages, assemble)
    size = pages * 2 * tokens
    shape = (tensors * size, 2 * pages * BLOCK)
    row = lax.broadcasted_iota(jnp.int32, shape, 0)
    col = lax.broadcasted_iota(jnp.int32, shape, 1)
    share = lax.rem(row // size + own_tensor, tensors)
    kind, page = (row // tokens) % 2, (row // (2 * tokens)) % pages
    wanted = (kind * pages + page) * BLOCK + share * tokens + row % tokens
    pick = (col == wanted).astype(jnp.float32).astype(jnp.bfloat16)
    moved = jnp.dot(pick, rows[...].astype(jnp.bfloat16), preferred_element_type=jnp.float32)
    moved = moved.astype(jnp.bfloat16)
    for distance in range(tensors):
        outs[distance][...] = moved[distance * size : (distance + 1) * size]


def attention_kernel(groups, heads_q, heads_k, plan, prefix_keys, prefix_values, cosine, sine, *rest):
    arrived, (out, new_keys, new_values) = rest[:groups], rest[groups:]
    slots = out.shape[0]
    capacity = slots // groups
    ratio = heads_q // heads_k
    width_q = heads_q * HEAD
    width_k = heads_k * HEAD
    scale = math.log2(math.e) / math.sqrt(HEAD)
    span = CTXP + 2 * BLOCK
    lane = lax.broadcasted_iota(jnp.int32, (BLOCK, span), 1)
    token = lax.broadcasted_iota(jnp.int32, (BLOCK, span), 0)
    fresh = (lane >= CTXP + BLOCK) & (lane - (CTXP + BLOCK) <= token)
    before = (lane >= CTXP) & (lane < CTXP + BLOCK)

    blocks = []
    for distance in range(groups):
        first_slot = plan[COLUMN, distance]
        for step in range(capacity):
            j = first_slot + groups * step
            here = arrived[distance].at[step]
            cos = cosine[pl.ds(plan[OFFSET, j], BLOCK), :]
            sin = sine[pl.ds(plan[OFFSET, j], BLOCK), :]
            new_keys[j] = jnp.concatenate(
                [
                    turned(here[:, first : first + HEAD].astype(jnp.float32), cos, sin)
                    for first in range(width_q, width_q + width_k, HEAD)
                ],
                axis=1,
            )
            new_values[j] = here[:, width_q + width_k :].astype(jnp.float32)
            blocks.append((j, here, cos, sin))

    for at in range(0, len(blocks), 8):
        some = blocks[at : at + 8]
        for h in range(heads_k):
            part = slice(h * HEAD, (h + 1) * HEAD)
            scores = []
            for j, here, cos, sin in some:
                prev = jnp.maximum(j - 1, 0)
                region = pl.ds(pl.multiple_of(plan[PROMPT, j] * CTXP, CTXP), CTXP)
                mask = fresh | (lane < plan[CACHED, j]) & (lane < CTXP) | before & (plan[LIVE, j] == 2)
                new_key = jnp.concatenate([new_keys[prev, :, part], new_keys[j, :, part]], axis=0)
                key = jnp.concatenate([prefix_keys[region, part], new_key.astype(jnp.bfloat16)], axis=0)
                query = jnp.concatenate(
                    [
                        turned(here[:, n * HEAD : (n + 1) * HEAD].astype(jnp.float32), cos, sin)
                        for n in range(h * ratio, (h + 1) * ratio)
                    ],
                    axis=0,
                ).astype(jnp.bfloat16)
                score = lax.dot_general(
                    query, key, (((1,), (1,)), ((), ())), preferred_element_type=jnp.float32
                )
                scores.append(jnp.where(mask[None], score.reshape(ratio, BLOCK, span), -1e30))
            score = jnp.concatenate(scores, axis=0)
            top = jnp.max(score, axis=2, keepdims=True)
            powers = jnp.exp2((score - top) * scale)
            weights = powers * (1.0 / jnp.sum(powers, axis=2, keepdims=True))
            weights = weights.reshape(len(some), ratio * BLOCK, span).astype(jnp.bfloat16)
            for place, (j, here, cos, sin) in enumerate(some):
                prev = jnp.maximum(j - 1, 0)
                region = pl.ds(pl.multiple_of(plan[PROMPT, j] * CTXP, CTXP), CTXP)
                new_value = jnp.concatenate([new_values[prev, :, part], new_values[j, :, part]], axis=0)
                value = jnp.concatenate([prefix_values[region, part], new_value.astype(jnp.bfloat16)], axis=0)
                mixed = jnp.dot(weights[place], value, preferred_element_type=jnp.float32)
                mixed = jnp.where(plan[LIVE, j] > 0, mixed, 0.0)
                for n in range(ratio):
                    first = (h * ratio + n) * HEAD
                    out[j, :, first : first + HEAD] = mixed[n * BLOCK : (n + 1) * BLOCK].astype(
                        jnp.bfloat16
                    )


def cache_kernel(tensors, *rest):
    arrived, out = rest[:tensors], rest[tensors + 1]
    own_tensor = lax.axis_index("tensor")
    width_k = arrived[0].shape[1]
    for distance in range(tensors):
        sender = lax.rem(own_tensor - distance + tensors, tensors)
        at = pl.ds(pl.multiple_of(sender * width_k, HEAD), width_k)
        part = arrived[distance][...].astype(jnp.float32)
        out[:, :, at] = part.reshape(out.shape[0], out.shape[1], width_k).astype(jnp.bfloat16)


def in_hbm(operand):
    return pltpu.with_memory_space_constraint(operand, pltpu.HBM)


def shifted(chunks, axis):
    size = lax.axis_size(axis)
    return [chunks[0]] + [
        lax.ppermute(chunks[d], axis, [(i, (i + d) % size) for i in range(size)])
        for d in range(1, size)
    ]


def per_device(
    queries,
    keys,
    values,
    prefix_keys,
    prefix_values,
    spread,
    turn,
    new_blocks,
    prefix_len,
    owner,
    page_start,
):
    groups = lax.axis_size("group")
    tensors = lax.axis_size("tensor")
    width_q = queries.shape[1]
    width_k = keys.shape[1]
    heads_q = width_q // HEAD
    heads_k = width_k // HEAD
    slots = queries.shape[0] // BLOCK
    capacity = slots // groups
    prompts = new_blocks.shape[1]
    tokens = BLOCK // tensors
    pages = prompts * MAXP
    cosine, sine = (jnp.asarray(table) for table in rope_table())
    params = pltpu.CompilerParams(vmem_limit_bytes=VMEM_LIMIT)
    blocks_q = queries.reshape(slots, BLOCK, width_q)
    blocks_k = keys.reshape(slots, BLOCK, width_k)
    blocks_v = values.reshape(slots, BLOCK, width_k)

    chunk = jax.ShapeDtypeStruct((capacity, BLOCK, width_q + 2 * width_k), jnp.bfloat16)
    page_chunk = jax.ShapeDtypeStruct((groups, BLOCK, 2 * width_k), jnp.bfloat16)
    sent = pl.pallas_call(
        functools.partial(dispatch_kernel, groups),
        out_shape=[chunk] * groups + [page_chunk] * groups,
        in_specs=[HBM] * 7,
        out_specs=[VMEM] * (2 * groups),
        scratch_shapes=[
            *(pltpu.SMEM(array.shape, jnp.int32) for array in (spread, turn, new_blocks, owner)),
            *(pltpu.VMEM(array.shape, jnp.bfloat16) for array in (blocks_q, blocks_k, blocks_v)),
            pltpu.SMEM((groups * groups + 1,), jnp.int32),
            pltpu.SemaphoreType.DMA((7,)),
        ],
        compiler_params=params,
        name="dispatch",
    )(
        *(
            in_hbm(operand)
            for operand in (spread, turn, new_blocks, owner, blocks_q, blocks_k, blocks_v)
        )
    )
    arrived = shifted(sent[:groups], "group")
    handed = shifted(sent[groups:], "group")

    part = jax.ShapeDtypeStruct((pages * 2 * tokens, width_k), jnp.bfloat16)
    *finished, plan = pl.pallas_call(
        functools.partial(pages_kernel, groups, tensors),
        out_shape=[part] * tensors + [jax.ShapeDtypeStruct((7, max(slots, groups) + 1), jnp.int32)],
        in_specs=[SMEM] * 5 + [VMEM] * (2 + groups),
        out_specs=[VMEM] * tensors + [SMEM],
        compiler_params=params,
        scratch_shapes=[
            pltpu.VMEM((groups * groups, BLOCK, 2 * width_k), jnp.bfloat16),
            pltpu.VMEM((2 * pages * BLOCK, width_k), jnp.float32),
        ],
        name="finish_pages",
    )(spread, new_blocks, prefix_len, owner, page_start, cosine, sine, *handed)
    parts = shifted(finished, "tensor")

    attention = pl.pallas_call(
        functools.partial(attention_kernel, groups, heads_q, heads_k),
        out_shape=jax.ShapeDtypeStruct((slots, BLOCK, width_q), jnp.bfloat16),
        in_specs=[SMEM] + [VMEM] * (4 + groups),
        out_specs=VMEM,
        scratch_shapes=[pltpu.VMEM((slots, BLOCK, width_k), jnp.float32)] * 2,
        compiler_params=params,
        name="attention",
    )(plan, prefix_keys, prefix_values, cosine, sine, *arrived)

    cache = pl.pallas_call(
        functools.partial(cache_kernel, tensors),
        out_shape=jax.ShapeDtypeStruct((pages * 2, tokens, tensors * width_k), jnp.bfloat16),
        in_specs=[VMEM] * tensors + [ANY],
        out_specs=VMEM,
        compiler_params=params,
        name="place_pages",
    )(*parts, in_hbm(attention))
    return (
        attention.reshape(slots * BLOCK, width_q),
        cache.reshape(pages, 2, tokens, tensors * width_k),
    )


def solution(mesh):
    return jax.shard_map(
        per_device,
        mesh=mesh,
        in_specs=(
            P(("parts", "group"), "tensor"),
            P(("parts", "group"), "tensor"),
            P(("parts", "group"), "tensor"),
            P(("parts", "group"), "tensor"),
            P(("parts", "group"), "tensor"),
            P("parts"),
            P("parts"),
            P("parts", None),
            P("parts", None),
            P("parts", None),
            P("parts", None),
        ),
        out_specs=(P(("parts", "group"), "tensor"), P(("parts", "group"), None, "tensor", None)),
        check_vma=False,
    )
```

```python
import functools
import math

import jax
import jax.numpy as jnp
import numpy as np
from jax import lax
from jax.experimental import pallas as pl
from jax.experimental.pallas import tpu as pltpu
from jax.sharding import PartitionSpec as P

HEAD = 128
BLOCK = 8
MAXP = 2
CTXP = 64

VMEM_LIMIT = 24 * 1024 * 1024

SMEM = pl.BlockSpec(memory_space=pltpu.SMEM)
VMEM = pl.BlockSpec(memory_space=pltpu.VMEM)
PROMPT, OFFSET, LIVE, CACHED, SOURCE, COLUMN, PLACE = range(7)
ANY = pl.BlockSpec(memory_space=pl.ANY)
HBM = pl.BlockSpec(memory_space=pltpu.HBM)


def rope_table():
    count = CTXP + MAXP * BLOCK
    half = HEAD // 2
    frequency = np.exp(np.arange(half) * (-2.0 * math.log(500000.0) / HEAD))
    angles = np.arange(count)[:, None] * frequency[None, :]
    cosine, sine = np.cos(angles), np.sin(angles)
    return (
        np.concatenate([cosine, cosine], axis=1).astype(np.float32),
        np.concatenate([-sine, sine], axis=1).astype(np.float32),
    )


def loop(count, body, unrolled=16):
    if count <= unrolled:
        for index in range(count):
            body(index)
    else:
        lax.fori_loop(0, count, lambda index, carry: (body(index), carry)[1], 0)


def turned(head_block, cosine, sine):
    return head_block * cosine + pltpu.roll(head_block, HEAD // 2, 1) * sine


def dispatch_kernel(
    groups, spread_in, turn_in, new_blocks_in, owner_in, queries_in, keys_in, values_in, *rest
):
    outs, handed, rest = rest[:groups], rest[groups : 2 * groups], rest[2 * groups :]
    spread, turn, new_blocks, owner, queries, keys, values, table, sem = rest
    own = lax.axis_index("group")
    slots, _, width_q = queries.shape
    width_k = keys.shape[2]
    capacity = slots // groups
    prompts = new_blocks.shape[1]
    copies = [
        pltpu.make_async_copy(source, target, sem.at[n])
        for n, (source, target) in enumerate(
            (
                (spread_in, spread),
                (turn_in, turn),
                (new_blocks_in, new_blocks),
                (owner_in, owner),
                (keys_in, keys),
                (values_in, values),
                (queries_in, queries),
            )
        )
    ]
    for copy in copies:
        copy.start()
    for copy in copies[:4]:
        copy.wait()

    def clear(n):
        table[n] = 0

    loop(groups * groups, clear)

    def column(c):
        target = lax.rem(own - spread[c] + groups, groups)

        def find(p, carry):
            start, holders = carry
            blocks = new_blocks[target, p]
            holders = [
                jnp.where((c + groups * n >= start) & (c + groups * n < start + blocks), owner[target, p], holder)
                for n, holder in enumerate(holders)
            ]
            return start + blocks, holders

        carry = (jnp.int32(0), [jnp.int32(-1)] * capacity)
        if prompts <= 8:
            for p in range(prompts):
                carry = find(p, carry)
        else:
            carry = lax.fori_loop(0, prompts, find, carry)
        for n, holder in enumerate(carry[1]):
            at = lax.rem(holder - own + groups, groups) * groups + target
            table[jnp.where(holder >= 0, at, groups * groups)] = lax.rem(c + groups * n + turn[own], slots)

    loop(groups, column)
    for copy in copies[4:]:
        copy.wait()
    for distance in range(groups):
        first_slot = column_of(spread, groups, distance) + turn[own]
        out = outs[distance]
        for step in range(capacity):
            source = lax.rem(first_slot + groups * step, slots)
            out[step, :, :width_q] = queries[source]
            out[step, :, width_q : width_q + width_k] = keys[source]
            out[step, :, width_q + width_k :] = values[source]

        def page(g):
            source = table[distance * groups + g]
            handed[distance][g, :, :width_k] = keys[source]
            handed[distance][g, :, width_k:] = values[source]

        loop(groups, page)


def column_of(spread, groups, distance):
    wanted = (groups - distance) % groups
    if groups <= 8:
        return sum(jnp.where(spread[c] == wanted, c, 0) for c in range(groups))
    return lax.fori_loop(
        0, groups, lambda c, found: jnp.where(spread[c] == wanted, c, found), jnp.int32(0)
    )


def make_plan(groups, own, spread, new_blocks, prefix_len, owner, page_start, plan):
    prompts = new_blocks.shape[1]
    slots = prompts * MAXP

    def clear(j):
        plan[PROMPT, j] = 0
        plan[OFFSET, j] = 0
        plan[LIVE, j] = 0
        plan[CACHED, j] = 0

    loop(slots, clear)

    def one(p, start):
        blocks = new_blocks[own, p]
        cached = prefix_len[own, p]
        for step in range(MAXP):
            at = jnp.where(step < blocks, start + step, slots)
            plan[PROMPT, at] = p
            plan[OFFSET, at] = cached + step * BLOCK
            plan[LIVE, at] = 1 + step
            plan[CACHED, at] = cached
        return start + blocks

    start = jnp.int32(0)
    if prompts <= 8:
        for p in range(prompts):
            start = one(p, start)
    else:
        lax.fori_loop(0, prompts, one, start)

    def of_group(g):
        def one(p, start):
            blocks = new_blocks[g, p]
            mine = owner[g, p] == own
            for step in range(MAXP):
                root = lax.rem(g + spread[lax.rem(start + step, groups)], groups)
                at = jnp.where(mine, page_start[g, p] + step, slots)
                away = lax.rem(own - root + groups, groups)
                plan[SOURCE, at] = jnp.where(step < blocks, away * groups + g, -1)
                plan[PLACE, at] = prefix_len[g, p] + step * BLOCK
            return start + blocks

        start = jnp.int32(0)
        if prompts <= 8:
            for p in range(prompts):
                start = one(p, start)
        else:
            lax.fori_loop(0, prompts, one, start)

    loop(groups, of_group)
    for distance in range(groups):
        plan[COLUMN, distance] = column_of(spread, groups, distance)


def pages_kernel(
    groups, tensors, spread, new_blocks, prefix_len, owner, page_start, cosine, sine, *rest
):
    chunks, rest = rest[:groups], rest[groups:]
    outs, (plan, blocks, rows) = rest[:tensors], rest[tensors:]
    own = lax.axis_index("group")
    own_tensor = lax.axis_index("tensor")
    pages = new_blocks.shape[1] * MAXP
    width_k = rows.shape[1]
    tokens = BLOCK // tensors
    for distance in range(groups):
        blocks[distance * groups : (distance + 1) * groups] = chunks[distance][...]
    make_plan(groups, own, spread, new_blocks, prefix_len, owner, page_start, plan)

    def assemble(page):
        source = plan[SOURCE, page]
        place = plan[PLACE, page]
        block = blocks[jnp.maximum(source, 0)].astype(jnp.float32)
        block = jnp.where(source >= 0, block, 0.0)
        cos = cosine[pl.ds(place, BLOCK), :]
        sin = sine[pl.ds(place, BLOCK), :]
        for first in range(0, width_k, HEAD):
            part = slice(first, first + HEAD)
            rows[pl.ds(pl.multiple_of(page * BLOCK, BLOCK), BLOCK), part] = turned(
                block[:, part], cos, sin
            )
        rows[pl.ds(pl.multiple_of((pages + page) * BLOCK, BLOCK), BLOCK), :] = block[:, width_k:]

    loop(pages, assemble)
    size = pages * 2 * tokens
    shape = (tensors * size, 2 * pages * BLOCK)
    row = lax.broadcasted_iota(jnp.int32, shape, 0)
    col = lax.broadcasted_iota(jnp.int32, shape, 1)
    share = lax.rem(row // size + own_tensor, tensors)
    kind, page = (row // tokens) % 2, (row // (2 * tokens)) % pages
    wanted = (kind * pages + page) * BLOCK + share * tokens + row % tokens
    pick = (col == wanted).astype(jnp.float32).astype(jnp.bfloat16)
    moved = jnp.dot(pick, rows[...].astype(jnp.bfloat16), preferred_element_type=jnp.float32)
    moved = moved.astype(jnp.bfloat16)
    for distance in range(tensors):
        outs[distance][...] = moved[distance * size : (distance + 1) * size]


def attention_kernel(groups, heads_q, heads_k, plan, prefix_keys, prefix_values, cosine, sine, *rest):
    arrived, (out, new_keys, new_values) = rest[:groups], rest[groups:]
    slots = out.shape[0]
    capacity = slots // groups
    ratio = heads_q // heads_k
    width_q = heads_q * HEAD
    width_k = heads_k * HEAD
    scale = math.log2(math.e) / math.sqrt(HEAD)
    span = CTXP + 2 * BLOCK
    lane = lax.broadcasted_iota(jnp.int32, (BLOCK, span), 1)
    token = lax.broadcasted_iota(jnp.int32, (BLOCK, span), 0)
    fresh = (lane >= CTXP + BLOCK) & (lane - (CTXP + BLOCK) <= token)
    before = (lane >= CTXP) & (lane < CTXP + BLOCK)

    blocks = []
    for distance in range(groups):
        first_slot = plan[COLUMN, distance]
        for step in range(capacity):
            j = first_slot + groups * step
            here = arrived[distance].at[step]
            cos = cosine[pl.ds(plan[OFFSET, j], BLOCK), :]
            sin = sine[pl.ds(plan[OFFSET, j], BLOCK), :]
            new_keys[j] = jnp.concatenate(
                [
                    turned(here[:, first : first + HEAD].astype(jnp.float32), cos, sin)
                    for first in range(width_q, width_q + width_k, HEAD)
                ],
                axis=1,
            )
            new_values[j] = here[:, width_q + width_k :].astype(jnp.float32)
            blocks.append((j, here, cos, sin))

    for at in range(0, len(blocks), 8):
        some = blocks[at : at + 8]
        for h in range(heads_k):
            part = slice(h * HEAD, (h + 1) * HEAD)
            scores = []
            for j, here, cos, sin in some:
                prev = jnp.maximum(j - 1, 0)
                region = pl.ds(pl.multiple_of(plan[PROMPT, j] * CTXP, CTXP), CTXP)
                mask = fresh | (lane < plan[CACHED, j]) & (lane < CTXP) | before & (plan[LIVE, j] == 2)
                new_key = jnp.concatenate([new_keys[prev, :, part], new_keys[j, :, part]], axis=0)
                key = jnp.concatenate([prefix_keys[region, part], new_key.astype(jnp.bfloat16)], axis=0)
                query = jnp.concatenate(
                    [
                        turned(here[:, n * HEAD : (n + 1) * HEAD].astype(jnp.float32), cos, sin)
                        for n in range(h * ratio, (h + 1) * ratio)
                    ],
                    axis=0,
                ).astype(jnp.bfloat16)
                score = lax.dot_general(
                    query, key, (((1,), (1,)), ((), ())), preferred_element_type=jnp.float32
                )
                scores.append(jnp.where(mask[None], score.reshape(ratio, BLOCK, span), -1e30))
            score = jnp.concatenate(scores, axis=0)
            top = jnp.max(score, axis=2, keepdims=True)
            powers = jnp.exp2((score - top) * scale)
            weights = powers * (1.0 / jnp.sum(powers, axis=2, keepdims=True))
            weights = weights.reshape(len(some), ratio * BLOCK, span).astype(jnp.bfloat16)
            for place, (j, here, cos, sin) in enumerate(some):
                prev = jnp.maximum(j - 1, 0)
                region = pl.ds(pl.multiple_of(plan[PROMPT, j] * CTXP, CTXP), CTXP)
                new_value = jnp.concatenate([new_values[prev, :, part], new_values[j, :, part]], axis=0)
                value = jnp.concatenate([prefix_values[region, part], new_value.astype(jnp.bfloat16)], axis=0)
                mixed = jnp.dot(weights[place], value, preferred_element_type=jnp.float32)
                mixed = jnp.where(plan[LIVE, j] > 0, mixed, 0.0)
                for n in range(ratio):
                    first = (h * ratio + n) * HEAD
                    out[j, :, first : first + HEAD] = mixed[n * BLOCK : (n + 1) * BLOCK].astype(
                        jnp.bfloat16
                    )


def cache_kernel(tensors, *rest):
    arrived, out = rest[:tensors], rest[tensors + 1]
    own_tensor = lax.axis_index("tensor")
    width_k = arrived[0].shape[1]
    for distance in range(tensors):
        sender = lax.rem(own_tensor - distance + tensors, tensors)
        at = pl.ds(pl.multiple_of(sender * width_k, HEAD), width_k)
        part = arrived[distance][...].astype(jnp.float32)
        out[:, :, at] = part.reshape(out.shape[0], out.shape[1], width_k).astype(jnp.bfloat16)


def in_hbm(operand):
    return pltpu.with_memory_space_constraint(operand, pltpu.HBM)


def after(arrays, others):
    return pl.pallas_call(
        lambda *refs: None,
        out_shape=[jax.ShapeDtypeStruct(array.shape, array.dtype) for array in arrays],
        in_specs=[ANY] * (len(arrays) + len(others)),
        out_specs=[ANY] * len(arrays),
        input_output_aliases={n: n for n in range(len(arrays))},
        compiler_params=pltpu.CompilerParams(vmem_limit_bytes=VMEM_LIMIT),
        name="hold",
    )(*arrays, *others)


def shifted(chunks, axis):
    size = lax.axis_size(axis)
    return [chunks[0]] + [
        lax.ppermute(chunks[d], axis, [(i, (i + d) % size) for i in range(size)])
        for d in range(1, size)
    ]


def per_device(
    queries,
    keys,
    values,
    prefix_keys,
    prefix_values,
    spread,
    turn,
    new_blocks,
    prefix_len,
    owner,
    page_start,
):
    groups = lax.axis_size("group")
    tensors = lax.axis_size("tensor")
    width_q = queries.shape[1]
    width_k = keys.shape[1]
    heads_q = width_q // HEAD
    heads_k = width_k // HEAD
    slots = queries.shape[0] // BLOCK
    capacity = slots // groups
    prompts = new_blocks.shape[1]
    tokens = BLOCK // tensors
    pages = prompts * MAXP
    cosine, sine = (jnp.asarray(table) for table in rope_table())
    params = pltpu.CompilerParams(vmem_limit_bytes=VMEM_LIMIT)
    blocks_q = queries.reshape(slots, BLOCK, width_q)
    blocks_k = keys.reshape(slots, BLOCK, width_k)
    blocks_v = values.reshape(slots, BLOCK, width_k)

    chunk = jax.ShapeDtypeStruct((capacity, BLOCK, width_q + 2 * width_k), jnp.bfloat16)
    page_chunk = jax.ShapeDtypeStruct((groups, BLOCK, 2 * width_k), jnp.bfloat16)
    sent = pl.pallas_call(
        functools.partial(dispatch_kernel, groups),
        out_shape=[chunk] * groups + [page_chunk] * groups,
        in_specs=[HBM] * 7,
        out_specs=[VMEM] * (2 * groups),
        scratch_shapes=[
            *(pltpu.SMEM(array.shape, jnp.int32) for array in (spread, turn, new_blocks, owner)),
            *(pltpu.VMEM(array.shape, jnp.bfloat16) for array in (blocks_q, blocks_k, blocks_v)),
            pltpu.SMEM((groups * groups + 1,), jnp.int32),
            pltpu.SemaphoreType.DMA((7,)),
        ],
        compiler_params=params,
        name="dispatch",
    )(
        *(
            in_hbm(operand)
            for operand in (spread, turn, new_blocks, owner, blocks_q, blocks_k, blocks_v)
        )
    )
    handed = shifted(sent[groups:], "group")
    arrived = shifted([sent[0], *after(sent[1:groups], handed[1:])], "group")

    part = jax.ShapeDtypeStruct((pages * 2 * tokens, width_k), jnp.bfloat16)
    *finished, plan = pl.pallas_call(
        functools.partial(pages_kernel, groups, tensors),
        out_shape=[part] * tensors + [jax.ShapeDtypeStruct((7, max(slots, groups) + 1), jnp.int32)],
        in_specs=[SMEM] * 5 + [VMEM] * (2 + groups),
        out_specs=[VMEM] * tensors + [SMEM],
        compiler_params=params,
        scratch_shapes=[
            pltpu.VMEM((groups * groups, BLOCK, 2 * width_k), jnp.bfloat16),
            pltpu.VMEM((2 * pages * BLOCK, width_k), jnp.float32),
        ],
        name="finish_pages",
    )(spread, new_blocks, prefix_len, owner, page_start, cosine, sine, *handed)
    parts = shifted(finished, "tensor")

    attention = pl.pallas_call(
        functools.partial(attention_kernel, groups, heads_q, heads_k),
        out_shape=jax.ShapeDtypeStruct((slots, BLOCK, width_q), jnp.bfloat16),
        in_specs=[SMEM] + [VMEM] * (4 + groups),
        out_specs=VMEM,
        scratch_shapes=[pltpu.VMEM((slots, BLOCK, width_k), jnp.float32)] * 2,
        compiler_params=params,
        name="attention",
    )(plan, prefix_keys, prefix_values, cosine, sine, *arrived)

    cache = pl.pallas_call(
        functools.partial(cache_kernel, tensors),
        out_shape=jax.ShapeDtypeStruct((pages * 2, tokens, tensors * width_k), jnp.bfloat16),
        in_specs=[VMEM] * tensors + [ANY],
        out_specs=VMEM,
        compiler_params=params,
        name="place_pages",
    )(*parts, in_hbm(attention))
    return (
        attention.reshape(slots * BLOCK, width_q),
        cache.reshape(pages, 2, tokens, tensors * width_k),
    )


def solution(mesh):
    return jax.shard_map(
        per_device,
        mesh=mesh,
        in_specs=(
            P(("parts", "group"), "tensor"),
            P(("parts", "group"), "tensor"),
            P(("parts", "group"), "tensor"),
            P(("parts", "group"), "tensor"),
            P(("parts", "group"), "tensor"),
            P("parts"),
            P("parts"),
            P("parts", None),
            P("parts", None),
            P("parts", None),
            P("parts", None),
        ),
        out_specs=(P(("parts", "group"), "tensor"), P(("parts", "group"), None, "tensor", None)),
        check_vma=False,
    )
```

```python
import functools
import math

import jax
import jax.numpy as jnp
import numpy as np
from jax import lax
from jax.experimental import pallas as pl
from jax.experimental.pallas import tpu as pltpu
from jax.sharding import PartitionSpec as P

HEAD = 128
BLOCK = 8
MAXP = 2
CTXP = 64

VMEM_LIMIT = 24 * 1024 * 1024

SMEM = pl.BlockSpec(memory_space=pltpu.SMEM)
VMEM = pl.BlockSpec(memory_space=pltpu.VMEM)
PROMPT, OFFSET, LIVE, CACHED, SOURCE, COLUMN, PLACE = range(7)
ANY = pl.BlockSpec(memory_space=pl.ANY)
HBM = pl.BlockSpec(memory_space=pltpu.HBM)


def rope_table():
    count = CTXP + MAXP * BLOCK
    half = HEAD // 2
    frequency = np.exp(np.arange(half) * (-2.0 * math.log(500000.0) / HEAD))
    angles = np.arange(count)[:, None] * frequency[None, :]
    cosine, sine = np.cos(angles), np.sin(angles)
    return (
        np.concatenate([cosine, cosine], axis=1).astype(np.float32),
        np.concatenate([-sine, sine], axis=1).astype(np.float32),
    )


def loop(count, body, unrolled=16):
    if count <= unrolled:
        for index in range(count):
            body(index)
    else:
        lax.fori_loop(0, count, lambda index, carry: (body(index), carry)[1], 0)


def turned(head_block, cosine, sine):
    return head_block * cosine + pltpu.roll(head_block, HEAD // 2, 1) * sine


def dispatch_kernel(
    groups, spread_in, turn_in, new_blocks_in, owner_in, queries_in, keys_in, values_in, *rest
):
    outs, handed, rest = rest[:groups], rest[groups], rest[groups + 1 :]
    spread, turn, new_blocks, owner, queries, keys, values, table, sem = rest
    own = lax.axis_index("group")
    slots, _, width_q = queries.shape
    width_k = keys.shape[2]
    capacity = slots // groups
    prompts = new_blocks.shape[1]
    copies = [
        pltpu.make_async_copy(source, target, sem.at[n])
        for n, (source, target) in enumerate(
            (
                (spread_in, spread),
                (turn_in, turn),
                (new_blocks_in, new_blocks),
                (owner_in, owner),
                (keys_in, keys),
                (values_in, values),
                (queries_in, queries),
            )
        )
    ]
    for copy in copies:
        copy.start()
    for copy in copies[:4]:
        copy.wait()

    def clear(n):
        table[n] = 0

    loop(groups * groups, clear)

    def column(c):
        target = lax.rem(own - spread[c] + groups, groups)

        def find(p, carry):
            start, holders = carry
            blocks = new_blocks[target, p]
            holders = [
                jnp.where((c + groups * n >= start) & (c + groups * n < start + blocks), owner[target, p], holder)
                for n, holder in enumerate(holders)
            ]
            return start + blocks, holders

        carry = (jnp.int32(0), [jnp.int32(-1)] * capacity)
        if prompts <= 8:
            for p in range(prompts):
                carry = find(p, carry)
        else:
            carry = lax.fori_loop(0, prompts, find, carry)
        for n, holder in enumerate(carry[1]):
            at = jnp.where(holder >= 0, holder * groups + target, groups * groups)
            table[at] = lax.rem(c + groups * n + turn[own], slots)

    loop(groups, column)
    for copy in copies[4:]:
        copy.wait()
    for distance in range(groups):
        first_slot = column_of(spread, groups, distance) + turn[own]
        out = outs[distance]
        for step in range(capacity):
            source = lax.rem(first_slot + groups * step, slots)
            out[step, :, :width_q] = queries[source]
            out[step, :, width_q : width_q + width_k] = keys[source]
            out[step, :, width_q + width_k :] = values[source]

    def page(n):
        handed[n, :, :width_k] = keys[table[n]]
        handed[n, :, width_k:] = values[table[n]]

    loop(groups * groups, page)


def column_of(spread, groups, distance):
    wanted = (groups - distance) % groups
    if groups <= 8:
        return sum(jnp.where(spread[c] == wanted, c, 0) for c in range(groups))
    return lax.fori_loop(
        0, groups, lambda c, found: jnp.where(spread[c] == wanted, c, found), jnp.int32(0)
    )


def make_plan(groups, own, spread, new_blocks, prefix_len, owner, page_start, plan):
    prompts = new_blocks.shape[1]
    slots = prompts * MAXP

    def clear(j):
        plan[PROMPT, j] = 0
        plan[OFFSET, j] = 0
        plan[LIVE, j] = 0
        plan[CACHED, j] = 0

    loop(slots, clear)

    def one(p, start):
        blocks = new_blocks[own, p]
        cached = prefix_len[own, p]
        for step in range(MAXP):
            at = jnp.where(step < blocks, start + step, slots)
            plan[PROMPT, at] = p
            plan[OFFSET, at] = cached + step * BLOCK
            plan[LIVE, at] = 1 + step
            plan[CACHED, at] = cached
        return start + blocks

    start = jnp.int32(0)
    if prompts <= 8:
        for p in range(prompts):
            start = one(p, start)
    else:
        lax.fori_loop(0, prompts, one, start)

    def of_group(g):
        def one(p, start):
            blocks = new_blocks[g, p]
            mine = owner[g, p] == own
            for step in range(MAXP):
                root = lax.rem(g + spread[lax.rem(start + step, groups)], groups)
                at = jnp.where(mine, page_start[g, p] + step, slots)
                plan[SOURCE, at] = jnp.where(step < blocks, root * groups + g, -1)
                plan[PLACE, at] = prefix_len[g, p] + step * BLOCK
            return start + blocks

        start = jnp.int32(0)
        if prompts <= 8:
            for p in range(prompts):
                start = one(p, start)
        else:
            lax.fori_loop(0, prompts, one, start)

    loop(groups, of_group)
    for distance in range(groups):
        plan[COLUMN, distance] = column_of(spread, groups, distance)


def pages_kernel(
    groups, tensors, spread, new_blocks, prefix_len, owner, page_start, cosine, sine, blocks, *rest
):
    outs, (plan, rows) = rest[:tensors], rest[tensors:]
    own = lax.axis_index("group")
    own_tensor = lax.axis_index("tensor")
    pages = new_blocks.shape[1] * MAXP
    width_k = rows.shape[1]
    tokens = BLOCK // tensors
    make_plan(groups, own, spread, new_blocks, prefix_len, owner, page_start, plan)

    def assemble(page):
        source = plan[SOURCE, page]
        place = plan[PLACE, page]
        block = blocks[jnp.maximum(source, 0)].astype(jnp.float32)
        block = jnp.where(source >= 0, block, 0.0)
        cos = cosine[pl.ds(place, BLOCK), :]
        sin = sine[pl.ds(place, BLOCK), :]
        for first in range(0, width_k, HEAD):
            part = slice(first, first + HEAD)
            rows[pl.ds(pl.multiple_of(page * BLOCK, BLOCK), BLOCK), part] = turned(
                block[:, part], cos, sin
            )
        rows[pl.ds(pl.multiple_of((pages + page) * BLOCK, BLOCK), BLOCK), :] = block[:, width_k:]

    loop(pages, assemble)
    size = pages * 2 * tokens
    shape = (tensors * size, 2 * pages * BLOCK)
    row = lax.broadcasted_iota(jnp.int32, shape, 0)
    col = lax.broadcasted_iota(jnp.int32, shape, 1)
    share = lax.rem(row // size + own_tensor, tensors)
    kind, page = (row // tokens) % 2, (row // (2 * tokens)) % pages
    wanted = (kind * pages + page) * BLOCK + share * tokens + row % tokens
    pick = (col == wanted).astype(jnp.float32).astype(jnp.bfloat16)
    moved = jnp.dot(pick, rows[...].astype(jnp.bfloat16), preferred_element_type=jnp.float32)
    moved = moved.astype(jnp.bfloat16)
    for distance in range(tensors):
        outs[distance][...] = moved[distance * size : (distance + 1) * size]


def attention_kernel(groups, heads_q, heads_k, plan, prefix_keys, prefix_values, cosine, sine, *rest):
    arrived, (out, new_keys, new_values) = rest[:groups], rest[groups:]
    slots = out.shape[0]
    capacity = slots // groups
    ratio = heads_q // heads_k
    width_q = heads_q * HEAD
    width_k = heads_k * HEAD
    scale = math.log2(math.e) / math.sqrt(HEAD)
    span = CTXP + 2 * BLOCK
    lane = lax.broadcasted_iota(jnp.int32, (BLOCK, span), 1)
    token = lax.broadcasted_iota(jnp.int32, (BLOCK, span), 0)
    fresh = (lane >= CTXP + BLOCK) & (lane - (CTXP + BLOCK) <= token)
    before = (lane >= CTXP) & (lane < CTXP + BLOCK)

    blocks = []
    for distance in range(groups):
        first_slot = plan[COLUMN, distance]
        for step in range(capacity):
            j = first_slot + groups * step
            here = arrived[distance].at[step]
            cos = cosine[pl.ds(plan[OFFSET, j], BLOCK), :]
            sin = sine[pl.ds(plan[OFFSET, j], BLOCK), :]
            new_keys[j] = jnp.concatenate(
                [
                    turned(here[:, first : first + HEAD].astype(jnp.float32), cos, sin)
                    for first in range(width_q, width_q + width_k, HEAD)
                ],
                axis=1,
            )
            new_values[j] = here[:, width_q + width_k :].astype(jnp.float32)
            blocks.append((j, here, cos, sin))

    for at in range(0, len(blocks), 8):
        some = blocks[at : at + 8]
        for h in range(heads_k):
            part = slice(h * HEAD, (h + 1) * HEAD)
            scores = []
            for j, here, cos, sin in some:
                prev = jnp.maximum(j - 1, 0)
                region = pl.ds(pl.multiple_of(plan[PROMPT, j] * CTXP, CTXP), CTXP)
                mask = fresh | (lane < plan[CACHED, j]) & (lane < CTXP) | before & (plan[LIVE, j] == 2)
                new_key = jnp.concatenate([new_keys[prev, :, part], new_keys[j, :, part]], axis=0)
                key = jnp.concatenate([prefix_keys[region, part], new_key.astype(jnp.bfloat16)], axis=0)
                query = jnp.concatenate(
                    [
                        turned(here[:, n * HEAD : (n + 1) * HEAD].astype(jnp.float32), cos, sin)
                        for n in range(h * ratio, (h + 1) * ratio)
                    ],
                    axis=0,
                ).astype(jnp.bfloat16)
                score = lax.dot_general(
                    query, key, (((1,), (1,)), ((), ())), preferred_element_type=jnp.float32
                )
                scores.append(jnp.where(mask[None], score.reshape(ratio, BLOCK, span), -1e30))
            score = jnp.concatenate(scores, axis=0)
            top = jnp.max(score, axis=2, keepdims=True)
            powers = jnp.exp2((score - top) * scale)
            weights = powers * (1.0 / jnp.sum(powers, axis=2, keepdims=True))
            weights = weights.reshape(len(some), ratio * BLOCK, span).astype(jnp.bfloat16)
            for place, (j, here, cos, sin) in enumerate(some):
                prev = jnp.maximum(j - 1, 0)
                region = pl.ds(pl.multiple_of(plan[PROMPT, j] * CTXP, CTXP), CTXP)
                new_value = jnp.concatenate([new_values[prev, :, part], new_values[j, :, part]], axis=0)
                value = jnp.concatenate([prefix_values[region, part], new_value.astype(jnp.bfloat16)], axis=0)
                mixed = jnp.dot(weights[place], value, preferred_element_type=jnp.float32)
                mixed = jnp.where(plan[LIVE, j] > 0, mixed, 0.0)
                for n in range(ratio):
                    first = (h * ratio + n) * HEAD
                    out[j, :, first : first + HEAD] = mixed[n * BLOCK : (n + 1) * BLOCK].astype(
                        jnp.bfloat16
                    )


def cache_kernel(tensors, *rest):
    arrived, out = rest[:tensors], rest[tensors + 1]
    own_tensor = lax.axis_index("tensor")
    width_k = arrived[0].shape[1]
    for distance in range(tensors):
        sender = lax.rem(own_tensor - distance + tensors, tensors)
        at = pl.ds(pl.multiple_of(sender * width_k, HEAD), width_k)
        part = arrived[distance][...].astype(jnp.float32)
        out[:, :, at] = part.reshape(out.shape[0], out.shape[1], width_k).astype(jnp.bfloat16)


def in_hbm(operand):
    return pltpu.with_memory_space_constraint(operand, pltpu.HBM)


def shifted(chunks, axis):
    size = lax.axis_size(axis)
    return [chunks[0]] + [
        lax.ppermute(chunks[d], axis, [(i, (i + d) % size) for i in range(size)])
        for d in range(1, size)
    ]


def per_device(
    queries,
    keys,
    values,
    prefix_keys,
    prefix_values,
    spread,
    turn,
    new_blocks,
    prefix_len,
    owner,
    page_start,
):
    groups = lax.axis_size("group")
    tensors = lax.axis_size("tensor")
    width_q = queries.shape[1]
    width_k = keys.shape[1]
    heads_q = width_q // HEAD
    heads_k = width_k // HEAD
    slots = queries.shape[0] // BLOCK
    capacity = slots // groups
    prompts = new_blocks.shape[1]
    tokens = BLOCK // tensors
    pages = prompts * MAXP
    cosine, sine = (jnp.asarray(table) for table in rope_table())
    params = pltpu.CompilerParams(vmem_limit_bytes=VMEM_LIMIT)
    blocks_q = queries.reshape(slots, BLOCK, width_q)
    blocks_k = keys.reshape(slots, BLOCK, width_k)
    blocks_v = values.reshape(slots, BLOCK, width_k)

    chunk = jax.ShapeDtypeStruct((capacity, BLOCK, width_q + 2 * width_k), jnp.bfloat16)
    page_chunk = jax.ShapeDtypeStruct((groups * groups, BLOCK, 2 * width_k), jnp.bfloat16)
    sent = pl.pallas_call(
        functools.partial(dispatch_kernel, groups),
        out_shape=[chunk] * groups + [page_chunk],
        in_specs=[HBM] * 7,
        out_specs=[VMEM] * (groups + 1),
        scratch_shapes=[
            *(pltpu.SMEM(array.shape, jnp.int32) for array in (spread, turn, new_blocks, owner)),
            *(pltpu.VMEM(array.shape, jnp.bfloat16) for array in (blocks_q, blocks_k, blocks_v)),
            pltpu.SMEM((groups * groups + 1,), jnp.int32),
            pltpu.SemaphoreType.DMA((7,)),
        ],
        compiler_params=params,
        name="dispatch",
    )(
        *(
            in_hbm(operand)
            for operand in (spread, turn, new_blocks, owner, blocks_q, blocks_k, blocks_v)
        )
    )
    arrived = shifted(sent[:groups], "group")
    handed = lax.all_to_all(sent[groups], "group", split_axis=0, concat_axis=0, tiled=True)

    part = jax.ShapeDtypeStruct((pages * 2 * tokens, width_k), jnp.bfloat16)
    *finished, plan = pl.pallas_call(
        functools.partial(pages_kernel, groups, tensors),
        out_shape=[part] * tensors + [jax.ShapeDtypeStruct((7, max(slots, groups) + 1), jnp.int32)],
        in_specs=[SMEM] * 5 + [VMEM] * 3,
        out_specs=[VMEM] * tensors + [SMEM],
        compiler_params=params,
        scratch_shapes=[
            pltpu.VMEM((2 * pages * BLOCK, width_k), jnp.float32),
        ],
        name="finish_pages",
    )(spread, new_blocks, prefix_len, owner, page_start, cosine, sine, handed)
    parts = shifted(finished, "tensor")

    attention = pl.pallas_call(
        functools.partial(attention_kernel, groups, heads_q, heads_k),
        out_shape=jax.ShapeDtypeStruct((slots, BLOCK, width_q), jnp.bfloat16),
        in_specs=[SMEM] + [VMEM] * (4 + groups),
        out_specs=VMEM,
        scratch_shapes=[pltpu.VMEM((slots, BLOCK, width_k), jnp.float32)] * 2,
        compiler_params=params,
        name="attention",
    )(plan, prefix_keys, prefix_values, cosine, sine, *arrived)

    cache = pl.pallas_call(
        functools.partial(cache_kernel, tensors),
        out_shape=jax.ShapeDtypeStruct((pages * 2, tokens, tensors * width_k), jnp.bfloat16),
        in_specs=[VMEM] * tensors + [ANY],
        out_specs=VMEM,
        compiler_params=params,
        name="place_pages",
    )(*parts, in_hbm(attention))
    return (
        attention.reshape(slots * BLOCK, width_q),
        cache.reshape(pages, 2, tokens, tensors * width_k),
    )


def solution(mesh):
    return jax.shard_map(
        per_device,
        mesh=mesh,
        in_specs=(
            P(("parts", "group"), "tensor"),
            P(("parts", "group"), "tensor"),
            P(("parts", "group"), "tensor"),
            P(("parts", "group"), "tensor"),
            P(("parts", "group"), "tensor"),
            P("parts"),
            P("parts"),
            P("parts", None),
            P("parts", None),
            P("parts", None),
            P("parts", None),
        ),
        out_specs=(P(("parts", "group"), "tensor"), P(("parts", "group"), None, "tensor", None)),
        check_vma=False,
    )
```

```python
import functools
import math

import jax
import jax.numpy as jnp
import numpy as np
from jax import lax
from jax.experimental import pallas as pl
from jax.experimental.pallas import tpu as pltpu
from jax.sharding import PartitionSpec as P

HEAD = 128
BLOCK = 8
MAXP = 2
CTXP = 64

VMEM_LIMIT = 24 * 1024 * 1024

SMEM = pl.BlockSpec(memory_space=pltpu.SMEM)
VMEM = pl.BlockSpec(memory_space=pltpu.VMEM)
JOINED = 1
PROMPT, OFFSET, LIVE, CACHED, SOURCE, COLUMN, PLACE = range(7)
ANY = pl.BlockSpec(memory_space=pl.ANY)
HBM = pl.BlockSpec(memory_space=pltpu.HBM)


def rope_table():
    count = CTXP + MAXP * BLOCK
    half = HEAD // 2
    frequency = np.exp(np.arange(half) * (-2.0 * math.log(500000.0) / HEAD))
    angles = np.arange(count)[:, None] * frequency[None, :]
    cosine, sine = np.cos(angles), np.sin(angles)
    return (
        np.concatenate([cosine, cosine], axis=1).astype(np.float32),
        np.concatenate([-sine, sine], axis=1).astype(np.float32),
    )


def loop(count, body, unrolled=16):
    if count <= unrolled:
        for index in range(count):
            body(index)
    else:
        lax.fori_loop(0, count, lambda index, carry: (body(index), carry)[1], 0)


def turned(head_block, cosine, sine):
    return head_block * cosine + pltpu.roll(head_block, HEAD // 2, 1) * sine


def dispatch_kernel(
    groups, spread_in, turn_in, new_blocks_in, owner_in, queries_in, keys_in, values_in, *rest
):
    outs, handed, rest = rest[:groups], list(rest[groups : 2 * groups - 1]), rest[2 * groups - 1 :]
    handed.insert(JOINED, None)
    spread, turn, new_blocks, owner, queries, keys, values, table, sem = rest
    own = lax.axis_index("group")
    slots, _, width_q = queries.shape
    width_k = keys.shape[2]
    capacity = slots // groups
    prompts = new_blocks.shape[1]
    copies = [
        pltpu.make_async_copy(source, target, sem.at[n])
        for n, (source, target) in enumerate(
            (
                (spread_in, spread),
                (turn_in, turn),
                (new_blocks_in, new_blocks),
                (owner_in, owner),
                (keys_in, keys),
                (values_in, values),
                (queries_in, queries),
            )
        )
    ]
    for copy in copies:
        copy.start()
    for copy in copies[:4]:
        copy.wait()

    def clear(n):
        table[n] = 0

    loop(groups * groups, clear)

    def column(c):
        target = lax.rem(own - spread[c] + groups, groups)

        def find(p, carry):
            start, holders = carry
            blocks = new_blocks[target, p]
            holders = [
                jnp.where((c + groups * n >= start) & (c + groups * n < start + blocks), owner[target, p], holder)
                for n, holder in enumerate(holders)
            ]
            return start + blocks, holders

        carry = (jnp.int32(0), [jnp.int32(-1)] * capacity)
        if prompts <= 8:
            for p in range(prompts):
                carry = find(p, carry)
        else:
            carry = lax.fori_loop(0, prompts, find, carry)
        for n, holder in enumerate(carry[1]):
            at = lax.rem(holder - own + groups, groups) * groups + target
            table[jnp.where(holder >= 0, at, groups * groups)] = lax.rem(c + groups * n + turn[own], slots)

    loop(groups, column)
    for copy in copies[4:]:
        copy.wait()
    for distance in range(groups):
        first_slot = column_of(spread, groups, distance) + turn[own]
        out = outs[distance]
        wide = 2 * width_k
        per_slot = width_q // wide + 1
        for step in range(capacity):
            source = lax.rem(first_slot + groups * step, slots)
            for n in range(per_slot - 1):
                out[step * per_slot + n] = queries[source, :, n * wide : (n + 1) * wide]
            last = step * per_slot + per_slot - 1
            out[last, :, :width_k] = keys[source]
            out[last, :, width_k:] = values[source]
        target, base = (out, capacity * per_slot) if distance == JOINED else (handed[distance], 0)

        def page(g):
            source = table[distance * groups + g]
            target[base + g, :, :width_k] = keys[source]
            target[base + g, :, width_k:] = values[source]

        loop(groups, page)


def column_of(spread, groups, distance):
    wanted = (groups - distance) % groups
    if groups <= 8:
        return sum(jnp.where(spread[c] == wanted, c, 0) for c in range(groups))
    return lax.fori_loop(
        0, groups, lambda c, found: jnp.where(spread[c] == wanted, c, found), jnp.int32(0)
    )


def make_plan(groups, own, spread, new_blocks, prefix_len, owner, page_start, plan):
    prompts = new_blocks.shape[1]
    slots = prompts * MAXP

    def clear(j):
        plan[PROMPT, j] = 0
        plan[OFFSET, j] = 0
        plan[LIVE, j] = 0
        plan[CACHED, j] = 0

    loop(slots, clear)

    def one(p, start):
        blocks = new_blocks[own, p]
        cached = prefix_len[own, p]
        for step in range(MAXP):
            at = jnp.where(step < blocks, start + step, slots)
            plan[PROMPT, at] = p
            plan[OFFSET, at] = cached + step * BLOCK
            plan[LIVE, at] = 1 + step
            plan[CACHED, at] = cached
        return start + blocks

    start = jnp.int32(0)
    if prompts <= 8:
        for p in range(prompts):
            start = one(p, start)
    else:
        lax.fori_loop(0, prompts, one, start)

    def of_group(g):
        def one(p, start):
            blocks = new_blocks[g, p]
            mine = owner[g, p] == own
            for step in range(MAXP):
                root = lax.rem(g + spread[lax.rem(start + step, groups)], groups)
                at = jnp.where(mine, page_start[g, p] + step, slots)
                away = lax.rem(own - root + groups, groups)
                plan[SOURCE, at] = jnp.where(step < blocks, away * groups + g, -1)
                plan[PLACE, at] = prefix_len[g, p] + step * BLOCK
            return start + blocks

        start = jnp.int32(0)
        if prompts <= 8:
            for p in range(prompts):
                start = one(p, start)
        else:
            lax.fori_loop(0, prompts, one, start)

    loop(groups, of_group)
    for distance in range(groups):
        plan[COLUMN, distance] = column_of(spread, groups, distance)


def pages_kernel(
    groups, tensors, spread, new_blocks, prefix_len, owner, page_start, cosine, sine, *rest
):
    chunks, rest = rest[:groups], rest[groups:]
    outs, (plan, blocks, rows) = rest[:tensors], rest[tensors:]
    own = lax.axis_index("group")
    own_tensor = lax.axis_index("tensor")
    pages = new_blocks.shape[1] * MAXP
    width_k = rows.shape[1]
    tokens = BLOCK // tensors
    for distance in range(groups):
        first = chunks[distance].shape[0] - groups
        blocks[distance * groups : (distance + 1) * groups] = chunks[distance][first:]
    make_plan(groups, own, spread, new_blocks, prefix_len, owner, page_start, plan)

    def assemble(page):
        source = plan[SOURCE, page]
        place = plan[PLACE, page]
        block = blocks[jnp.maximum(source, 0)].astype(jnp.float32)
        block = jnp.where(source >= 0, block, 0.0)
        cos = cosine[pl.ds(place, BLOCK), :]
        sin = sine[pl.ds(place, BLOCK), :]
        for first in range(0, width_k, HEAD):
            part = slice(first, first + HEAD)
            rows[pl.ds(pl.multiple_of(page * BLOCK, BLOCK), BLOCK), part] = turned(
                block[:, part], cos, sin
            )
        rows[pl.ds(pl.multiple_of((pages + page) * BLOCK, BLOCK), BLOCK), :] = block[:, width_k:]

    loop(pages, assemble)
    size = pages * 2 * tokens
    shape = (tensors * size, 2 * pages * BLOCK)
    row = lax.broadcasted_iota(jnp.int32, shape, 0)
    col = lax.broadcasted_iota(jnp.int32, shape, 1)
    share = lax.rem(row // size + own_tensor, tensors)
    kind, page = (row // tokens) % 2, (row // (2 * tokens)) % pages
    wanted = (kind * pages + page) * BLOCK + share * tokens + row % tokens
    pick = (col == wanted).astype(jnp.float32).astype(jnp.bfloat16)
    moved = jnp.dot(pick, rows[...].astype(jnp.bfloat16), preferred_element_type=jnp.float32)
    moved = moved.astype(jnp.bfloat16)
    for distance in range(tensors):
        outs[distance][...] = moved[distance * size : (distance + 1) * size]


def columns(chunk, step, width_q, first, width):
    wide = chunk.shape[2]
    row = step * (width_q // wide + 1) + first // wide
    return chunk[row, :, first % wide : first % wide + width]


def attention_kernel(groups, heads_q, heads_k, plan, prefix_keys, prefix_values, cosine, sine, *rest):
    arrived, (out, new_keys, new_values) = rest[:groups], rest[groups:]
    slots = out.shape[0]
    capacity = slots // groups
    ratio = heads_q // heads_k
    width_q = heads_q * HEAD
    width_k = heads_k * HEAD
    scale = math.log2(math.e) / math.sqrt(HEAD)
    span = CTXP + 2 * BLOCK
    lane = lax.broadcasted_iota(jnp.int32, (BLOCK, span), 1)
    token = lax.broadcasted_iota(jnp.int32, (BLOCK, span), 0)
    fresh = (lane >= CTXP + BLOCK) & (lane - (CTXP + BLOCK) <= token)
    before = (lane >= CTXP) & (lane < CTXP + BLOCK)

    blocks = []
    for distance in range(groups):
        first_slot = plan[COLUMN, distance]
        for step in range(capacity):
            j = first_slot + groups * step
            here = functools.partial(columns, arrived[distance], step, width_q)
            cos = cosine[pl.ds(plan[OFFSET, j], BLOCK), :]
            sin = sine[pl.ds(plan[OFFSET, j], BLOCK), :]
            new_keys[j] = jnp.concatenate(
                [
                    turned(here(first, HEAD).astype(jnp.float32), cos, sin)
                    for first in range(width_q, width_q + width_k, HEAD)
                ],
                axis=1,
            )
            new_values[j] = here(width_q + width_k, width_k).astype(jnp.float32)
            blocks.append((j, here, cos, sin))

    for at in range(0, len(blocks), 8):
        some = blocks[at : at + 8]
        for h in range(heads_k):
            part = slice(h * HEAD, (h + 1) * HEAD)
            scores = []
            for j, here, cos, sin in some:
                prev = jnp.maximum(j - 1, 0)
                region = pl.ds(pl.multiple_of(plan[PROMPT, j] * CTXP, CTXP), CTXP)
                mask = fresh | (lane < plan[CACHED, j]) & (lane < CTXP) | before & (plan[LIVE, j] == 2)
                new_key = jnp.concatenate([new_keys[prev, :, part], new_keys[j, :, part]], axis=0)
                key = jnp.concatenate([prefix_keys[region, part], new_key.astype(jnp.bfloat16)], axis=0)
                query = jnp.concatenate(
                    [
                        turned(here(n * HEAD, HEAD).astype(jnp.float32), cos, sin)
                        for n in range(h * ratio, (h + 1) * ratio)
                    ],
                    axis=0,
                ).astype(jnp.bfloat16)
                score = lax.dot_general(
                    query, key, (((1,), (1,)), ((), ())), preferred_element_type=jnp.float32
                )
                scores.append(jnp.where(mask[None], score.reshape(ratio, BLOCK, span), -1e30))
            score = jnp.concatenate(scores, axis=0)
            top = jnp.max(score, axis=2, keepdims=True)
            powers = jnp.exp2((score - top) * scale)
            weights = powers * (1.0 / jnp.sum(powers, axis=2, keepdims=True))
            weights = weights.reshape(len(some), ratio * BLOCK, span).astype(jnp.bfloat16)
            for place, (j, here, cos, sin) in enumerate(some):
                prev = jnp.maximum(j - 1, 0)
                region = pl.ds(pl.multiple_of(plan[PROMPT, j] * CTXP, CTXP), CTXP)
                new_value = jnp.concatenate([new_values[prev, :, part], new_values[j, :, part]], axis=0)
                value = jnp.concatenate([prefix_values[region, part], new_value.astype(jnp.bfloat16)], axis=0)
                mixed = jnp.dot(weights[place], value, preferred_element_type=jnp.float32)
                mixed = jnp.where(plan[LIVE, j] > 0, mixed, 0.0)
                for n in range(ratio):
                    first = (h * ratio + n) * HEAD
                    out[j, :, first : first + HEAD] = mixed[n * BLOCK : (n + 1) * BLOCK].astype(
                        jnp.bfloat16
                    )


def cache_kernel(tensors, *rest):
    arrived, out = rest[:tensors], rest[tensors + 1]
    own_tensor = lax.axis_index("tensor")
    width_k = arrived[0].shape[1]
    for distance in range(tensors):
        sender = lax.rem(own_tensor - distance + tensors, tensors)
        at = pl.ds(pl.multiple_of(sender * width_k, HEAD), width_k)
        part = arrived[distance][...].astype(jnp.float32)
        out[:, :, at] = part.reshape(out.shape[0], out.shape[1], width_k).astype(jnp.bfloat16)


def in_hbm(operand):
    return pltpu.with_memory_space_constraint(operand, pltpu.HBM)


def after(arrays, others):
    return pl.pallas_call(
        lambda *refs: None,
        out_shape=[jax.ShapeDtypeStruct(array.shape, array.dtype) for array in arrays],
        in_specs=[ANY] * (len(arrays) + len(others)),
        out_specs=[ANY] * len(arrays),
        input_output_aliases={n: n for n in range(len(arrays))},
        compiler_params=pltpu.CompilerParams(vmem_limit_bytes=VMEM_LIMIT),
        name="hold",
    )(*arrays, *others)


def shifted(chunks, axis):
    size = lax.axis_size(axis)
    return [chunks[0]] + [
        chunks[d] is not None
        and lax.ppermute(chunks[d], axis, [(i, (i + d) % size) for i in range(size)])
        for d in range(1, size)
    ]


def per_device(
    queries,
    keys,
    values,
    prefix_keys,
    prefix_values,
    spread,
    turn,
    new_blocks,
    prefix_len,
    owner,
    page_start,
):
    groups = lax.axis_size("group")
    tensors = lax.axis_size("tensor")
    width_q = queries.shape[1]
    width_k = keys.shape[1]
    heads_q = width_q // HEAD
    heads_k = width_k // HEAD
    slots = queries.shape[0] // BLOCK
    capacity = slots // groups
    prompts = new_blocks.shape[1]
    tokens = BLOCK // tensors
    pages = prompts * MAXP
    cosine, sine = (jnp.asarray(table) for table in rope_table())
    params = pltpu.CompilerParams(vmem_limit_bytes=VMEM_LIMIT)
    blocks_q = queries.reshape(slots, BLOCK, width_q)
    blocks_k = keys.reshape(slots, BLOCK, width_k)
    blocks_v = values.reshape(slots, BLOCK, width_k)

    wide = 2 * width_k
    chunk_rows = capacity * (width_q // wide + 1)

    def chunk(rows):
        return jax.ShapeDtypeStruct((rows, BLOCK, wide), jnp.bfloat16)

    sent = pl.pallas_call(
        functools.partial(dispatch_kernel, groups),
        out_shape=[
            chunk(chunk_rows + (groups if distance == JOINED else 0)) for distance in range(groups)
        ]
        + [chunk(groups)] * (groups - 1),
        in_specs=[HBM] * 7,
        out_specs=[VMEM] * (2 * groups - 1),
        scratch_shapes=[
            *(pltpu.SMEM(array.shape, jnp.int32) for array in (spread, turn, new_blocks, owner)),
            *(pltpu.VMEM(array.shape, jnp.bfloat16) for array in (blocks_q, blocks_k, blocks_v)),
            pltpu.SMEM((groups * groups + 1,), jnp.int32),
            pltpu.SemaphoreType.DMA((7,)),
        ],
        compiler_params=params,
        name="dispatch",
    )(
        *(
            in_hbm(operand)
            for operand in (spread, turn, new_blocks, owner, blocks_q, blocks_k, blocks_v)
        )
    )
    own, pages_only = list(sent[:groups]), list(sent[groups:])
    pages_only.insert(JOINED, own[JOINED])
    handed = shifted(pages_only, "group")
    later = [distance for distance in range(1, groups) if distance != JOINED]
    held = dict(zip(later, after([own[distance] for distance in later], handed[1:])))
    moved = shifted([own[0]] + [held.get(distance) for distance in range(1, groups)], "group")
    arrived = [handed[n] if n == JOINED else moved[n] for n in range(groups)]

    part = jax.ShapeDtypeStruct((pages * 2 * tokens, width_k), jnp.bfloat16)
    *finished, plan = pl.pallas_call(
        functools.partial(pages_kernel, groups, tensors),
        out_shape=[part] * tensors + [jax.ShapeDtypeStruct((7, max(slots, groups) + 1), jnp.int32)],
        in_specs=[SMEM] * 5 + [VMEM] * (2 + groups),
        out_specs=[VMEM] * tensors + [SMEM],
        compiler_params=params,
        scratch_shapes=[
            pltpu.VMEM((groups * groups, BLOCK, 2 * width_k), jnp.bfloat16),
            pltpu.VMEM((2 * pages * BLOCK, width_k), jnp.float32),
        ],
        name="finish_pages",
    )(spread, new_blocks, prefix_len, owner, page_start, cosine, sine, *handed)
    parts = shifted(finished, "tensor")

    attention = pl.pallas_call(
        functools.partial(attention_kernel, groups, heads_q, heads_k),
        out_shape=jax.ShapeDtypeStruct((slots, BLOCK, width_q), jnp.bfloat16),
        in_specs=[SMEM] + [VMEM] * (4 + groups),
        out_specs=VMEM,
        scratch_shapes=[pltpu.VMEM((slots, BLOCK, width_k), jnp.float32)] * 2,
        compiler_params=params,
        name="attention",
    )(plan, prefix_keys, prefix_values, cosine, sine, *arrived)

    cache = pl.pallas_call(
        functools.partial(cache_kernel, tensors),
        out_shape=jax.ShapeDtypeStruct((pages * 2, tokens, tensors * width_k), jnp.bfloat16),
        in_specs=[VMEM] * tensors + [ANY],
        out_specs=VMEM,
        compiler_params=params,
        name="place_pages",
    )(*parts, in_hbm(attention))
    return (
        attention.reshape(slots * BLOCK, width_q),
        cache.reshape(pages, 2, tokens, tensors * width_k),
    )


def solution(mesh):
    return jax.shard_map(
        per_device,
        mesh=mesh,
        in_specs=(
            P(("parts", "group"), "tensor"),
            P(("parts", "group"), "tensor"),
            P(("parts", "group"), "tensor"),
            P(("parts", "group"), "tensor"),
            P(("parts", "group"), "tensor"),
            P("parts"),
            P("parts"),
            P("parts", None),
            P("parts", None),
            P("parts", None),
            P("parts", None),
        ),
        out_specs=(P(("parts", "group"), "tensor"), P(("parts", "group"), None, "tensor", None)),
        check_vma=False,
    )
```

```python
import functools
import math

import jax
import jax.numpy as jnp
import numpy as np
from jax import lax
from jax.experimental import pallas as pl
from jax.experimental.pallas import tpu as pltpu
from jax.sharding import PartitionSpec as P

HEAD = 128
BLOCK = 8
MAXP = 2
CTXP = 64

VMEM_LIMIT = 24 * 1024 * 1024

SMEM = pl.BlockSpec(memory_space=pltpu.SMEM)
VMEM = pl.BlockSpec(memory_space=pltpu.VMEM)
JOINED = 1
PROMPT, OFFSET, LIVE, CACHED, SOURCE, COLUMN, PLACE = range(7)
ANY = pl.BlockSpec(memory_space=pl.ANY)
HBM = pl.BlockSpec(memory_space=pltpu.HBM)


def rope_table():
    count = CTXP + MAXP * BLOCK
    half = HEAD // 2
    frequency = np.exp(np.arange(half) * (-2.0 * math.log(500000.0) / HEAD))
    angles = np.arange(count)[:, None] * frequency[None, :]
    cosine, sine = np.cos(angles), np.sin(angles)
    return (
        np.concatenate([cosine, cosine], axis=1).astype(np.float32),
        np.concatenate([-sine, sine], axis=1).astype(np.float32),
    )


def loop(count, body, unrolled=16):
    if count <= unrolled:
        for index in range(count):
            body(index)
    else:
        lax.fori_loop(0, count, lambda index, carry: (body(index), carry)[1], 0)


def turned(head_block, cosine, sine):
    return head_block * cosine + pltpu.roll(head_block, HEAD // 2, 1) * sine


def dispatch_kernel(
    groups, spread_in, turn_in, new_blocks_in, owner_in, queries_in, keys_in, values_in, *rest
):
    outs, handed, rest = rest[:groups], list(rest[groups : 2 * groups - 1]), rest[2 * groups - 1 :]
    handed.insert(JOINED, None)
    spread, turn, new_blocks, owner, queries, keys, values, table, sem = rest
    own = lax.axis_index("group")
    slots, _, width_q = queries.shape
    width_k = keys.shape[2]
    capacity = slots // groups
    prompts = new_blocks.shape[1]
    copies = [
        pltpu.make_async_copy(source, target, sem.at[n])
        for n, (source, target) in enumerate(
            (
                (spread_in, spread),
                (turn_in, turn),
                (new_blocks_in, new_blocks),
                (owner_in, owner),
                (keys_in, keys),
                (values_in, values),
                (queries_in, queries),
            )
        )
    ]
    for copy in copies:
        copy.start()
    for copy in copies[:4]:
        copy.wait()

    def clear(n):
        table[n] = 0

    loop(groups * groups, clear)

    def column(c):
        target = lax.rem(own - spread[c] + groups, groups)

        def find(p, carry):
            start, holders = carry
            blocks = new_blocks[target, p]
            holders = [
                jnp.where((c + groups * n >= start) & (c + groups * n < start + blocks), owner[target, p], holder)
                for n, holder in enumerate(holders)
            ]
            return start + blocks, holders

        carry = (jnp.int32(0), [jnp.int32(-1)] * capacity)
        if prompts <= 8:
            for p in range(prompts):
                carry = find(p, carry)
        else:
            carry = lax.fori_loop(0, prompts, find, carry)
        for n, holder in enumerate(carry[1]):
            at = lax.rem(holder - own + groups, groups) * groups + target
            table[jnp.where(holder >= 0, at, groups * groups)] = lax.rem(c + groups * n + turn[own], slots)

    loop(groups, column)
    for copy in copies[4:]:
        copy.wait()
    for distance in range(groups):
        first_slot = column_of(spread, groups, distance) + turn[own]
        out = outs[distance]
        wide = 2 * width_k
        per_slot = width_q // wide + 1
        for step in range(capacity):
            source = lax.rem(first_slot + groups * step, slots)
            for n in range(per_slot - 1):
                out[step * per_slot + n] = queries[source, :, n * wide : (n + 1) * wide]
            last = step * per_slot + per_slot - 1
            out[last, :, :width_k] = keys[source]
            out[last, :, width_k:] = values[source]
        target, base = (out, capacity * per_slot) if distance == JOINED else (handed[distance], 0)

        def page(g):
            source = table[distance * groups + g]
            target[base + g, :, :width_k] = keys[source]
            target[base + g, :, width_k:] = values[source]

        loop(groups, page)


def column_of(spread, groups, distance):
    wanted = (groups - distance) % groups
    if groups <= 8:
        return sum(jnp.where(spread[c] == wanted, c, 0) for c in range(groups))
    return lax.fori_loop(
        0, groups, lambda c, found: jnp.where(spread[c] == wanted, c, found), jnp.int32(0)
    )


def make_plan(groups, own, spread, new_blocks, prefix_len, owner, page_start, plan):
    prompts = new_blocks.shape[1]
    slots = prompts * MAXP

    def clear(j):
        plan[PROMPT, j] = 0
        plan[OFFSET, j] = 0
        plan[LIVE, j] = 0
        plan[CACHED, j] = 0

    loop(slots, clear)

    def one(p, start):
        blocks = new_blocks[own, p]
        cached = prefix_len[own, p]
        for step in range(MAXP):
            at = jnp.where(step < blocks, start + step, slots)
            plan[PROMPT, at] = p
            plan[OFFSET, at] = cached + step * BLOCK
            plan[LIVE, at] = 1 + step
            plan[CACHED, at] = cached
        return start + blocks

    start = jnp.int32(0)
    if prompts <= 8:
        for p in range(prompts):
            start = one(p, start)
    else:
        lax.fori_loop(0, prompts, one, start)

    def of_group(g):
        def one(p, start):
            blocks = new_blocks[g, p]
            mine = owner[g, p] == own
            for step in range(MAXP):
                root = lax.rem(g + spread[lax.rem(start + step, groups)], groups)
                at = jnp.where(mine, page_start[g, p] + step, slots)
                away = lax.rem(own - root + groups, groups)
                plan[SOURCE, at] = jnp.where(step < blocks, away * groups + g, -1)
                plan[PLACE, at] = prefix_len[g, p] + step * BLOCK
            return start + blocks

        start = jnp.int32(0)
        if prompts <= 8:
            for p in range(prompts):
                start = one(p, start)
        else:
            lax.fori_loop(0, prompts, one, start)

    loop(groups, of_group)
    for distance in range(groups):
        plan[COLUMN, distance] = column_of(spread, groups, distance)


def plan_kernel(groups, tensors, spread, new_blocks, prefix_len, owner, page_start, _, plan, pick):
    own = lax.axis_index("group")
    own_tensor = lax.axis_index("tensor")
    make_plan(groups, own, spread, new_blocks, prefix_len, owner, page_start, plan)
    pages = new_blocks.shape[1] * MAXP
    tokens = BLOCK // tensors
    size = pages * 2 * tokens
    row = lax.broadcasted_iota(jnp.int32, pick.shape, 0)
    col = lax.broadcasted_iota(jnp.int32, pick.shape, 1)
    share = lax.rem(row // size + own_tensor, tensors)
    kind, page = (row // tokens) % 2, (row // (2 * tokens)) % pages
    wanted = (kind * pages + page) * BLOCK + share * tokens + row % tokens
    pick[...] = (col == wanted).astype(jnp.float32).astype(jnp.bfloat16)


def pages_kernel(groups, tensors, plan, pick, cosine, sine, *rest):
    chunks, rest = rest[:groups], rest[groups:]
    outs, (blocks, rows) = rest[:tensors], rest[tensors:]
    width_k = rows.shape[1]
    pages = rows.shape[0] // (2 * BLOCK)
    size = pick.shape[0] // tensors
    for distance in range(groups):
        first = chunks[distance].shape[0] - groups
        blocks[distance * groups : (distance + 1) * groups] = chunks[distance][first:]

    def assemble(page):
        source = plan[SOURCE, page]
        place = plan[PLACE, page]
        block = blocks[jnp.maximum(source, 0)].astype(jnp.float32)
        block = jnp.where(source >= 0, block, 0.0)
        cos = cosine[pl.ds(place, BLOCK), :]
        sin = sine[pl.ds(place, BLOCK), :]
        for first in range(0, width_k, HEAD):
            part = slice(first, first + HEAD)
            rows[pl.ds(pl.multiple_of(page * BLOCK, BLOCK), BLOCK), part] = turned(
                block[:, part], cos, sin
            )
        rows[pl.ds(pl.multiple_of((pages + page) * BLOCK, BLOCK), BLOCK), :] = block[:, width_k:]

    loop(pages, assemble)
    moved = jnp.dot(pick[...], rows[...].astype(jnp.bfloat16), preferred_element_type=jnp.float32)
    moved = moved.astype(jnp.bfloat16)
    for distance in range(tensors):
        outs[distance][...] = moved[distance * size : (distance + 1) * size]


def columns(chunk, step, width_q, first, width):
    wide = chunk.shape[2]
    row = step * (width_q // wide + 1) + first // wide
    return chunk[row, :, first % wide : first % wide + width]


def attention_kernel(groups, heads_q, heads_k, plan, prefix_keys, prefix_values, cosine, sine, *rest):
    arrived, (out, new_keys, new_values) = rest[:groups], rest[groups:]
    slots = out.shape[0]
    capacity = slots // groups
    ratio = heads_q // heads_k
    width_q = heads_q * HEAD
    width_k = heads_k * HEAD
    scale = math.log2(math.e) / math.sqrt(HEAD)
    span = CTXP + 2 * BLOCK
    lane = lax.broadcasted_iota(jnp.int32, (BLOCK, span), 1)
    token = lax.broadcasted_iota(jnp.int32, (BLOCK, span), 0)
    fresh = (lane >= CTXP + BLOCK) & (lane - (CTXP + BLOCK) <= token)
    before = (lane >= CTXP) & (lane < CTXP + BLOCK)

    blocks = []
    for distance in range(groups):
        first_slot = plan[COLUMN, distance]
        for step in range(capacity):
            j = first_slot + groups * step
            here = functools.partial(columns, arrived[distance], step, width_q)
            cos = cosine[pl.ds(plan[OFFSET, j], BLOCK), :]
            sin = sine[pl.ds(plan[OFFSET, j], BLOCK), :]
            new_keys[j] = jnp.concatenate(
                [
                    turned(here(first, HEAD).astype(jnp.float32), cos, sin)
                    for first in range(width_q, width_q + width_k, HEAD)
                ],
                axis=1,
            )
            new_values[j] = here(width_q + width_k, width_k).astype(jnp.float32)
            blocks.append((j, here, cos, sin))

    for at in range(0, len(blocks), 8):
        some = blocks[at : at + 8]
        for h in range(heads_k):
            part = slice(h * HEAD, (h + 1) * HEAD)
            scores = []
            for j, here, cos, sin in some:
                prev = jnp.maximum(j - 1, 0)
                region = pl.ds(pl.multiple_of(plan[PROMPT, j] * CTXP, CTXP), CTXP)
                mask = fresh | (lane < plan[CACHED, j]) & (lane < CTXP) | before & (plan[LIVE, j] == 2)
                new_key = jnp.concatenate([new_keys[prev, :, part], new_keys[j, :, part]], axis=0)
                key = jnp.concatenate([prefix_keys[region, part], new_key.astype(jnp.bfloat16)], axis=0)
                query = jnp.concatenate(
                    [
                        turned(here(n * HEAD, HEAD).astype(jnp.float32), cos, sin)
                        for n in range(h * ratio, (h + 1) * ratio)
                    ],
                    axis=0,
                ).astype(jnp.bfloat16)
                score = lax.dot_general(
                    query, key, (((1,), (1,)), ((), ())), preferred_element_type=jnp.float32
                )
                scores.append(jnp.where(mask[None], score.reshape(ratio, BLOCK, span), -1e30))
            score = jnp.concatenate(scores, axis=0)
            top = jnp.max(score, axis=2, keepdims=True)
            powers = jnp.exp2((score - top) * scale)
            weights = powers * (1.0 / jnp.sum(powers, axis=2, keepdims=True))
            weights = weights.reshape(len(some), ratio * BLOCK, span).astype(jnp.bfloat16)
            for place, (j, here, cos, sin) in enumerate(some):
                prev = jnp.maximum(j - 1, 0)
                region = pl.ds(pl.multiple_of(plan[PROMPT, j] * CTXP, CTXP), CTXP)
                new_value = jnp.concatenate([new_values[prev, :, part], new_values[j, :, part]], axis=0)
                value = jnp.concatenate([prefix_values[region, part], new_value.astype(jnp.bfloat16)], axis=0)
                mixed = jnp.dot(weights[place], value, preferred_element_type=jnp.float32)
                mixed = jnp.where(plan[LIVE, j] > 0, mixed, 0.0)
                for n in range(ratio):
                    first = (h * ratio + n) * HEAD
                    out[j, :, first : first + HEAD] = mixed[n * BLOCK : (n + 1) * BLOCK].astype(
                        jnp.bfloat16
                    )


def cache_kernel(tensors, *rest):
    arrived, out = rest[:tensors], rest[tensors + 1]
    own_tensor = lax.axis_index("tensor")
    width_k = arrived[0].shape[1]
    for distance in range(tensors):
        sender = lax.rem(own_tensor - distance + tensors, tensors)
        at = pl.ds(pl.multiple_of(sender * width_k, HEAD), width_k)
        part = arrived[distance][...].astype(jnp.float32)
        out[:, :, at] = part.reshape(out.shape[0], out.shape[1], width_k).astype(jnp.bfloat16)


def in_hbm(operand):
    return pltpu.with_memory_space_constraint(operand, pltpu.HBM)


def after(arrays, others):
    return pl.pallas_call(
        lambda *refs: None,
        out_shape=[jax.ShapeDtypeStruct(array.shape, array.dtype) for array in arrays],
        in_specs=[ANY] * (len(arrays) + len(others)),
        out_specs=[ANY] * len(arrays),
        input_output_aliases={n: n for n in range(len(arrays))},
        compiler_params=pltpu.CompilerParams(vmem_limit_bytes=VMEM_LIMIT),
        name="hold",
    )(*arrays, *others)


def shifted(chunks, axis):
    size = lax.axis_size(axis)
    return [chunks[0]] + [
        chunks[d] is not None
        and lax.ppermute(chunks[d], axis, [(i, (i + d) % size) for i in range(size)])
        for d in range(1, size)
    ]


def per_device(
    queries,
    keys,
    values,
    prefix_keys,
    prefix_values,
    spread,
    turn,
    new_blocks,
    prefix_len,
    owner,
    page_start,
):
    groups = lax.axis_size("group")
    tensors = lax.axis_size("tensor")
    width_q = queries.shape[1]
    width_k = keys.shape[1]
    heads_q = width_q // HEAD
    heads_k = width_k // HEAD
    slots = queries.shape[0] // BLOCK
    capacity = slots // groups
    prompts = new_blocks.shape[1]
    tokens = BLOCK // tensors
    pages = prompts * MAXP
    cosine, sine = (jnp.asarray(table) for table in rope_table())
    params = pltpu.CompilerParams(vmem_limit_bytes=VMEM_LIMIT)
    blocks_q = queries.reshape(slots, BLOCK, width_q)
    blocks_k = keys.reshape(slots, BLOCK, width_k)
    blocks_v = values.reshape(slots, BLOCK, width_k)

    wide = 2 * width_k
    chunk_rows = capacity * (width_q // wide + 1)

    def chunk(rows):
        return jax.ShapeDtypeStruct((rows, BLOCK, wide), jnp.bfloat16)

    sent = pl.pallas_call(
        functools.partial(dispatch_kernel, groups),
        out_shape=[
            chunk(chunk_rows + (groups if distance == JOINED else 0)) for distance in range(groups)
        ]
        + [chunk(groups)] * (groups - 1),
        in_specs=[HBM] * 7,
        out_specs=[VMEM] * (2 * groups - 1),
        scratch_shapes=[
            *(pltpu.SMEM(array.shape, jnp.int32) for array in (spread, turn, new_blocks, owner)),
            *(pltpu.VMEM(array.shape, jnp.bfloat16) for array in (blocks_q, blocks_k, blocks_v)),
            pltpu.SMEM((groups * groups + 1,), jnp.int32),
            pltpu.SemaphoreType.DMA((7,)),
        ],
        compiler_params=params,
        name="dispatch",
    )(
        *(
            in_hbm(operand)
            for operand in (spread, turn, new_blocks, owner, blocks_q, blocks_k, blocks_v)
        )
    )
    part_rows = pages * 2 * tokens
    plan, pick = pl.pallas_call(
        functools.partial(plan_kernel, groups, tensors),
        out_shape=[
            jax.ShapeDtypeStruct((7, max(slots, groups) + 1), jnp.int32),
            jax.ShapeDtypeStruct((tensors * part_rows, 2 * pages * BLOCK), jnp.bfloat16),
        ],
        in_specs=[SMEM] * 5 + [ANY],
        out_specs=[SMEM, VMEM],
        compiler_params=params,
        name="plan",
    )(spread, new_blocks, prefix_len, owner, page_start, sent[0])
    own, pages_only = list(sent[:groups]), list(sent[groups:])
    pages_only.insert(JOINED, own[JOINED])
    handed = shifted(pages_only, "group")
    later = [distance for distance in range(1, groups) if distance != JOINED]
    held = dict(zip(later, after([own[distance] for distance in later], [*handed[1:], plan])))
    moved = shifted([own[0]] + [held.get(distance) for distance in range(1, groups)], "group")
    arrived = [handed[n] if n == JOINED else moved[n] for n in range(groups)]

    part = jax.ShapeDtypeStruct((part_rows, width_k), jnp.bfloat16)
    finished = pl.pallas_call(
        functools.partial(pages_kernel, groups, tensors),
        out_shape=[part] * tensors,
        in_specs=[SMEM] + [VMEM] * (3 + groups),
        out_specs=[VMEM] * tensors,
        compiler_params=params,
        scratch_shapes=[
            pltpu.VMEM((groups * groups, BLOCK, 2 * width_k), jnp.bfloat16),
            pltpu.VMEM((2 * pages * BLOCK, width_k), jnp.float32),
        ],
        name="finish_pages",
    )(plan, pick, cosine, sine, *handed)
    parts = shifted(finished, "tensor")

    attention = pl.pallas_call(
        functools.partial(attention_kernel, groups, heads_q, heads_k),
        out_shape=jax.ShapeDtypeStruct((slots, BLOCK, width_q), jnp.bfloat16),
        in_specs=[SMEM] + [VMEM] * (4 + groups),
        out_specs=VMEM,
        scratch_shapes=[pltpu.VMEM((slots, BLOCK, width_k), jnp.float32)] * 2,
        compiler_params=params,
        name="attention",
    )(plan, prefix_keys, prefix_values, cosine, sine, *arrived)

    cache = pl.pallas_call(
        functools.partial(cache_kernel, tensors),
        out_shape=jax.ShapeDtypeStruct((pages * 2, tokens, tensors * width_k), jnp.bfloat16),
        in_specs=[VMEM] * tensors + [ANY],
        out_specs=VMEM,
        compiler_params=params,
        name="place_pages",
    )(*parts, in_hbm(attention))
    return (
        attention.reshape(slots * BLOCK, width_q),
        cache.reshape(pages, 2, tokens, tensors * width_k),
    )


def solution(mesh):
    return jax.shard_map(
        per_device,
        mesh=mesh,
        in_specs=(
            P(("parts", "group"), "tensor"),
            P(("parts", "group"), "tensor"),
            P(("parts", "group"), "tensor"),
            P(("parts", "group"), "tensor"),
            P(("parts", "group"), "tensor"),
            P("parts"),
            P("parts"),
            P("parts", None),
            P("parts", None),
            P("parts", None),
            P("parts", None),
        ),
        out_specs=(P(("parts", "group"), "tensor"), P(("parts", "group"), None, "tensor", None)),
        check_vma=False,
    )
```

```python
import functools
import math

import jax
import jax.numpy as jnp
import numpy as np
from jax import lax
from jax.experimental import pallas as pl
from jax.experimental.pallas import tpu as pltpu
from jax.sharding import PartitionSpec as P

HEAD = 128
BLOCK = 8
MAXP = 2
CTXP = 64

VMEM_LIMIT = 24 * 1024 * 1024

SMEM = pl.BlockSpec(memory_space=pltpu.SMEM)
VMEM = pl.BlockSpec(memory_space=pltpu.VMEM)
JOINED = 1
PROMPT, OFFSET, LIVE, CACHED, SOURCE, COLUMN, PLACE = range(7)
ANY = pl.BlockSpec(memory_space=pl.ANY)
HBM = pl.BlockSpec(memory_space=pltpu.HBM)


def rope_table():
    count = CTXP + MAXP * BLOCK
    half = HEAD // 2
    frequency = np.exp(np.arange(half) * (-2.0 * math.log(500000.0) / HEAD))
    angles = np.arange(count)[:, None] * frequency[None, :]
    cosine, sine = np.cos(angles), np.sin(angles)
    return (
        np.concatenate([cosine, cosine], axis=1).astype(np.float32),
        np.concatenate([-sine, sine], axis=1).astype(np.float32),
    )


def loop(count, body, unrolled=16):
    if count <= unrolled:
        for index in range(count):
            body(index)
    else:
        lax.fori_loop(0, count, lambda index, carry: (body(index), carry)[1], 0)


def turned(head_block, cosine, sine):
    return head_block * cosine + pltpu.roll(head_block, HEAD // 2, 1) * sine


def dispatch_kernel(
    groups, spread_in, turn_in, new_blocks_in, owner_in, queries_in, keys_in, values_in, *rest
):
    outs, handed, rest = rest[:groups], list(rest[groups : 2 * groups - 1]), rest[2 * groups - 1 :]
    handed.insert(JOINED, None)
    spread, turn, new_blocks, owner, queries, keys, values, table, sem = rest
    own = lax.axis_index("group")
    slots, _, width_q = queries.shape
    width_k = keys.shape[2]
    capacity = slots // groups
    prompts = new_blocks.shape[1]
    copies = [
        pltpu.make_async_copy(source, target, sem.at[n])
        for n, (source, target) in enumerate(
            (
                (spread_in, spread),
                (turn_in, turn),
                (new_blocks_in, new_blocks),
                (owner_in, owner),
                (keys_in, keys),
                (values_in, values),
                (queries_in, queries),
            )
        )
    ]
    for copy in copies:
        copy.start()
    for copy in copies[:4]:
        copy.wait()

    def clear(n):
        table[n] = 0

    loop(groups * groups, clear)

    def column(c):
        target = lax.rem(own - spread[c] + groups, groups)

        def find(p, carry):
            start, holders = carry
            blocks = new_blocks[target, p]
            holders = [
                jnp.where((c + groups * n >= start) & (c + groups * n < start + blocks), owner[target, p], holder)
                for n, holder in enumerate(holders)
            ]
            return start + blocks, holders

        carry = (jnp.int32(0), [jnp.int32(-1)] * capacity)
        if prompts <= 8:
            for p in range(prompts):
                carry = find(p, carry)
        else:
            carry = lax.fori_loop(0, prompts, find, carry)
        for n, holder in enumerate(carry[1]):
            at = lax.rem(holder - own + groups, groups) * groups + target
            table[jnp.where(holder >= 0, at, groups * groups)] = lax.rem(c + groups * n + turn[own], slots)

    loop(groups, column)
    for copy in copies[4:]:
        copy.wait()
    for distance in range(groups):
        first_slot = column_of(spread, groups, distance) + turn[own]
        out = outs[distance]
        wide = 2 * width_k
        per_slot = width_q // wide + 1
        for step in range(capacity):
            source = lax.rem(first_slot + groups * step, slots)
            for n in range(per_slot - 1):
                out[step * per_slot + n] = queries[source, :, n * wide : (n + 1) * wide]
            last = step * per_slot + per_slot - 1
            out[last, :, :width_k] = keys[source]
            out[last, :, width_k:] = values[source]
        target, base = (out, capacity * per_slot) if distance == JOINED else (handed[distance], 0)

        def page(g):
            source = table[distance * groups + g]
            target[base + g, :, :width_k] = keys[source]
            target[base + g, :, width_k:] = values[source]

        loop(groups, page)


def column_of(spread, groups, distance):
    wanted = (groups - distance) % groups
    if groups <= 8:
        return sum(jnp.where(spread[c] == wanted, c, 0) for c in range(groups))
    return lax.fori_loop(
        0, groups, lambda c, found: jnp.where(spread[c] == wanted, c, found), jnp.int32(0)
    )


def make_plan(groups, own, spread, new_blocks, prefix_len, owner, page_start, plan):
    prompts = new_blocks.shape[1]
    slots = prompts * MAXP

    def clear(j):
        plan[PROMPT, j] = 0
        plan[OFFSET, j] = 0
        plan[LIVE, j] = 0
        plan[CACHED, j] = 0

    loop(slots, clear)

    def one(p, start):
        blocks = new_blocks[own, p]
        cached = prefix_len[own, p]
        for step in range(MAXP):
            at = jnp.where(step < blocks, start + step, slots)
            plan[PROMPT, at] = p
            plan[OFFSET, at] = cached + step * BLOCK
            plan[LIVE, at] = 1 + step
            plan[CACHED, at] = cached
        return start + blocks

    start = jnp.int32(0)
    if prompts <= 8:
        for p in range(prompts):
            start = one(p, start)
    else:
        lax.fori_loop(0, prompts, one, start)

    def of_group(g):
        def one(p, start):
            blocks = new_blocks[g, p]
            mine = owner[g, p] == own
            for step in range(MAXP):
                root = lax.rem(g + spread[lax.rem(start + step, groups)], groups)
                at = jnp.where(mine, page_start[g, p] + step, slots)
                away = lax.rem(own - root + groups, groups)
                plan[SOURCE, at] = jnp.where(step < blocks, away * groups + g, -1)
                plan[PLACE, at] = prefix_len[g, p] + step * BLOCK
            return start + blocks

        start = jnp.int32(0)
        if prompts <= 8:
            for p in range(prompts):
                start = one(p, start)
        else:
            lax.fori_loop(0, prompts, one, start)

    loop(groups, of_group)
    for distance in range(groups):
        plan[COLUMN, distance] = column_of(spread, groups, distance)


def plan_kernel(groups, tensors, spread, new_blocks, prefix_len, owner, page_start, _, plan, pick):
    own = lax.axis_index("group")
    own_tensor = lax.axis_index("tensor")
    make_plan(groups, own, spread, new_blocks, prefix_len, owner, page_start, plan)
    pages = new_blocks.shape[1] * MAXP
    tokens = BLOCK // tensors
    size = pages * 2 * tokens
    row = lax.broadcasted_iota(jnp.int32, pick.shape, 0)
    col = lax.broadcasted_iota(jnp.int32, pick.shape, 1)
    share = lax.rem(row // size + own_tensor, tensors)
    kind, page = (row // tokens) % 2, (row // (2 * tokens)) % pages
    wanted = (kind * pages + page) * BLOCK + share * tokens + row % tokens
    pick[...] = (col == wanted).astype(jnp.float32).astype(jnp.bfloat16)


def pages_kernel(groups, tensors, plan, pick, cosine, sine, *rest):
    chunks, rest = rest[:groups], rest[groups:]
    outs, (blocks, rows) = rest[:tensors], rest[tensors:]
    width_k = rows.shape[1]
    pages = rows.shape[0] // (2 * BLOCK)
    size = pick.shape[0] // tensors
    for distance in range(groups):
        first = chunks[distance].shape[0] - groups
        blocks[distance * groups : (distance + 1) * groups] = chunks[distance][first:]

    def assemble(page):
        source = plan[SOURCE, page]
        place = plan[PLACE, page]
        block = blocks[jnp.maximum(source, 0)].astype(jnp.float32)
        block = jnp.where(source >= 0, block, 0.0)
        cos = cosine[pl.ds(place, BLOCK), :]
        sin = sine[pl.ds(place, BLOCK), :]
        for first in range(0, width_k, HEAD):
            part = slice(first, first + HEAD)
            rows[pl.ds(pl.multiple_of(page * BLOCK, BLOCK), BLOCK), part] = turned(
                block[:, part], cos, sin
            )
        rows[pl.ds(pl.multiple_of((pages + page) * BLOCK, BLOCK), BLOCK), :] = block[:, width_k:]

    loop(pages, assemble)
    moved = jnp.dot(pick[...], rows[...].astype(jnp.bfloat16), preferred_element_type=jnp.float32)
    moved = moved.astype(jnp.bfloat16)
    for distance in range(tensors):
        outs[distance][...] = moved[distance * size : (distance + 1) * size]


def columns(chunk, step, width_q, first, width):
    wide = chunk.shape[2]
    row = step * (width_q // wide + 1) + first // wide
    return chunk[row, :, first % wide : first % wide + width]


def attention_kernel(groups, heads_q, heads_k, plan, prefix_keys, prefix_values, cosine, sine, *rest):
    arrived, (out, new_keys, new_values) = rest[:groups], rest[groups:]
    slots = out.shape[0]
    capacity = slots // groups
    ratio = heads_q // heads_k
    width_q = heads_q * HEAD
    width_k = heads_k * HEAD
    scale = math.log2(math.e) / math.sqrt(HEAD)
    span = CTXP + 2 * BLOCK
    lane = lax.broadcasted_iota(jnp.int32, (BLOCK, span), 1)
    token = lax.broadcasted_iota(jnp.int32, (BLOCK, span), 0)
    fresh = (lane >= CTXP + BLOCK) & (lane - (CTXP + BLOCK) <= token)
    before = (lane >= CTXP) & (lane < CTXP + BLOCK)

    blocks = []
    for distance in range(groups):
        first_slot = plan[COLUMN, distance]
        for step in range(capacity):
            j = first_slot + groups * step
            here = functools.partial(columns, arrived[distance], step, width_q)
            cos = cosine[pl.ds(plan[OFFSET, j], BLOCK), :]
            sin = sine[pl.ds(plan[OFFSET, j], BLOCK), :]
            new_keys[j] = jnp.concatenate(
                [
                    turned(here(first, HEAD).astype(jnp.float32), cos, sin)
                    for first in range(width_q, width_q + width_k, HEAD)
                ],
                axis=1,
            )
            new_values[j] = here(width_q + width_k, width_k).astype(jnp.float32)
            blocks.append((j, here, cos, sin))

    for at in range(0, len(blocks), 8):
        some = blocks[at : at + 8]
        for h in range(heads_k):
            part = slice(h * HEAD, (h + 1) * HEAD)
            scores = []
            for j, here, cos, sin in some:
                prev = jnp.maximum(j - 1, 0)
                region = pl.ds(pl.multiple_of(plan[PROMPT, j] * CTXP, CTXP), CTXP)
                mask = fresh | (lane < plan[CACHED, j]) & (lane < CTXP) | before & (plan[LIVE, j] == 2)
                new_key = jnp.concatenate([new_keys[prev, :, part], new_keys[j, :, part]], axis=0)
                key = jnp.concatenate([prefix_keys[region, part], new_key.astype(jnp.bfloat16)], axis=0)
                query = jnp.concatenate(
                    [
                        turned(here(n * HEAD, HEAD).astype(jnp.float32), cos, sin)
                        for n in range(h * ratio, (h + 1) * ratio)
                    ],
                    axis=0,
                ).astype(jnp.bfloat16)
                score = lax.dot_general(
                    query, key, (((1,), (1,)), ((), ())), preferred_element_type=jnp.float32
                )
                scores.append(jnp.where(mask[None], score.reshape(ratio, BLOCK, span), -1e30))
            score = jnp.concatenate(scores, axis=0)
            top = jnp.max(score, axis=2, keepdims=True)
            powers = jnp.exp2((score - top) * scale)
            weights = powers * (1.0 / jnp.sum(powers, axis=2, keepdims=True))
            weights = weights.reshape(len(some), ratio * BLOCK, span).astype(jnp.bfloat16)
            for place, (j, here, cos, sin) in enumerate(some):
                prev = jnp.maximum(j - 1, 0)
                region = pl.ds(pl.multiple_of(plan[PROMPT, j] * CTXP, CTXP), CTXP)
                new_value = jnp.concatenate([new_values[prev, :, part], new_values[j, :, part]], axis=0)
                value = jnp.concatenate([prefix_values[region, part], new_value.astype(jnp.bfloat16)], axis=0)
                mixed = jnp.dot(weights[place], value, preferred_element_type=jnp.float32)
                mixed = jnp.where(plan[LIVE, j] > 0, mixed, 0.0)
                for n in range(ratio):
                    first = (h * ratio + n) * HEAD
                    out[j, :, first : first + HEAD] = mixed[n * BLOCK : (n + 1) * BLOCK].astype(
                        jnp.bfloat16
                    )


def cache_kernel(tensors, *rest):
    arrived, out = rest[:tensors], rest[tensors + 1]
    own_tensor = lax.axis_index("tensor")
    width_k = arrived[0].shape[1]
    for distance in range(tensors):
        sender = lax.rem(own_tensor - distance + tensors, tensors)
        at = pl.ds(pl.multiple_of(sender * width_k, HEAD), width_k)
        part = arrived[distance][...].astype(jnp.float32)
        out[:, :, at] = part.reshape(out.shape[0], out.shape[1], width_k).astype(jnp.bfloat16)


def in_hbm(operand):
    return pltpu.with_memory_space_constraint(operand, pltpu.HBM)


def after(arrays, others):
    return pl.pallas_call(
        lambda *refs: None,
        out_shape=[jax.ShapeDtypeStruct(array.shape, array.dtype) for array in arrays],
        in_specs=[ANY] * (len(arrays) + len(others)),
        out_specs=[ANY] * len(arrays),
        input_output_aliases={n: n for n in range(len(arrays))},
        compiler_params=pltpu.CompilerParams(vmem_limit_bytes=VMEM_LIMIT),
        name="hold",
    )(*arrays, *others)


def shifted(chunks, axis):
    size = lax.axis_size(axis)
    return [chunks[0]] + [
        chunks[d] is not None
        and lax.ppermute(chunks[d], axis, [(i, (i + d) % size) for i in range(size)])
        for d in range(1, size)
    ]


def per_device(
    queries,
    keys,
    values,
    prefix_keys,
    prefix_values,
    spread,
    turn,
    new_blocks,
    prefix_len,
    owner,
    page_start,
):
    groups = lax.axis_size("group")
    tensors = lax.axis_size("tensor")
    width_q = queries.shape[1]
    width_k = keys.shape[1]
    heads_q = width_q // HEAD
    heads_k = width_k // HEAD
    slots = queries.shape[0] // BLOCK
    capacity = slots // groups
    prompts = new_blocks.shape[1]
    tokens = BLOCK // tensors
    pages = prompts * MAXP
    cosine, sine = (jnp.asarray(table) for table in rope_table())
    params = pltpu.CompilerParams(vmem_limit_bytes=VMEM_LIMIT)
    blocks_q = queries.reshape(slots, BLOCK, width_q)
    blocks_k = keys.reshape(slots, BLOCK, width_k)
    blocks_v = values.reshape(slots, BLOCK, width_k)

    wide = 2 * width_k
    chunk_rows = capacity * (width_q // wide + 1)

    def chunk(rows):
        return jax.ShapeDtypeStruct((rows, BLOCK, wide), jnp.bfloat16)

    sent = pl.pallas_call(
        functools.partial(dispatch_kernel, groups),
        out_shape=[
            chunk(chunk_rows + (groups if distance == JOINED else 0)) for distance in range(groups)
        ]
        + [chunk(groups)] * (groups - 1),
        in_specs=[HBM] * 7,
        out_specs=[VMEM] * (2 * groups - 1),
        scratch_shapes=[
            *(pltpu.SMEM(array.shape, jnp.int32) for array in (spread, turn, new_blocks, owner)),
            *(pltpu.VMEM(array.shape, jnp.bfloat16) for array in (blocks_q, blocks_k, blocks_v)),
            pltpu.SMEM((groups * groups + 1,), jnp.int32),
            pltpu.SemaphoreType.DMA((7,)),
        ],
        compiler_params=params,
        name="dispatch",
    )(
        *(
            in_hbm(operand)
            for operand in (spread, turn, new_blocks, owner, blocks_q, blocks_k, blocks_v)
        )
    )
    part_rows = pages * 2 * tokens
    plan, pick = pl.pallas_call(
        functools.partial(plan_kernel, groups, tensors),
        out_shape=[
            jax.ShapeDtypeStruct((7, max(slots, groups) + 1), jnp.int32),
            jax.ShapeDtypeStruct((tensors * part_rows, 2 * pages * BLOCK), jnp.bfloat16),
        ],
        in_specs=[SMEM] * 5 + [ANY],
        out_specs=[SMEM, VMEM],
        compiler_params=params,
        name="plan",
    )(spread, new_blocks, prefix_len, owner, page_start, sent[0])
    own, pages_only = list(sent[:groups]), list(sent[groups:])
    pages_only.insert(JOINED, own[JOINED])
    handed = shifted(pages_only, "group")
    later = [distance for distance in range(1, groups) if distance != JOINED]
    held = dict(zip(later, after([own[distance] for distance in later], [*(handed[n] for n in later), plan])))
    moved = shifted([own[0]] + [held.get(distance) for distance in range(1, groups)], "group")
    arrived = [handed[n] if n == JOINED else moved[n] for n in range(groups)]

    part = jax.ShapeDtypeStruct((part_rows, width_k), jnp.bfloat16)
    finished = pl.pallas_call(
        functools.partial(pages_kernel, groups, tensors),
        out_shape=[part] * tensors,
        in_specs=[SMEM] + [VMEM] * (3 + groups),
        out_specs=[VMEM] * tensors,
        compiler_params=params,
        scratch_shapes=[
            pltpu.VMEM((groups * groups, BLOCK, 2 * width_k), jnp.bfloat16),
            pltpu.VMEM((2 * pages * BLOCK, width_k), jnp.float32),
        ],
        name="finish_pages",
    )(plan, pick, cosine, sine, *handed)
    parts = shifted(finished, "tensor")

    attention = pl.pallas_call(
        functools.partial(attention_kernel, groups, heads_q, heads_k),
        out_shape=jax.ShapeDtypeStruct((slots, BLOCK, width_q), jnp.bfloat16),
        in_specs=[SMEM] + [VMEM] * (4 + groups),
        out_specs=VMEM,
        scratch_shapes=[pltpu.VMEM((slots, BLOCK, width_k), jnp.float32)] * 2,
        compiler_params=params,
        name="attention",
    )(plan, prefix_keys, prefix_values, cosine, sine, *arrived)

    cache = pl.pallas_call(
        functools.partial(cache_kernel, tensors),
        out_shape=jax.ShapeDtypeStruct((pages * 2, tokens, tensors * width_k), jnp.bfloat16),
        in_specs=[VMEM] * tensors + [ANY],
        out_specs=VMEM,
        compiler_params=params,
        name="place_pages",
    )(*parts, in_hbm(attention))
    return (
        attention.reshape(slots * BLOCK, width_q),
        cache.reshape(pages, 2, tokens, tensors * width_k),
    )


def solution(mesh):
    return jax.shard_map(
        per_device,
        mesh=mesh,
        in_specs=(
            P(("parts", "group"), "tensor"),
            P(("parts", "group"), "tensor"),
            P(("parts", "group"), "tensor"),
            P(("parts", "group"), "tensor"),
            P(("parts", "group"), "tensor"),
            P("parts"),
            P("parts"),
            P("parts", None),
            P("parts", None),
            P("parts", None),
            P("parts", None),
        ),
        out_specs=(P(("parts", "group"), "tensor"), P(("parts", "group"), None, "tensor", None)),
        check_vma=False,
    )
```

```python
import functools
import math

import jax
import jax.numpy as jnp
import numpy as np
from jax import lax
from jax.experimental import pallas as pl
from jax.experimental.pallas import tpu as pltpu
from jax.sharding import PartitionSpec as P

HEAD = 128
BLOCK = 8
MAXP = 2
CTXP = 64

VMEM_LIMIT = 24 * 1024 * 1024

SMEM = pl.BlockSpec(memory_space=pltpu.SMEM)
VMEM = pl.BlockSpec(memory_space=pltpu.VMEM)
JOINED = 2
PROMPT, OFFSET, LIVE, CACHED, SOURCE, COLUMN, PLACE = range(7)
ANY = pl.BlockSpec(memory_space=pl.ANY)
HBM = pl.BlockSpec(memory_space=pltpu.HBM)


def rope_table():
    count = CTXP + MAXP * BLOCK
    half = HEAD // 2
    frequency = np.exp(np.arange(half) * (-2.0 * math.log(500000.0) / HEAD))
    angles = np.arange(count)[:, None] * frequency[None, :]
    cosine, sine = np.cos(angles), np.sin(angles)
    return (
        np.concatenate([cosine, cosine], axis=1).astype(np.float32),
        np.concatenate([-sine, sine], axis=1).astype(np.float32),
    )


def loop(count, body, unrolled=16):
    if count <= unrolled:
        for index in range(count):
            body(index)
    else:
        lax.fori_loop(0, count, lambda index, carry: (body(index), carry)[1], 0)


def turned(head_block, cosine, sine):
    return head_block * cosine + pltpu.roll(head_block, HEAD // 2, 1) * sine


def dispatch_kernel(
    groups, spread_in, turn_in, new_blocks_in, owner_in, queries_in, keys_in, values_in, *rest
):
    outs, handed, rest = rest[:groups], list(rest[groups : 2 * groups - 1]), rest[2 * groups - 1 :]
    handed.insert(JOINED, None)
    spread, turn, new_blocks, owner, queries, keys, values, table, sem = rest
    own = lax.axis_index("group")
    slots, _, width_q = queries.shape
    width_k = keys.shape[2]
    capacity = slots // groups
    prompts = new_blocks.shape[1]
    copies = [
        pltpu.make_async_copy(source, target, sem.at[n])
        for n, (source, target) in enumerate(
            (
                (spread_in, spread),
                (turn_in, turn),
                (new_blocks_in, new_blocks),
                (owner_in, owner),
                (keys_in, keys),
                (values_in, values),
                (queries_in, queries),
            )
        )
    ]
    for copy in copies:
        copy.start()
    for copy in copies[:4]:
        copy.wait()

    def clear(n):
        table[n] = 0

    loop(groups * groups, clear)

    def column(c):
        target = lax.rem(own - spread[c] + groups, groups)

        def find(p, carry):
            start, holders = carry
            blocks = new_blocks[target, p]
            holders = [
                jnp.where((c + groups * n >= start) & (c + groups * n < start + blocks), owner[target, p], holder)
                for n, holder in enumerate(holders)
            ]
            return start + blocks, holders

        carry = (jnp.int32(0), [jnp.int32(-1)] * capacity)
        if prompts <= 8:
            for p in range(prompts):
                carry = find(p, carry)
        else:
            carry = lax.fori_loop(0, prompts, find, carry)
        for n, holder in enumerate(carry[1]):
            at = lax.rem(holder - own + groups, groups) * groups + target
            table[jnp.where(holder >= 0, at, groups * groups)] = lax.rem(c + groups * n + turn[own], slots)

    loop(groups, column)
    for copy in copies[4:]:
        copy.wait()
    for distance in range(groups):
        first_slot = column_of(spread, groups, distance) + turn[own]
        out = outs[distance]
        wide = 2 * width_k
        per_slot = width_q // wide + 1
        for step in range(capacity):
            source = lax.rem(first_slot + groups * step, slots)
            for n in range(per_slot - 1):
                out[step * per_slot + n] = queries[source, :, n * wide : (n + 1) * wide]
            last = step * per_slot + per_slot - 1
            out[last, :, :width_k] = keys[source]
            out[last, :, width_k:] = values[source]
        target, base = (out, capacity * per_slot) if distance == JOINED else (handed[distance], 0)

        def page(g):
            source = table[distance * groups + g]
            target[base + g, :, :width_k] = keys[source]
            target[base + g, :, width_k:] = values[source]

        loop(groups, page)


def column_of(spread, groups, distance):
    wanted = (groups - distance) % groups
    if groups <= 8:
        return sum(jnp.where(spread[c] == wanted, c, 0) for c in range(groups))
    return lax.fori_loop(
        0, groups, lambda c, found: jnp.where(spread[c] == wanted, c, found), jnp.int32(0)
    )


def make_plan(groups, own, spread, new_blocks, prefix_len, owner, page_start, plan):
    prompts = new_blocks.shape[1]
    slots = prompts * MAXP

    def clear(j):
        plan[PROMPT, j] = 0
        plan[OFFSET, j] = 0
        plan[LIVE, j] = 0
        plan[CACHED, j] = 0

    loop(slots, clear)

    def one(p, start):
        blocks = new_blocks[own, p]
        cached = prefix_len[own, p]
        for step in range(MAXP):
            at = jnp.where(step < blocks, start + step, slots)
            plan[PROMPT, at] = p
            plan[OFFSET, at] = cached + step * BLOCK
            plan[LIVE, at] = 1 + step
            plan[CACHED, at] = cached
        return start + blocks

    start = jnp.int32(0)
    if prompts <= 8:
        for p in range(prompts):
            start = one(p, start)
    else:
        lax.fori_loop(0, prompts, one, start)

    def of_group(g):
        def one(p, start):
            blocks = new_blocks[g, p]
            mine = owner[g, p] == own
            for step in range(MAXP):
                root = lax.rem(g + spread[lax.rem(start + step, groups)], groups)
                at = jnp.where(mine, page_start[g, p] + step, slots)
                away = lax.rem(own - root + groups, groups)
                plan[SOURCE, at] = jnp.where(step < blocks, away * groups + g, -1)
                plan[PLACE, at] = prefix_len[g, p] + step * BLOCK
            return start + blocks

        start = jnp.int32(0)
        if prompts <= 8:
            for p in range(prompts):
                start = one(p, start)
        else:
            lax.fori_loop(0, prompts, one, start)

    loop(groups, of_group)
    for distance in range(groups):
        plan[COLUMN, distance] = column_of(spread, groups, distance)


def plan_kernel(groups, tensors, spread, new_blocks, prefix_len, owner, page_start, _, plan, pick):
    own = lax.axis_index("group")
    own_tensor = lax.axis_index("tensor")
    make_plan(groups, own, spread, new_blocks, prefix_len, owner, page_start, plan)
    pages = new_blocks.shape[1] * MAXP
    tokens = BLOCK // tensors
    size = pages * 2 * tokens
    row = lax.broadcasted_iota(jnp.int32, pick.shape, 0)
    col = lax.broadcasted_iota(jnp.int32, pick.shape, 1)
    share = lax.rem(row // size + own_tensor, tensors)
    kind, page = (row // tokens) % 2, (row // (2 * tokens)) % pages
    wanted = (kind * pages + page) * BLOCK + share * tokens + row % tokens
    pick[...] = (col == wanted).astype(jnp.float32).astype(jnp.bfloat16)


def pages_kernel(groups, tensors, plan, pick, cosine, sine, *rest):
    chunks, rest = rest[:groups], rest[groups:]
    outs, (blocks, rows) = rest[:tensors], rest[tensors:]
    width_k = rows.shape[1]
    pages = rows.shape[0] // (2 * BLOCK)
    size = pick.shape[0] // tensors
    for distance in range(groups):
        first = chunks[distance].shape[0] - groups
        blocks[distance * groups : (distance + 1) * groups] = chunks[distance][first:]

    def assemble(page):
        source = plan[SOURCE, page]
        place = plan[PLACE, page]
        block = blocks[jnp.maximum(source, 0)].astype(jnp.float32)
        block = jnp.where(source >= 0, block, 0.0)
        cos = cosine[pl.ds(place, BLOCK), :]
        sin = sine[pl.ds(place, BLOCK), :]
        for first in range(0, width_k, HEAD):
            part = slice(first, first + HEAD)
            rows[pl.ds(pl.multiple_of(page * BLOCK, BLOCK), BLOCK), part] = turned(
                block[:, part], cos, sin
            )
        rows[pl.ds(pl.multiple_of((pages + page) * BLOCK, BLOCK), BLOCK), :] = block[:, width_k:]

    loop(pages, assemble)
    moved = jnp.dot(pick[...], rows[...].astype(jnp.bfloat16), preferred_element_type=jnp.float32)
    moved = moved.astype(jnp.bfloat16)
    for distance in range(tensors):
        outs[distance][...] = moved[distance * size : (distance + 1) * size]


def columns(chunk, step, width_q, first, width):
    wide = chunk.shape[2]
    row = step * (width_q // wide + 1) + first // wide
    return chunk[row, :, first % wide : first % wide + width]


def attention_kernel(groups, heads_q, heads_k, plan, prefix_keys, prefix_values, cosine, sine, *rest):
    arrived, (out, new_keys, new_values) = rest[:groups], rest[groups:]
    slots = out.shape[0]
    capacity = slots // groups
    ratio = heads_q // heads_k
    width_q = heads_q * HEAD
    width_k = heads_k * HEAD
    scale = math.log2(math.e) / math.sqrt(HEAD)
    span = CTXP + 2 * BLOCK
    lane = lax.broadcasted_iota(jnp.int32, (BLOCK, span), 1)
    token = lax.broadcasted_iota(jnp.int32, (BLOCK, span), 0)
    fresh = (lane >= CTXP + BLOCK) & (lane - (CTXP + BLOCK) <= token)
    before = (lane >= CTXP) & (lane < CTXP + BLOCK)

    blocks = []
    for distance in range(groups):
        first_slot = plan[COLUMN, distance]
        for step in range(capacity):
            j = first_slot + groups * step
            here = functools.partial(columns, arrived[distance], step, width_q)
            cos = cosine[pl.ds(plan[OFFSET, j], BLOCK), :]
            sin = sine[pl.ds(plan[OFFSET, j], BLOCK), :]
            new_keys[j] = jnp.concatenate(
                [
                    turned(here(first, HEAD).astype(jnp.float32), cos, sin)
                    for first in range(width_q, width_q + width_k, HEAD)
                ],
                axis=1,
            )
            new_values[j] = here(width_q + width_k, width_k).astype(jnp.float32)
            blocks.append((j, here, cos, sin))

    for at in range(0, len(blocks), 8):
        some = blocks[at : at + 8]
        for h in range(heads_k):
            part = slice(h * HEAD, (h + 1) * HEAD)
            scores = []
            for j, here, cos, sin in some:
                prev = jnp.maximum(j - 1, 0)
                region = pl.ds(pl.multiple_of(plan[PROMPT, j] * CTXP, CTXP), CTXP)
                mask = fresh | (lane < plan[CACHED, j]) & (lane < CTXP) | before & (plan[LIVE, j] == 2)
                new_key = jnp.concatenate([new_keys[prev, :, part], new_keys[j, :, part]], axis=0)
                key = jnp.concatenate([prefix_keys[region, part], new_key.astype(jnp.bfloat16)], axis=0)
                query = jnp.concatenate(
                    [
                        turned(here(n * HEAD, HEAD).astype(jnp.float32), cos, sin)
                        for n in range(h * ratio, (h + 1) * ratio)
                    ],
                    axis=0,
                ).astype(jnp.bfloat16)
                score = lax.dot_general(
                    query, key, (((1,), (1,)), ((), ())), preferred_element_type=jnp.float32
                )
                scores.append(jnp.where(mask[None], score.reshape(ratio, BLOCK, span), -1e30))
            score = jnp.concatenate(scores, axis=0)
            top = jnp.max(score, axis=2, keepdims=True)
            powers = jnp.exp2((score - top) * scale)
            weights = powers * (1.0 / jnp.sum(powers, axis=2, keepdims=True))
            weights = weights.reshape(len(some), ratio * BLOCK, span).astype(jnp.bfloat16)
            for place, (j, here, cos, sin) in enumerate(some):
                prev = jnp.maximum(j - 1, 0)
                region = pl.ds(pl.multiple_of(plan[PROMPT, j] * CTXP, CTXP), CTXP)
                new_value = jnp.concatenate([new_values[prev, :, part], new_values[j, :, part]], axis=0)
                value = jnp.concatenate([prefix_values[region, part], new_value.astype(jnp.bfloat16)], axis=0)
                mixed = jnp.dot(weights[place], value, preferred_element_type=jnp.float32)
                mixed = jnp.where(plan[LIVE, j] > 0, mixed, 0.0)
                for n in range(ratio):
                    first = (h * ratio + n) * HEAD
                    out[j, :, first : first + HEAD] = mixed[n * BLOCK : (n + 1) * BLOCK].astype(
                        jnp.bfloat16
                    )


def cache_kernel(tensors, *rest):
    arrived, out = rest[:tensors], rest[tensors + 1]
    own_tensor = lax.axis_index("tensor")
    width_k = arrived[0].shape[1]
    for distance in range(tensors):
        sender = lax.rem(own_tensor - distance + tensors, tensors)
        at = pl.ds(pl.multiple_of(sender * width_k, HEAD), width_k)
        part = arrived[distance][...].astype(jnp.float32)
        out[:, :, at] = part.reshape(out.shape[0], out.shape[1], width_k).astype(jnp.bfloat16)


def in_hbm(operand):
    return pltpu.with_memory_space_constraint(operand, pltpu.HBM)


def after(arrays, others):
    return pl.pallas_call(
        lambda *refs: None,
        out_shape=[jax.ShapeDtypeStruct(array.shape, array.dtype) for array in arrays],
        in_specs=[ANY] * (len(arrays) + len(others)),
        out_specs=[ANY] * len(arrays),
        input_output_aliases={n: n for n in range(len(arrays))},
        compiler_params=pltpu.CompilerParams(vmem_limit_bytes=VMEM_LIMIT),
        name="hold",
    )(*arrays, *others)


def shifted(chunks, axis):
    size = lax.axis_size(axis)
    return [chunks[0]] + [
        chunks[d] is not None
        and lax.ppermute(chunks[d], axis, [(i, (i + d) % size) for i in range(size)])
        for d in range(1, size)
    ]


def per_device(
    queries,
    keys,
    values,
    prefix_keys,
    prefix_values,
    spread,
    turn,
    new_blocks,
    prefix_len,
    owner,
    page_start,
):
    groups = lax.axis_size("group")
    tensors = lax.axis_size("tensor")
    width_q = queries.shape[1]
    width_k = keys.shape[1]
    heads_q = width_q // HEAD
    heads_k = width_k // HEAD
    slots = queries.shape[0] // BLOCK
    capacity = slots // groups
    prompts = new_blocks.shape[1]
    tokens = BLOCK // tensors
    pages = prompts * MAXP
    cosine, sine = (jnp.asarray(table) for table in rope_table())
    params = pltpu.CompilerParams(vmem_limit_bytes=VMEM_LIMIT)
    blocks_q = queries.reshape(slots, BLOCK, width_q)
    blocks_k = keys.reshape(slots, BLOCK, width_k)
    blocks_v = values.reshape(slots, BLOCK, width_k)

    wide = 2 * width_k
    chunk_rows = capacity * (width_q // wide + 1)

    def chunk(rows):
        return jax.ShapeDtypeStruct((rows, BLOCK, wide), jnp.bfloat16)

    sent = pl.pallas_call(
        functools.partial(dispatch_kernel, groups),
        out_shape=[
            chunk(chunk_rows + (groups if distance == JOINED else 0)) for distance in range(groups)
        ]
        + [chunk(groups)] * (groups - 1),
        in_specs=[HBM] * 7,
        out_specs=[VMEM] * (2 * groups - 1),
        scratch_shapes=[
            *(pltpu.SMEM(array.shape, jnp.int32) for array in (spread, turn, new_blocks, owner)),
            *(pltpu.VMEM(array.shape, jnp.bfloat16) for array in (blocks_q, blocks_k, blocks_v)),
            pltpu.SMEM((groups * groups + 1,), jnp.int32),
            pltpu.SemaphoreType.DMA((7,)),
        ],
        compiler_params=params,
        name="dispatch",
    )(
        *(
            in_hbm(operand)
            for operand in (spread, turn, new_blocks, owner, blocks_q, blocks_k, blocks_v)
        )
    )
    part_rows = pages * 2 * tokens
    plan, pick = pl.pallas_call(
        functools.partial(plan_kernel, groups, tensors),
        out_shape=[
            jax.ShapeDtypeStruct((7, max(slots, groups) + 1), jnp.int32),
            jax.ShapeDtypeStruct((tensors * part_rows, 2 * pages * BLOCK), jnp.bfloat16),
        ],
        in_specs=[SMEM] * 5 + [ANY],
        out_specs=[SMEM, VMEM],
        compiler_params=params,
        name="plan",
    )(spread, new_blocks, prefix_len, owner, page_start, sent[0])
    own, pages_only = list(sent[:groups]), list(sent[groups:])
    pages_only.insert(JOINED, own[JOINED])
    handed = shifted(pages_only, "group")
    later = [distance for distance in range(1, groups) if distance != JOINED]
    held = dict(zip(later, after([own[distance] for distance in later], [*(handed[n] for n in later), plan])))
    moved = shifted([own[0]] + [held.get(distance) for distance in range(1, groups)], "group")
    arrived = [handed[n] if n == JOINED else moved[n] for n in range(groups)]

    part = jax.ShapeDtypeStruct((part_rows, width_k), jnp.bfloat16)
    finished = pl.pallas_call(
        functools.partial(pages_kernel, groups, tensors),
        out_shape=[part] * tensors,
        in_specs=[SMEM] + [VMEM] * (3 + groups),
        out_specs=[VMEM] * tensors,
        compiler_params=params,
        scratch_shapes=[
            pltpu.VMEM((groups * groups, BLOCK, 2 * width_k), jnp.bfloat16),
            pltpu.VMEM((2 * pages * BLOCK, width_k), jnp.float32),
        ],
        name="finish_pages",
    )(plan, pick, cosine, sine, *handed)
    parts = shifted(finished, "tensor")

    attention = pl.pallas_call(
        functools.partial(attention_kernel, groups, heads_q, heads_k),
        out_shape=jax.ShapeDtypeStruct((slots, BLOCK, width_q), jnp.bfloat16),
        in_specs=[SMEM] + [VMEM] * (4 + groups),
        out_specs=VMEM,
        scratch_shapes=[pltpu.VMEM((slots, BLOCK, width_k), jnp.float32)] * 2,
        compiler_params=params,
        name="attention",
    )(plan, prefix_keys, prefix_values, cosine, sine, *arrived)

    cache = pl.pallas_call(
        functools.partial(cache_kernel, tensors),
        out_shape=jax.ShapeDtypeStruct((pages * 2, tokens, tensors * width_k), jnp.bfloat16),
        in_specs=[VMEM] * tensors + [ANY],
        out_specs=VMEM,
        compiler_params=params,
        name="place_pages",
    )(*parts, in_hbm(attention))
    return (
        attention.reshape(slots * BLOCK, width_q),
        cache.reshape(pages, 2, tokens, tensors * width_k),
    )


def solution(mesh):
    return jax.shard_map(
        per_device,
        mesh=mesh,
        in_specs=(
            P(("parts", "group"), "tensor"),
            P(("parts", "group"), "tensor"),
            P(("parts", "group"), "tensor"),
            P(("parts", "group"), "tensor"),
            P(("parts", "group"), "tensor"),
            P("parts"),
            P("parts"),
            P("parts", None),
            P("parts", None),
            P("parts", None),
            P("parts", None),
        ),
        out_specs=(P(("parts", "group"), "tensor"), P(("parts", "group"), None, "tensor", None)),
        check_vma=False,
    )
```

```python
import functools
import math

import jax
import jax.numpy as jnp
import numpy as np
from jax import lax
from jax.experimental import pallas as pl
from jax.experimental.pallas import tpu as pltpu
from jax.sharding import PartitionSpec as P

HEAD = 128
BLOCK = 8
MAXP = 2
CTXP = 64

VMEM_LIMIT = 24 * 1024 * 1024

SMEM = pl.BlockSpec(memory_space=pltpu.SMEM)
VMEM = pl.BlockSpec(memory_space=pltpu.VMEM)
JOINED = 3
PROMPT, OFFSET, LIVE, CACHED, SOURCE, COLUMN, PLACE = range(7)
ANY = pl.BlockSpec(memory_space=pl.ANY)
HBM = pl.BlockSpec(memory_space=pltpu.HBM)


def rope_table():
    count = CTXP + MAXP * BLOCK
    half = HEAD // 2
    frequency = np.exp(np.arange(half) * (-2.0 * math.log(500000.0) / HEAD))
    angles = np.arange(count)[:, None] * frequency[None, :]
    cosine, sine = np.cos(angles), np.sin(angles)
    return (
        np.concatenate([cosine, cosine], axis=1).astype(np.float32),
        np.concatenate([-sine, sine], axis=1).astype(np.float32),
    )


def loop(count, body, unrolled=16):
    if count <= unrolled:
        for index in range(count):
            body(index)
    else:
        lax.fori_loop(0, count, lambda index, carry: (body(index), carry)[1], 0)


def turned(head_block, cosine, sine):
    return head_block * cosine + pltpu.roll(head_block, HEAD // 2, 1) * sine


def dispatch_kernel(
    groups, spread_in, turn_in, new_blocks_in, owner_in, queries_in, keys_in, values_in, *rest
):
    outs, handed, rest = rest[:groups], list(rest[groups : 2 * groups - 1]), rest[2 * groups - 1 :]
    handed.insert(JOINED, None)
    spread, turn, new_blocks, owner, queries, keys, values, table, sem = rest
    own = lax.axis_index("group")
    slots, _, width_q = queries.shape
    width_k = keys.shape[2]
    capacity = slots // groups
    prompts = new_blocks.shape[1]
    copies = [
        pltpu.make_async_copy(source, target, sem.at[n])
        for n, (source, target) in enumerate(
            (
                (spread_in, spread),
                (turn_in, turn),
                (new_blocks_in, new_blocks),
                (owner_in, owner),
                (keys_in, keys),
                (values_in, values),
                (queries_in, queries),
            )
        )
    ]
    for copy in copies:
        copy.start()
    for copy in copies[:4]:
        copy.wait()

    def clear(n):
        table[n] = 0

    loop(groups * groups, clear)

    def column(c):
        target = lax.rem(own - spread[c] + groups, groups)

        def find(p, carry):
            start, holders = carry
            blocks = new_blocks[target, p]
            holders = [
                jnp.where((c + groups * n >= start) & (c + groups * n < start + blocks), owner[target, p], holder)
                for n, holder in enumerate(holders)
            ]
            return start + blocks, holders

        carry = (jnp.int32(0), [jnp.int32(-1)] * capacity)
        if prompts <= 8:
            for p in range(prompts):
                carry = find(p, carry)
        else:
            carry = lax.fori_loop(0, prompts, find, carry)
        for n, holder in enumerate(carry[1]):
            at = lax.rem(holder - own + groups, groups) * groups + target
            table[jnp.where(holder >= 0, at, groups * groups)] = lax.rem(c + groups * n + turn[own], slots)

    loop(groups, column)
    for copy in copies[4:]:
        copy.wait()
    for distance in range(groups):
        first_slot = column_of(spread, groups, distance) + turn[own]
        out = outs[distance]
        wide = 2 * width_k
        per_slot = width_q // wide + 1
        for step in range(capacity):
            source = lax.rem(first_slot + groups * step, slots)
            for n in range(per_slot - 1):
                out[step * per_slot + n] = queries[source, :, n * wide : (n + 1) * wide]
            last = step * per_slot + per_slot - 1
            out[last, :, :width_k] = keys[source]
            out[last, :, width_k:] = values[source]
        target, base = (out, capacity * per_slot) if distance == JOINED else (handed[distance], 0)

        def page(g):
            source = table[distance * groups + g]
            target[base + g, :, :width_k] = keys[source]
            target[base + g, :, width_k:] = values[source]

        loop(groups, page)


def column_of(spread, groups, distance):
    wanted = (groups - distance) % groups
    if groups <= 8:
        return sum(jnp.where(spread[c] == wanted, c, 0) for c in range(groups))
    return lax.fori_loop(
        0, groups, lambda c, found: jnp.where(spread[c] == wanted, c, found), jnp.int32(0)
    )


def make_plan(groups, own, spread, new_blocks, prefix_len, owner, page_start, plan):
    prompts = new_blocks.shape[1]
    slots = prompts * MAXP

    def clear(j):
        plan[PROMPT, j] = 0
        plan[OFFSET, j] = 0
        plan[LIVE, j] = 0
        plan[CACHED, j] = 0

    loop(slots, clear)

    def one(p, start):
        blocks = new_blocks[own, p]
        cached = prefix_len[own, p]
        for step in range(MAXP):
            at = jnp.where(step < blocks, start + step, slots)
            plan[PROMPT, at] = p
            plan[OFFSET, at] = cached + step * BLOCK
            plan[LIVE, at] = 1 + step
            plan[CACHED, at] = cached
        return start + blocks

    start = jnp.int32(0)
    if prompts <= 8:
        for p in range(prompts):
            start = one(p, start)
    else:
        lax.fori_loop(0, prompts, one, start)

    def of_group(g):
        def one(p, start):
            blocks = new_blocks[g, p]
            mine = owner[g, p] == own
            for step in range(MAXP):
                root = lax.rem(g + spread[lax.rem(start + step, groups)], groups)
                at = jnp.where(mine, page_start[g, p] + step, slots)
                away = lax.rem(own - root + groups, groups)
                plan[SOURCE, at] = jnp.where(step < blocks, away * groups + g, -1)
                plan[PLACE, at] = prefix_len[g, p] + step * BLOCK
            return start + blocks

        start = jnp.int32(0)
        if prompts <= 8:
            for p in range(prompts):
                start = one(p, start)
        else:
            lax.fori_loop(0, prompts, one, start)

    loop(groups, of_group)
    for distance in range(groups):
        plan[COLUMN, distance] = column_of(spread, groups, distance)


def plan_kernel(groups, tensors, spread, new_blocks, prefix_len, owner, page_start, _, plan, pick):
    own = lax.axis_index("group")
    own_tensor = lax.axis_index("tensor")
    make_plan(groups, own, spread, new_blocks, prefix_len, owner, page_start, plan)
    pages = new_blocks.shape[1] * MAXP
    tokens = BLOCK // tensors
    size = pages * 2 * tokens
    row = lax.broadcasted_iota(jnp.int32, pick.shape, 0)
    col = lax.broadcasted_iota(jnp.int32, pick.shape, 1)
    share = lax.rem(row // size + own_tensor, tensors)
    kind, page = (row // tokens) % 2, (row // (2 * tokens)) % pages
    wanted = (kind * pages + page) * BLOCK + share * tokens + row % tokens
    pick[...] = (col == wanted).astype(jnp.float32).astype(jnp.bfloat16)


def pages_kernel(groups, tensors, plan, pick, cosine, sine, *rest):
    chunks, rest = rest[:groups], rest[groups:]
    outs, (blocks, rows) = rest[:tensors], rest[tensors:]
    width_k = rows.shape[1]
    pages = rows.shape[0] // (2 * BLOCK)
    size = pick.shape[0] // tensors
    for distance in range(groups):
        first = chunks[distance].shape[0] - groups
        blocks[distance * groups : (distance + 1) * groups] = chunks[distance][first:]

    def assemble(page):
        source = plan[SOURCE, page]
        place = plan[PLACE, page]
        block = blocks[jnp.maximum(source, 0)].astype(jnp.float32)
        block = jnp.where(source >= 0, block, 0.0)
        cos = cosine[pl.ds(place, BLOCK), :]
        sin = sine[pl.ds(place, BLOCK), :]
        for first in range(0, width_k, HEAD):
            part = slice(first, first + HEAD)
            rows[pl.ds(pl.multiple_of(page * BLOCK, BLOCK), BLOCK), part] = turned(
                block[:, part], cos, sin
            )
        rows[pl.ds(pl.multiple_of((pages + page) * BLOCK, BLOCK), BLOCK), :] = block[:, width_k:]

    loop(pages, assemble)
    moved = jnp.dot(pick[...], rows[...].astype(jnp.bfloat16), preferred_element_type=jnp.float32)
    moved = moved.astype(jnp.bfloat16)
    for distance in range(tensors):
        outs[distance][...] = moved[distance * size : (distance + 1) * size]


def columns(chunk, step, width_q, first, width):
    wide = chunk.shape[2]
    row = step * (width_q // wide + 1) + first // wide
    return chunk[row, :, first % wide : first % wide + width]


def attention_kernel(groups, heads_q, heads_k, plan, prefix_keys, prefix_values, cosine, sine, *rest):
    arrived, (out, new_keys, new_values) = rest[:groups], rest[groups:]
    slots = out.shape[0]
    capacity = slots // groups
    ratio = heads_q // heads_k
    width_q = heads_q * HEAD
    width_k = heads_k * HEAD
    scale = math.log2(math.e) / math.sqrt(HEAD)
    span = CTXP + 2 * BLOCK
    lane = lax.broadcasted_iota(jnp.int32, (BLOCK, span), 1)
    token = lax.broadcasted_iota(jnp.int32, (BLOCK, span), 0)
    fresh = (lane >= CTXP + BLOCK) & (lane - (CTXP + BLOCK) <= token)
    before = (lane >= CTXP) & (lane < CTXP + BLOCK)

    blocks = []
    for distance in range(groups):
        first_slot = plan[COLUMN, distance]
        for step in range(capacity):
            j = first_slot + groups * step
            here = functools.partial(columns, arrived[distance], step, width_q)
            cos = cosine[pl.ds(plan[OFFSET, j], BLOCK), :]
            sin = sine[pl.ds(plan[OFFSET, j], BLOCK), :]
            new_keys[j] = jnp.concatenate(
                [
                    turned(here(first, HEAD).astype(jnp.float32), cos, sin)
                    for first in range(width_q, width_q + width_k, HEAD)
                ],
                axis=1,
            )
            new_values[j] = here(width_q + width_k, width_k).astype(jnp.float32)
            blocks.append((j, here, cos, sin))

    for at in range(0, len(blocks), 8):
        some = blocks[at : at + 8]
        for h in range(heads_k):
            part = slice(h * HEAD, (h + 1) * HEAD)
            scores = []
            for j, here, cos, sin in some:
                prev = jnp.maximum(j - 1, 0)
                region = pl.ds(pl.multiple_of(plan[PROMPT, j] * CTXP, CTXP), CTXP)
                mask = fresh | (lane < plan[CACHED, j]) & (lane < CTXP) | before & (plan[LIVE, j] == 2)
                new_key = jnp.concatenate([new_keys[prev, :, part], new_keys[j, :, part]], axis=0)
                key = jnp.concatenate([prefix_keys[region, part], new_key.astype(jnp.bfloat16)], axis=0)
                query = jnp.concatenate(
                    [
                        turned(here(n * HEAD, HEAD).astype(jnp.float32), cos, sin)
                        for n in range(h * ratio, (h + 1) * ratio)
                    ],
                    axis=0,
                ).astype(jnp.bfloat16)
                score = lax.dot_general(
                    query, key, (((1,), (1,)), ((), ())), preferred_element_type=jnp.float32
                )
                scores.append(jnp.where(mask[None], score.reshape(ratio, BLOCK, span), -1e30))
            score = jnp.concatenate(scores, axis=0)
            top = jnp.max(score, axis=2, keepdims=True)
            powers = jnp.exp2((score - top) * scale)
            weights = powers * (1.0 / jnp.sum(powers, axis=2, keepdims=True))
            weights = weights.reshape(len(some), ratio * BLOCK, span).astype(jnp.bfloat16)
            for place, (j, here, cos, sin) in enumerate(some):
                prev = jnp.maximum(j - 1, 0)
                region = pl.ds(pl.multiple_of(plan[PROMPT, j] * CTXP, CTXP), CTXP)
                new_value = jnp.concatenate([new_values[prev, :, part], new_values[j, :, part]], axis=0)
                value = jnp.concatenate([prefix_values[region, part], new_value.astype(jnp.bfloat16)], axis=0)
                mixed = jnp.dot(weights[place], value, preferred_element_type=jnp.float32)
                mixed = jnp.where(plan[LIVE, j] > 0, mixed, 0.0)
                for n in range(ratio):
                    first = (h * ratio + n) * HEAD
                    out[j, :, first : first + HEAD] = mixed[n * BLOCK : (n + 1) * BLOCK].astype(
                        jnp.bfloat16
                    )


def cache_kernel(tensors, *rest):
    arrived, out = rest[:tensors], rest[tensors + 1]
    own_tensor = lax.axis_index("tensor")
    width_k = arrived[0].shape[1]
    for distance in range(tensors):
        sender = lax.rem(own_tensor - distance + tensors, tensors)
        at = pl.ds(pl.multiple_of(sender * width_k, HEAD), width_k)
        part = arrived[distance][...].astype(jnp.float32)
        out[:, :, at] = part.reshape(out.shape[0], out.shape[1], width_k).astype(jnp.bfloat16)


def in_hbm(operand):
    return pltpu.with_memory_space_constraint(operand, pltpu.HBM)


def after(arrays, others):
    return pl.pallas_call(
        lambda *refs: None,
        out_shape=[jax.ShapeDtypeStruct(array.shape, array.dtype) for array in arrays],
        in_specs=[ANY] * (len(arrays) + len(others)),
        out_specs=[ANY] * len(arrays),
        input_output_aliases={n: n for n in range(len(arrays))},
        compiler_params=pltpu.CompilerParams(vmem_limit_bytes=VMEM_LIMIT),
        name="hold",
    )(*arrays, *others)


def shifted(chunks, axis):
    size = lax.axis_size(axis)
    return [chunks[0]] + [
        chunks[d] is not None
        and lax.ppermute(chunks[d], axis, [(i, (i + d) % size) for i in range(size)])
        for d in range(1, size)
    ]


def per_device(
    queries,
    keys,
    values,
    prefix_keys,
    prefix_values,
    spread,
    turn,
    new_blocks,
    prefix_len,
    owner,
    page_start,
):
    groups = lax.axis_size("group")
    tensors = lax.axis_size("tensor")
    width_q = queries.shape[1]
    width_k = keys.shape[1]
    heads_q = width_q // HEAD
    heads_k = width_k // HEAD
    slots = queries.shape[0] // BLOCK
    capacity = slots // groups
    prompts = new_blocks.shape[1]
    tokens = BLOCK // tensors
    pages = prompts * MAXP
    cosine, sine = (jnp.asarray(table) for table in rope_table())
    params = pltpu.CompilerParams(vmem_limit_bytes=VMEM_LIMIT)
    blocks_q = queries.reshape(slots, BLOCK, width_q)
    blocks_k = keys.reshape(slots, BLOCK, width_k)
    blocks_v = values.reshape(slots, BLOCK, width_k)

    wide = 2 * width_k
    chunk_rows = capacity * (width_q // wide + 1)

    def chunk(rows):
        return jax.ShapeDtypeStruct((rows, BLOCK, wide), jnp.bfloat16)

    sent = pl.pallas_call(
        functools.partial(dispatch_kernel, groups),
        out_shape=[
            chunk(chunk_rows + (groups if distance == JOINED else 0)) for distance in range(groups)
        ]
        + [chunk(groups)] * (groups - 1),
        in_specs=[HBM] * 7,
        out_specs=[VMEM] * (2 * groups - 1),
        scratch_shapes=[
            *(pltpu.SMEM(array.shape, jnp.int32) for array in (spread, turn, new_blocks, owner)),
            *(pltpu.VMEM(array.shape, jnp.bfloat16) for array in (blocks_q, blocks_k, blocks_v)),
            pltpu.SMEM((groups * groups + 1,), jnp.int32),
            pltpu.SemaphoreType.DMA((7,)),
        ],
        compiler_params=params,
        name="dispatch",
    )(
        *(
            in_hbm(operand)
            for operand in (spread, turn, new_blocks, owner, blocks_q, blocks_k, blocks_v)
        )
    )
    part_rows = pages * 2 * tokens
    plan, pick = pl.pallas_call(
        functools.partial(plan_kernel, groups, tensors),
        out_shape=[
            jax.ShapeDtypeStruct((7, max(slots, groups) + 1), jnp.int32),
            jax.ShapeDtypeStruct((tensors * part_rows, 2 * pages * BLOCK), jnp.bfloat16),
        ],
        in_specs=[SMEM] * 5 + [ANY],
        out_specs=[SMEM, VMEM],
        compiler_params=params,
        name="plan",
    )(spread, new_blocks, prefix_len, owner, page_start, sent[0])
    own, pages_only = list(sent[:groups]), list(sent[groups:])
    pages_only.insert(JOINED, own[JOINED])
    handed = shifted(pages_only, "group")
    later = [distance for distance in range(1, groups) if distance != JOINED]
    held = dict(zip(later, after([own[distance] for distance in later], [*(handed[n] for n in later), plan])))
    moved = shifted([own[0]] + [held.get(distance) for distance in range(1, groups)], "group")
    arrived = [handed[n] if n == JOINED else moved[n] for n in range(groups)]

    part = jax.ShapeDtypeStruct((part_rows, width_k), jnp.bfloat16)
    finished = pl.pallas_call(
        functools.partial(pages_kernel, groups, tensors),
        out_shape=[part] * tensors,
        in_specs=[SMEM] + [VMEM] * (3 + groups),
        out_specs=[VMEM] * tensors,
        compiler_params=params,
        scratch_shapes=[
            pltpu.VMEM((groups * groups, BLOCK, 2 * width_k), jnp.bfloat16),
            pltpu.VMEM((2 * pages * BLOCK, width_k), jnp.float32),
        ],
        name="finish_pages",
    )(plan, pick, cosine, sine, *handed)
    parts = shifted(finished, "tensor")

    attention = pl.pallas_call(
        functools.partial(attention_kernel, groups, heads_q, heads_k),
        out_shape=jax.ShapeDtypeStruct((slots, BLOCK, width_q), jnp.bfloat16),
        in_specs=[SMEM] + [VMEM] * (4 + groups),
        out_specs=VMEM,
        scratch_shapes=[pltpu.VMEM((slots, BLOCK, width_k), jnp.float32)] * 2,
        compiler_params=params,
        name="attention",
    )(plan, prefix_keys, prefix_values, cosine, sine, *arrived)

    cache = pl.pallas_call(
        functools.partial(cache_kernel, tensors),
        out_shape=jax.ShapeDtypeStruct((pages * 2, tokens, tensors * width_k), jnp.bfloat16),
        in_specs=[VMEM] * tensors + [ANY],
        out_specs=VMEM,
        compiler_params=params,
        name="place_pages",
    )(*parts, in_hbm(attention))
    return (
        attention.reshape(slots * BLOCK, width_q),
        cache.reshape(pages, 2, tokens, tensors * width_k),
    )


def solution(mesh):
    return jax.shard_map(
        per_device,
        mesh=mesh,
        in_specs=(
            P(("parts", "group"), "tensor"),
            P(("parts", "group"), "tensor"),
            P(("parts", "group"), "tensor"),
            P(("parts", "group"), "tensor"),
            P(("parts", "group"), "tensor"),
            P("parts"),
            P("parts"),
            P("parts", None),
            P("parts", None),
            P("parts", None),
            P("parts", None),
        ),
        out_specs=(P(("parts", "group"), "tensor"), P(("parts", "group"), None, "tensor", None)),
        check_vma=False,
    )
```

```python
import functools
import math

import jax
import jax.numpy as jnp
import numpy as np
from jax import lax
from jax.experimental import pallas as pl
from jax.experimental.pallas import tpu as pltpu
from jax.sharding import PartitionSpec as P

HEAD = 128
BLOCK = 8
MAXP = 2
CTXP = 64

VMEM_LIMIT = 24 * 1024 * 1024

SMEM = pl.BlockSpec(memory_space=pltpu.SMEM)
VMEM = pl.BlockSpec(memory_space=pltpu.VMEM)
JOINED = 1
PROMPT, OFFSET, LIVE, CACHED, SOURCE, COLUMN, PLACE = range(7)
ANY = pl.BlockSpec(memory_space=pl.ANY)
HBM = pl.BlockSpec(memory_space=pltpu.HBM)


def rope_table():
    count = CTXP + MAXP * BLOCK
    half = HEAD // 2
    frequency = np.exp(np.arange(half) * (-2.0 * math.log(500000.0) / HEAD))
    angles = np.arange(count)[:, None] * frequency[None, :]
    cosine, sine = np.cos(angles), np.sin(angles)
    return (
        np.concatenate([cosine, cosine], axis=1).astype(np.float32),
        np.concatenate([-sine, sine], axis=1).astype(np.float32),
    )


def loop(count, body, unrolled=16):
    if count <= unrolled:
        for index in range(count):
            body(index)
    else:
        lax.fori_loop(0, count, lambda index, carry: (body(index), carry)[1], 0)


def turned(head_block, cosine, sine):
    return head_block * cosine + pltpu.roll(head_block, HEAD // 2, 1) * sine


def dispatch_kernel(
    groups, spread_in, turn_in, new_blocks_in, owner_in, queries_in, keys_in, values_in, *rest
):
    outs, handed, rest = rest[:groups], list(rest[groups : 2 * groups - 1]), rest[2 * groups - 1 :]
    handed.insert(JOINED, None)
    spread, turn, new_blocks, owner, queries, keys, values, table, sem = rest
    own = lax.axis_index("group")
    slots, _, width_q = queries.shape
    width_k = keys.shape[2]
    capacity = slots // groups
    prompts = new_blocks.shape[1]
    copies = [
        pltpu.make_async_copy(source, target, sem.at[n])
        for n, (source, target) in enumerate(
            (
                (spread_in, spread),
                (turn_in, turn),
                (new_blocks_in, new_blocks),
                (owner_in, owner),
                (keys_in, keys),
                (values_in, values),
                (queries_in, queries),
            )
        )
    ]
    for copy in copies:
        copy.start()
    for copy in copies[:4]:
        copy.wait()

    def clear(n):
        table[n] = 0

    loop(groups * groups, clear)

    def column(c):
        target = lax.rem(own - spread[c] + groups, groups)

        def find(p, carry):
            start, holders = carry
            blocks = new_blocks[target, p]
            holders = [
                jnp.where((c + groups * n >= start) & (c + groups * n < start + blocks), owner[target, p], holder)
                for n, holder in enumerate(holders)
            ]
            return start + blocks, holders

        carry = (jnp.int32(0), [jnp.int32(-1)] * capacity)
        if prompts <= 8:
            for p in range(prompts):
                carry = find(p, carry)
        else:
            carry = lax.fori_loop(0, prompts, find, carry)
        for n, holder in enumerate(carry[1]):
            at = lax.rem(holder - own + groups, groups) * groups + target
            table[jnp.where(holder >= 0, at, groups * groups)] = lax.rem(c + groups * n + turn[own], slots)

    loop(groups, column)
    for copy in copies[4:]:
        copy.wait()
    for distance in range(groups):
        first_slot = column_of(spread, groups, distance) + turn[own]
        out = outs[distance]
        wide = 2 * width_k
        per_slot = width_q // wide + 1
        for step in range(capacity):
            source = lax.rem(first_slot + groups * step, slots)
            for n in range(per_slot - 1):
                out[step * per_slot + n] = queries[source, :, n * wide : (n + 1) * wide]
            last = step * per_slot + per_slot - 1
            out[last, :, :width_k] = keys[source]
            out[last, :, width_k:] = values[source]
        target, base = (out, capacity * per_slot) if distance == JOINED else (handed[distance], 0)

        def page(g):
            source = table[distance * groups + g]
            target[base + g, :, :width_k] = keys[source]
            target[base + g, :, width_k:] = values[source]

        loop(groups, page)


def column_of(spread, groups, distance):
    wanted = (groups - distance) % groups
    if groups <= 8:
        return sum(jnp.where(spread[c] == wanted, c, 0) for c in range(groups))
    return lax.fori_loop(
        0, groups, lambda c, found: jnp.where(spread[c] == wanted, c, found), jnp.int32(0)
    )


def make_plan(groups, own, spread, new_blocks, prefix_len, owner, page_start, plan):
    prompts = new_blocks.shape[1]
    slots = prompts * MAXP

    def clear(j):
        plan[PROMPT, j] = 0
        plan[OFFSET, j] = 0
        plan[LIVE, j] = 0
        plan[CACHED, j] = 0

    loop(slots, clear)

    def one(p, start):
        blocks = new_blocks[own, p]
        cached = prefix_len[own, p]
        for step in range(MAXP):
            at = jnp.where(step < blocks, start + step, slots)
            plan[PROMPT, at] = p
            plan[OFFSET, at] = cached + step * BLOCK
            plan[LIVE, at] = 1 + step
            plan[CACHED, at] = cached
        return start + blocks

    start = jnp.int32(0)
    if prompts <= 8:
        for p in range(prompts):
            start = one(p, start)
    else:
        lax.fori_loop(0, prompts, one, start)

    def of_group(g):
        def one(p, start):
            blocks = new_blocks[g, p]
            mine = owner[g, p] == own
            for step in range(MAXP):
                root = lax.rem(g + spread[lax.rem(start + step, groups)], groups)
                at = jnp.where(mine, page_start[g, p] + step, slots)
                away = lax.rem(own - root + groups, groups)
                plan[SOURCE, at] = jnp.where(step < blocks, away * groups + g, -1)
                plan[PLACE, at] = prefix_len[g, p] + step * BLOCK
            return start + blocks

        start = jnp.int32(0)
        if prompts <= 8:
            for p in range(prompts):
                start = one(p, start)
        else:
            lax.fori_loop(0, prompts, one, start)

    loop(groups, of_group)
    for distance in range(groups):
        plan[COLUMN, distance] = column_of(spread, groups, distance)


def plan_kernel(groups, tensors, spread, new_blocks, prefix_len, owner, page_start, _, plan, pick):
    own = lax.axis_index("group")
    own_tensor = lax.axis_index("tensor")
    make_plan(groups, own, spread, new_blocks, prefix_len, owner, page_start, plan)
    pages = new_blocks.shape[1] * MAXP
    tokens = BLOCK // tensors
    size = pages * 2 * tokens
    row = lax.broadcasted_iota(jnp.int32, pick.shape, 0)
    col = lax.broadcasted_iota(jnp.int32, pick.shape, 1)
    share = lax.rem(row // size + own_tensor, tensors)
    kind, page = (row // tokens) % 2, (row // (2 * tokens)) % pages
    wanted = (kind * pages + page) * BLOCK + share * tokens + row % tokens
    pick[...] = (col == wanted).astype(jnp.float32).astype(jnp.bfloat16)


def pages_kernel(groups, tensors, plan, pick, cosine, sine, *rest):
    chunks, rest = rest[:groups], rest[groups:]
    outs, (blocks, rows) = rest[:tensors], rest[tensors:]
    width_k = rows.shape[1]
    pages = rows.shape[0] // (2 * BLOCK)
    size = pick.shape[0] // tensors
    for distance in range(groups):
        first = chunks[distance].shape[0] - groups
        blocks[distance * groups : (distance + 1) * groups] = chunks[distance][first:]

    def assemble(page):
        source = plan[SOURCE, page]
        place = plan[PLACE, page]
        block = blocks[jnp.maximum(source, 0)].astype(jnp.float32)
        block = jnp.where(source >= 0, block, 0.0)
        cos = cosine[pl.ds(place, BLOCK), :]
        sin = sine[pl.ds(place, BLOCK), :]
        for first in range(0, width_k, HEAD):
            part = slice(first, first + HEAD)
            rows[pl.ds(pl.multiple_of(page * BLOCK, BLOCK), BLOCK), part] = turned(
                block[:, part], cos, sin
            )
        rows[pl.ds(pl.multiple_of((pages + page) * BLOCK, BLOCK), BLOCK), :] = block[:, width_k:]

    loop(pages, assemble)
    moved = jnp.dot(pick[...], rows[...].astype(jnp.bfloat16), preferred_element_type=jnp.float32)
    moved = moved.astype(jnp.bfloat16)
    for distance in range(tensors):
        outs[distance][...] = moved[distance * size : (distance + 1) * size]


def columns(chunk, step, width_q, first, width):
    wide = chunk.shape[2]
    row = step * (width_q // wide + 1) + first // wide
    return chunk[row, :, first % wide : first % wide + width]


def attention_kernel(groups, heads_q, heads_k, plan, prefix_keys, prefix_values, cosine, sine, *rest):
    arrived, (out, new_keys, new_values) = rest[:groups], rest[groups:]
    slots = out.shape[0]
    capacity = slots // groups
    ratio = heads_q // heads_k
    width_q = heads_q * HEAD
    width_k = heads_k * HEAD
    scale = math.log2(math.e) / math.sqrt(HEAD)
    span = CTXP + 2 * BLOCK
    lane = lax.broadcasted_iota(jnp.int32, (BLOCK, span), 1)
    token = lax.broadcasted_iota(jnp.int32, (BLOCK, span), 0)
    fresh = (lane >= CTXP + BLOCK) & (lane - (CTXP + BLOCK) <= token)
    before = (lane >= CTXP) & (lane < CTXP + BLOCK)

    blocks = []
    for distance in range(groups):
        first_slot = plan[COLUMN, distance]
        for step in range(capacity):
            j = first_slot + groups * step
            here = functools.partial(columns, arrived[distance], step, width_q)
            cos = cosine[pl.ds(plan[OFFSET, j], BLOCK), :]
            sin = sine[pl.ds(plan[OFFSET, j], BLOCK), :]
            new_keys[j] = jnp.concatenate(
                [
                    turned(here(first, HEAD).astype(jnp.float32), cos, sin)
                    for first in range(width_q, width_q + width_k, HEAD)
                ],
                axis=1,
            )
            new_values[j] = here(width_q + width_k, width_k).astype(jnp.float32)
            blocks.append((j, here, cos, sin))

    for at in range(0, len(blocks), 4):
        some = blocks[at : at + 4]
        for h in range(heads_k):
            part = slice(h * HEAD, (h + 1) * HEAD)
            scores = []
            for j, here, cos, sin in some:
                prev = jnp.maximum(j - 1, 0)
                region = pl.ds(pl.multiple_of(plan[PROMPT, j] * CTXP, CTXP), CTXP)
                mask = fresh | (lane < plan[CACHED, j]) & (lane < CTXP) | before & (plan[LIVE, j] == 2)
                new_key = jnp.concatenate([new_keys[prev, :, part], new_keys[j, :, part]], axis=0)
                key = jnp.concatenate([prefix_keys[region, part], new_key.astype(jnp.bfloat16)], axis=0)
                query = jnp.concatenate(
                    [
                        turned(here(n * HEAD, HEAD).astype(jnp.float32), cos, sin)
                        for n in range(h * ratio, (h + 1) * ratio)
                    ],
                    axis=0,
                ).astype(jnp.bfloat16)
                score = lax.dot_general(
                    query, key, (((1,), (1,)), ((), ())), preferred_element_type=jnp.float32
                )
                scores.append(jnp.where(mask[None], score.reshape(ratio, BLOCK, span), -1e30))
            score = jnp.concatenate(scores, axis=0)
            top = jnp.max(score, axis=2, keepdims=True)
            powers = jnp.exp2((score - top) * scale)
            weights = powers * (1.0 / jnp.sum(powers, axis=2, keepdims=True))
            weights = weights.reshape(len(some), ratio * BLOCK, span).astype(jnp.bfloat16)
            for place, (j, here, cos, sin) in enumerate(some):
                prev = jnp.maximum(j - 1, 0)
                region = pl.ds(pl.multiple_of(plan[PROMPT, j] * CTXP, CTXP), CTXP)
                new_value = jnp.concatenate([new_values[prev, :, part], new_values[j, :, part]], axis=0)
                value = jnp.concatenate([prefix_values[region, part], new_value.astype(jnp.bfloat16)], axis=0)
                mixed = jnp.dot(weights[place], value, preferred_element_type=jnp.float32)
                mixed = jnp.where(plan[LIVE, j] > 0, mixed, 0.0)
                for n in range(ratio):
                    first = (h * ratio + n) * HEAD
                    out[j, :, first : first + HEAD] = mixed[n * BLOCK : (n + 1) * BLOCK].astype(
                        jnp.bfloat16
                    )


def cache_kernel(tensors, *rest):
    arrived, out = rest[:tensors], rest[tensors + 1]
    own_tensor = lax.axis_index("tensor")
    width_k = arrived[0].shape[1]
    for distance in range(tensors):
        sender = lax.rem(own_tensor - distance + tensors, tensors)
        at = pl.ds(pl.multiple_of(sender * width_k, HEAD), width_k)
        part = arrived[distance][...].astype(jnp.float32)
        out[:, :, at] = part.reshape(out.shape[0], out.shape[1], width_k).astype(jnp.bfloat16)


def in_hbm(operand):
    return pltpu.with_memory_space_constraint(operand, pltpu.HBM)


def after(arrays, others):
    return pl.pallas_call(
        lambda *refs: None,
        out_shape=[jax.ShapeDtypeStruct(array.shape, array.dtype) for array in arrays],
        in_specs=[ANY] * (len(arrays) + len(others)),
        out_specs=[ANY] * len(arrays),
        input_output_aliases={n: n for n in range(len(arrays))},
        compiler_params=pltpu.CompilerParams(vmem_limit_bytes=VMEM_LIMIT),
        name="hold",
    )(*arrays, *others)


def shifted(chunks, axis):
    size = lax.axis_size(axis)
    return [chunks[0]] + [
        chunks[d] is not None
        and lax.ppermute(chunks[d], axis, [(i, (i + d) % size) for i in range(size)])
        for d in range(1, size)
    ]


def per_device(
    queries,
    keys,
    values,
    prefix_keys,
    prefix_values,
    spread,
    turn,
    new_blocks,
    prefix_len,
    owner,
    page_start,
):
    groups = lax.axis_size("group")
    tensors = lax.axis_size("tensor")
    width_q = queries.shape[1]
    width_k = keys.shape[1]
    heads_q = width_q // HEAD
    heads_k = width_k // HEAD
    slots = queries.shape[0] // BLOCK
    capacity = slots // groups
    prompts = new_blocks.shape[1]
    tokens = BLOCK // tensors
    pages = prompts * MAXP
    cosine, sine = (jnp.asarray(table) for table in rope_table())
    params = pltpu.CompilerParams(vmem_limit_bytes=VMEM_LIMIT)
    blocks_q = queries.reshape(slots, BLOCK, width_q)
    blocks_k = keys.reshape(slots, BLOCK, width_k)
    blocks_v = values.reshape(slots, BLOCK, width_k)

    wide = 2 * width_k
    chunk_rows = capacity * (width_q // wide + 1)

    def chunk(rows):
        return jax.ShapeDtypeStruct((rows, BLOCK, wide), jnp.bfloat16)

    sent = pl.pallas_call(
        functools.partial(dispatch_kernel, groups),
        out_shape=[
            chunk(chunk_rows + (groups if distance == JOINED else 0)) for distance in range(groups)
        ]
        + [chunk(groups)] * (groups - 1),
        in_specs=[HBM] * 7,
        out_specs=[VMEM] * (2 * groups - 1),
        scratch_shapes=[
            *(pltpu.SMEM(array.shape, jnp.int32) for array in (spread, turn, new_blocks, owner)),
            *(pltpu.VMEM(array.shape, jnp.bfloat16) for array in (blocks_q, blocks_k, blocks_v)),
            pltpu.SMEM((groups * groups + 1,), jnp.int32),
            pltpu.SemaphoreType.DMA((7,)),
        ],
        compiler_params=params,
        name="dispatch",
    )(
        *(
            in_hbm(operand)
            for operand in (spread, turn, new_blocks, owner, blocks_q, blocks_k, blocks_v)
        )
    )
    part_rows = pages * 2 * tokens
    plan, pick = pl.pallas_call(
        functools.partial(plan_kernel, groups, tensors),
        out_shape=[
            jax.ShapeDtypeStruct((7, max(slots, groups) + 1), jnp.int32),
            jax.ShapeDtypeStruct((tensors * part_rows, 2 * pages * BLOCK), jnp.bfloat16),
        ],
        in_specs=[SMEM] * 5 + [ANY],
        out_specs=[SMEM, VMEM],
        compiler_params=params,
        name="plan",
    )(spread, new_blocks, prefix_len, owner, page_start, sent[0])
    own, pages_only = list(sent[:groups]), list(sent[groups:])
    pages_only.insert(JOINED, own[JOINED])
    handed = shifted(pages_only, "group")
    later = [distance for distance in range(1, groups) if distance != JOINED]
    held = dict(zip(later, after([own[distance] for distance in later], [*(handed[n] for n in later), plan])))
    moved = shifted([own[0]] + [held.get(distance) for distance in range(1, groups)], "group")
    arrived = [handed[n] if n == JOINED else moved[n] for n in range(groups)]

    part = jax.ShapeDtypeStruct((part_rows, width_k), jnp.bfloat16)
    finished = pl.pallas_call(
        functools.partial(pages_kernel, groups, tensors),
        out_shape=[part] * tensors,
        in_specs=[SMEM] + [VMEM] * (3 + groups),
        out_specs=[VMEM] * tensors,
        compiler_params=params,
        scratch_shapes=[
            pltpu.VMEM((groups * groups, BLOCK, 2 * width_k), jnp.bfloat16),
            pltpu.VMEM((2 * pages * BLOCK, width_k), jnp.float32),
        ],
        name="finish_pages",
    )(plan, pick, cosine, sine, *handed)
    parts = shifted(finished, "tensor")

    attention = pl.pallas_call(
        functools.partial(attention_kernel, groups, heads_q, heads_k),
        out_shape=jax.ShapeDtypeStruct((slots, BLOCK, width_q), jnp.bfloat16),
        in_specs=[SMEM] + [VMEM] * (4 + groups),
        out_specs=VMEM,
        scratch_shapes=[pltpu.VMEM((slots, BLOCK, width_k), jnp.float32)] * 2,
        compiler_params=params,
        name="attention",
    )(plan, prefix_keys, prefix_values, cosine, sine, *arrived)

    cache = pl.pallas_call(
        functools.partial(cache_kernel, tensors),
        out_shape=jax.ShapeDtypeStruct((pages * 2, tokens, tensors * width_k), jnp.bfloat16),
        in_specs=[VMEM] * tensors + [ANY],
        out_specs=VMEM,
        compiler_params=params,
        name="place_pages",
    )(*parts, in_hbm(attention))
    return (
        attention.reshape(slots * BLOCK, width_q),
        cache.reshape(pages, 2, tokens, tensors * width_k),
    )


def solution(mesh):
    return jax.shard_map(
        per_device,
        mesh=mesh,
        in_specs=(
            P(("parts", "group"), "tensor"),
            P(("parts", "group"), "tensor"),
            P(("parts", "group"), "tensor"),
            P(("parts", "group"), "tensor"),
            P(("parts", "group"), "tensor"),
            P("parts"),
            P("parts"),
            P("parts", None),
            P("parts", None),
            P("parts", None),
            P("parts", None),
        ),
        out_specs=(P(("parts", "group"), "tensor"), P(("parts", "group"), None, "tensor", None)),
        check_vma=False,
    )
```
